256 devices in a mesh: tm: 8 (over y, core), space: 32 (over z, x).
Axes of the slice: x: 4, y: 4, z: 8, core: 2. Of those that a mesh axis runs over, the one named last changes fastest.
Arguments:
- observed: float32 [16, 192, 1440], P('tm', 'space'), may hold values from -8 to 8
- noise_var: float32 [16], replicated, may hold values from 0.05 to 1
- spectral_var: float32 [1440, 192], P('space'), may hold values from 0.2 to 5
- time_scale: float32 [1440, 192], P('space'), may hold values from 1.5 to 4
Outputs:
- smoothed: float32 [16, 192, 1440], P('tm', 'space')
The draws below stay inside these ranges and needn't reach their ends.
All inputs are finite; a program needn't handle non-finite values.
Results may differ from the reference program's by a relative error of at most 0.00007.
Values sent between devices are 32-bit elements; how exact they have to be, the bound alone decides.
No kernel may reach another device: no remote copies, remote signals or barrier semaphores. Data moves between devices by JAX's collectives and lax.ppermute only.
A program may use at most 64 MiB of HBM per device.

```python
import math
import jax
import jax.numpy as jnp
from jax import lax

LON = 1440
LAT = 192
HOURS = 16


def level_of(rng, shape, pieces, least, high):
    def one(axis_at, shards_of):
        heights = jax.random.uniform(jax.random.fold_in(jax.random.fold_in(rng, 6), axis_at), (shards_of,), jnp.float32, least / len(pieces), high / len(pieces))
        return jnp.repeat(jnp.exp(heights), shape[axis_at] // shards_of).reshape((-1,) + (1,) * (len(shape) - axis_at - 1))

    gain = one(*pieces[0])
    for cut in pieces[1:]:
        gain = gain * one(*cut)
    return gain


def centred(key, extent, spread, bound, pieces=(), dtype=jnp.bfloat16):
    drawn = jax.random.normal(key, extent, jnp.float32) * spread
    if len(pieces) > 0:
        drawn = level_of(key, extent, pieces, -0.22, 0.18) * drawn
    return jnp.clip(drawn, min=-bound, max=bound).astype(dtype)


def setup_inputs(seed: int = 0) -> dict:
    arg_keys = jax.random.split(jax.random.key(seed), 5)
    return {
        "observed": centred(arg_keys[0], (HOURS, LAT, LON), 1.5, 8.0, ((0, 8), (1, 32)), jnp.float32),
        "noise_var": jnp.clip(jnp.exp(jax.random.uniform(arg_keys[1], (HOURS,), jnp.float32, math.log(0.05), math.log(1.0))), 0.05, 1.0),
        "spectral_var": jnp.clip(jnp.exp(math.log(5.0) - 3.218876 * jax.random.uniform(arg_keys[2], (LON, LAT), jnp.float32) ** level_of(arg_keys[2], (LON, LAT), ((0, 32),), -0.2, 0.2)), 0.2, 5.0),
        "time_scale": jnp.clip(jnp.exp(math.log(4.0) - 0.98082925 * jax.random.uniform(arg_keys[3], (LON, LAT), jnp.float32) ** level_of(arg_keys[3], (LON, LAT), ((0, 32),), -0.2, 0.2)), 1.5, 4.0),
    }


HIGHEST = lax.Precision.HIGHEST
ROOT_FIVE = 2.23606797749979
NILPOTENT = ((1.0, 1.0, 0.0), (0.0, 1.0, 1.0), (-1.0, -3.0, -2.0))
NILPOTENT_SQUARED = ((1.0, 2.0, 1.0), (-1.0, -2.0, -1.0), (1.0, 2.0, 1.0))
STATIONARY = ((1.0, 0.0, -1.0 / 3.0), (0.0, 1.0 / 3.0, 0.0), (-1.0 / 3.0, 0.0, 1.0))

def lon_basis(size):
    mode_index = lax.broadcasted_iota(jnp.int32, (size, size), 0)
    longitude = lax.broadcasted_iota(jnp.int32, (size, size), 1)
    half_size = size // 2
    sine_rows = mode_index > half_size
    frequency = jnp.where(sine_rows, mode_index - half_size, mode_index)
    radians = (frequency * longitude % size).astype(jnp.float32) * (2.0 * math.pi / size)
    waveform = jnp.where(sine_rows, jnp.sin(radians), jnp.cos(radians))
    edge_rows = (mode_index == 0) | (mode_index == half_size)
    weight = jnp.where(edge_rows, math.sqrt(1.0 / size), math.sqrt(2.0 / size))
    return waveform * weight

def lat_basis(size):
    wavenumber = lax.broadcasted_iota(jnp.int32, (size, size), 0)
    latitude = lax.broadcasted_iota(jnp.int32, (size, size), 1)
    radians = (wavenumber * (2 * latitude + 1) % (4 * size)).astype(jnp.float32) * (math.pi / (2.0 * size))
    weight = jnp.where(wavenumber == 0, math.sqrt(1.0 / size), math.sqrt(2.0 / size))
    return jnp.cos(radians) * weight

def mat_mul(left, right):
    return [[left[across][0] * right[0][within] + left[across][1] * right[1][within] + left[across][2] * right[2][within] for within in range(3)] for across in range(3)]

def mat_vec(matrix, vector):
    return [matrix[across][0] * vector[0] + matrix[across][1] * vector[1] + matrix[across][2] * vector[2] for across in range(3)]

def transposed(matrix):
    return [[matrix[within][across] for within in range(3)] for across in range(3)]

def inverted(matrix):
    cofactor = [[matrix[1][1] * matrix[2][2] - matrix[1][2] * matrix[2][1], matrix[0][2] * matrix[2][1] - matrix[0][1] * matrix[2][2], matrix[0][1] * matrix[1][2] - matrix[0][2] * matrix[1][1]], [matrix[1][2] * matrix[2][0] - matrix[1][0] * matrix[2][2], matrix[0][0] * matrix[2][2] - matrix[0][2] * matrix[2][0], matrix[0][2] * matrix[1][0] - matrix[0][0] * matrix[1][2]], [matrix[1][0] * matrix[2][1] - matrix[1][1] * matrix[2][0], matrix[0][1] * matrix[2][0] - matrix[0][0] * matrix[2][1], matrix[0][0] * matrix[1][1] - matrix[0][1] * matrix[1][0]]]
    determinant = matrix[0][0] * cofactor[0][0] + matrix[0][1] * cofactor[1][0] + matrix[0][2] * cofactor[2][0]
    return [[cofactor[across][within] / determinant for within in range(3)] for across in range(3)]

def model_terms(variance, scale):
    decay_rate = ROOT_FIVE / scale
    damping = jnp.exp(-decay_rate)
    transition = [[damping * ((1.0 if across == within else 0.0) + decay_rate * NILPOTENT[across][within] + 0.5 * decay_rate * decay_rate * NILPOTENT_SQUARED[across][within]) for within in range(3)] for across in range(3)]
    stationary = [[variance * STATIONARY[across][within] for within in range(3)] for across in range(3)]
    carried = mat_mul(mat_mul(transition, stationary), transposed(transition))
    process_noise = [[stationary[across][within] - carried[across][within] for within in range(3)] for across in range(3)]
    return (transition, stationary, process_noise)

def predict_cov(covariance, transition, process_noise):
    carried = mat_mul(mat_mul(transition, covariance), transposed(transition))
    return [[carried[across][within] + process_noise[across][within] for within in range(3)] for across in range(3)]

def gain_and_cov(predicted_cov, noise):
    innovation_var = predicted_cov[0][0] + noise
    kalman_gain = [predicted_cov[across][0] / innovation_var for across in range(3)]
    covariance = [[predicted_cov[across][within] - kalman_gain[across] * predicted_cov[0][within] for within in range(3)] for across in range(3)]
    return (kalman_gain, covariance)

def smooth_series(spectra, noise_var, variance, scale):
    transition, stationary, process_noise = model_terms(variance, scale)
    zeros = jnp.zeros_like(variance)

    def forward(carry, inputs):
        mean_state, covariance = carry
        observed, noise = inputs
        predicted_cov = predict_cov(covariance, transition, process_noise)
        smoother_gain = mat_mul(mat_mul(covariance, transposed(transition)), inverted(predicted_cov))
        predicted = mat_vec(transition, mean_state)
        kalman_gain, covariance = gain_and_cov(predicted_cov, noise)
        residual = observed - predicted[0]
        mean_state = [predicted[across] + kalman_gain[across] * residual for across in range(3)]
        return ((mean_state, covariance), (mean_state, smoother_gain))
    _, (means, gains) = lax.scan(forward, ([zeros, zeros, zeros], stationary), (spectra, noise_var))

    def backward(later, inputs):
        mean_state, smoother_gain = inputs
        projected = mat_vec(transition, mean_state)
        difference = [later[across] - projected[across] for across in range(3)]
        correction = mat_vec(smoother_gain, difference)
        smoothed_state = [mean_state[across] + correction[across] for across in range(3)]
        return (smoothed_state, smoothed_state[0])
    last_state = [means[across][-1] for across in range(3)]
    earlier_means = [means[across][:-1] for across in range(3)]
    next_gains = [[gains[across][within][1:] for within in range(3)] for across in range(3)]
    _, field = lax.scan(backward, last_state, (earlier_means, next_gains), reverse=True)
    return jnp.concatenate([field, last_state[0][None]], axis=0)

def reference(observed, noise_var, spectral_var, time_scale):
    lon_table = lon_basis(LON)
    lat_table = lat_basis(LAT)
    spectra = jnp.einsum('hal,jl->hja', observed, lon_table, precision=HIGHEST)
    spectra = jnp.einsum('hja,na->hjn', spectra, lat_table, precision=HIGHEST)
    blocks = 16
    shaped = spectra.reshape(HOURS, blocks, LON // blocks, LAT).transpose(1, 0, 2, 3)
    variances = spectral_var.reshape(blocks, LON // blocks, LAT)
    scales = time_scale.reshape(blocks, LON // blocks, LAT)

    def per_block(bundle):
        series, variance, scale = bundle
        return smooth_series(series, noise_var, variance, scale)
    smooth = lax.map(per_block, (shaped, variances, scales))
    smooth = smooth.transpose(1, 0, 2, 3).reshape(HOURS, LON, LAT)
    latitude_grid = jnp.einsum('hjn,na->hja', smooth, lat_table, precision=HIGHEST)
    return jnp.einsum('hja,jl->hal', latitude_grid, lon_table, precision=HIGHEST)
```

```python
import functools
import math

import jax
import jax.numpy as jnp
import ml_dtypes
import numpy as np
from jax import lax
from jax.experimental import pallas as pl
from jax.experimental.pallas import tpu as pltpu
from jax.sharding import PartitionSpec as P

ROOT_FIVE = 2.23606797749979
NILPOTENT = ((1.0, 1.0, 0.0), (0.0, 1.0, 1.0), (-1.0, -3.0, -2.0))
NILPOTENT_SQUARED = ((1.0, 2.0, 1.0), (-1.0, -2.0, -1.0), (1.0, 2.0, 1.0))
STATIONARY = ((1.0, 0.0, -1.0 / 3.0), (0.0, 1.0 / 3.0, 0.0), (-1.0 / 3.0, 0.0, 1.0))
F32 = jnp.float32
BF16 = jnp.bfloat16
SUB = 8
LANES = 128
MIB = 2**20


def two_halves(table):
    high = table.astype(ml_dtypes.bfloat16)
    low = (table - high.astype(np.float64)).astype(ml_dtypes.bfloat16)
    return np.stack([high, low], axis=-3)


def lon_basis(size):
    mode = np.arange(size)[:, None]
    longitude = np.arange(size)[None, :]
    half = size // 2
    sine = mode > half
    frequency = np.where(sine, mode - half, mode)
    radians = (frequency * longitude % size) * (2.0 * math.pi / size)
    weight = np.where((mode == 0) | (mode == half), math.sqrt(1.0 / size), math.sqrt(2.0 / size))
    return np.where(sine, np.sin(radians), np.cos(radians)) * weight


def lat_basis(size):
    wavenumber = np.arange(size)[:, None]
    latitude = np.arange(size)[None, :]
    radians = (wavenumber * (2 * latitude + 1) % (4 * size)) * (math.pi / (2.0 * size))
    weight = np.where(wavenumber == 0, math.sqrt(1.0 / size), math.sqrt(2.0 / size))
    return np.cos(radians) * weight


def lon_tables(size, hour_blocks, bands):
    per_band = size // bands
    slots = -(-per_band // hour_blocks)
    half_slots = slots // 2
    basis = lon_basis(size)
    parity = np.arange(2)[:, None, None, None]
    slot = np.arange(half_slots)[None, :, None, None]
    block = np.arange(hour_blocks)[None, None, :, None]
    band = np.arange(bands)[None, None, None, :]
    within = slots * block + 2 * slot + (band * per_band + parity) % 2
    mode = np.where(within < per_band, per_band * band + within, 0)
    rows = basis[mode] * (within < per_band)[..., None]
    return rows.reshape(2, half_slots, hour_blocks * bands, size)[..., : size // 2]


def split(value):
    high = value.astype(BF16)
    return high, (value - high.astype(F32)).astype(BF16)


def product(value, table_high, table_low):
    rows = value.shape[0]
    high, low = split(value)
    both = jnp.dot(jnp.concatenate([high, low], axis=0), table_high, preferred_element_type=F32)
    return both[:rows] + both[rows:] + jnp.dot(high, table_low, preferred_element_type=F32)


def analyse_kernel(x_ref, table_ref, out_ref, folded, slots_of, table, sems):
    hours, lats, lon = x_ref.shape
    half_slots = table_ref.shape[1]
    copies = [
        pltpu.make_async_copy(table_ref.at[p, k], table.at[p, k], sems.at[p, k])
        for p in range(2)
        for k in range(half_slots)
    ]
    for copy in copies:
        copy.start()
    folded[...] = jnp.zeros_like(folded)
    slots_of[...] = jnp.zeros_like(slots_of)
    for h in range(hours):
        left = x_ref[h, :, : lon // 2]
        right = x_ref[h, :, lon // 2 :]
        folded[0, h * SUB : h * SUB + lats, :] = left + right
        folded[1, h * SUB : h * SUB + lats, :] = left - right
    rows = hours * SUB
    for p in range(2):
        value = folded[p]
        for k in range(half_slots):
            at = p * half_slots + k
            copies[at].wait()
            slots_of[at * rows : (at + 1) * rows, :] = product(value, table[p, k, 0], table[p, k, 1])
    out_ref[...] = slots_of[...].T


def gains_kernel(half_slots, where_ref, noise_ref, var_ref, scale_ref, trans_ref, gain_ref, var, scale):
    block = where_ref[0]
    odd = where_ref[1]
    last = var_ref.shape[0] - 1
    var[...] = jnp.ones_like(var)
    scale[...] = jnp.ones_like(scale)
    for p in range(2):
        for k in range(half_slots):
            row = jnp.minimum(2 * half_slots * block + 2 * k + (odd + p) % 2, last)
            at = p * half_slots + k
            var[at : at + 1, :] = var_ref[pl.ds(row, 1), :]
            scale[at : at + 1, :] = scale_ref[pl.ds(row, 1), :]
    variance = var[...]
    rate = ROOT_FIVE / scale[...]
    damping = jnp.exp(-rate)
    a = [
        [
            damping
            * (
                (1.0 if i == j else 0.0)
                + rate * NILPOTENT[i][j]
                + 0.5 * rate * rate * NILPOTENT_SQUARED[i][j]
            )
            for j in range(3)
        ]
        for i in range(3)
    ]
    for i in range(3):
        for j in range(3):
            trans_ref[3 * i + j] = a[i][j]

    def carried(cov):
        ap = [[a[i][0] * cov[0][j] + a[i][1] * cov[1][j] + a[i][2] * cov[2][j] for j in range(3)] for i in range(3)]
        upper = {
            (i, j): ap[i][0] * a[j][0] + ap[i][1] * a[j][1] + ap[i][2] * a[j][2]
            for i in range(3)
            for j in range(i, 3)
        }
        return [[upper[min(i, j), max(i, j)] for j in range(3)] for i in range(3)]

    cov = [[variance * STATIONARY[i][j] for j in range(3)] for i in range(3)]
    start = carried(cov)
    noise_cov = [[cov[i][j] - start[i][j] for j in range(3)] for i in range(3)]
    for h in range(gain_ref.shape[0]):
        noise = noise_ref[h]
        moved = carried(cov)
        pm = {(i, j): moved[i][j] + noise_cov[i][j] for i in range(3) for j in range(i, 3)}
        inverse = 1.0 / (pm[0, 0] + noise)
        k = [pm[0, j] * inverse for j in range(3)]
        for j in range(3):
            gain_ref[h, j] = k[j]
        gain_ref[h, 3] = inverse
        first = [noise * k[j] for j in range(3)]
        c11 = pm[1, 1] - k[1] * pm[0, 1]
        c12 = pm[1, 2] - k[1] * pm[0, 2]
        c22 = pm[2, 2] - k[2] * pm[0, 2]
        cov = [[first[0], first[1], first[2]], [first[1], c11, c12], [first[2], c12, c22]]


def smooth_kernel(lats, noise_ref, x_ref, trans_ref, gain_ref, into_ref, back_ref, out_ref, turned, grid, series):
    owners, lanes = x_ref.shape
    hours = gain_ref.shape[0]
    bands = grid.shape[1] // lats
    blocks = owners // bands
    per_block = hours // blocks
    stride = per_block * SUB
    parts, _, width = turned.shape
    for part in range(parts):
        turned[part] = x_ref[part * width : (part + 1) * width, :].T
    per_part = width // bands
    for h in range(per_block):
        for lat in range(lats):
            for part in range(parts):
                rows = turned[part, pl.ds(h * SUB + lat, SUB, stride=stride), :]
                for t in range(per_part):
                    at = ((part * per_part + t) * per_block + h) * SUB
                    grid[at : at + SUB, lat * bands : (lat + 1) * bands] = rows[:, t * bands : (t + 1) * bands]
    series[...] = product(grid[...], into_ref[0], into_ref[1])

    a = [[trans_ref[3 * i + j] for j in range(3)] for i in range(3)]
    scaled = []
    mean = None
    for h in range(hours):
        seen = series[h * SUB : (h + 1) * SUB, :]
        if mean is None:
            error = seen
            mean = [gain_ref[h, j] * error for j in range(3)]
        else:
            ahead = [a[i][0] * mean[0] + a[i][1] * mean[1] + a[i][2] * mean[2] for i in range(3)]
            error = seen - ahead[0]
            mean = [ahead[j] + gain_ref[h, j] * error for j in range(3)]
        scaled.append(error * gain_ref[h, 3])
    adjoint = None
    for h in reversed(range(hours)):
        drop = scaled[h]
        if adjoint is not None:
            drop = drop + (gain_ref[h, 0] * adjoint[0] + gain_ref[h, 1] * adjoint[1] + gain_ref[h, 2] * adjoint[2])
        here = slice(h * SUB, (h + 1) * SUB)
        series[here, :] = series[here, :] - noise_ref[h] * drop
        if adjoint is None:
            adjoint = [-(a[0][j] * drop) for j in range(3)]
        else:
            less = adjoint[0] - drop
            adjoint = [a[0][j] * less + a[1][j] * adjoint[1] + a[2][j] * adjoint[2] for j in range(3)]

    grid[...] = product(series[...], back_ref[0], back_ref[1])
    turned[...] = jnp.zeros_like(turned)
    for h in range(per_block):
        for lat in range(lats):
            for part in range(parts):
                rows = jnp.concatenate(
                    [
                        grid[(t * per_block + h) * SUB : (t * per_block + h + 1) * SUB, lat * bands : (lat + 1) * bands]
                        for t in range(part * per_part, (part + 1) * per_part)
                    ],
                    axis=1,
                )
                turned[part, pl.ds(h * SUB + lat, SUB, stride=stride), :] = rows
    for part in range(parts):
        out_ref[part * width : (part + 1) * width, :] = turned[part].T


def synthesise_kernel(x_ref, table_ref, out_ref, turned):
    hours, lats, lon = out_ref.shape
    half_slots = table_ref.shape[1]
    rows = hours * SUB
    turned[...] = x_ref[...].T
    halves = []
    for p in range(2):
        total = None
        for k in range(half_slots):
            at = p * half_slots + k
            part = product(turned[at * rows : (at + 1) * rows, :], table_ref[p, k, 0], table_ref[p, k, 1])
            total = part if total is None else total + part
        halves.append(total)
    even, odd = halves
    for h in range(hours):
        here = slice(h * SUB, h * SUB + lats)
        out_ref[h, :, : lon // 2] = even[here] + odd[here]
        out_ref[h, :, lon // 2 :] = even[here] - odd[here]


def params(mib):
    return pltpu.CompilerParams(vmem_limit_bytes=mib * MIB)


def per_device(tables, observed, noise_var, spectral_var, time_scale):
    lon_into, lon_back, lat_into, lat_back = tables
    hours_dev, lat_dev, lon_size = observed.shape
    hours = noise_var.shape[0]
    owners = lon_into.shape[-1]
    half_slots = lon_into.shape[1]
    lat_size = lat_into.shape[-1]
    lanes = SUB * hours_dev * SUB
    vmem = pl.BlockSpec(memory_space=pltpu.VMEM)
    smem = pl.BlockSpec(memory_space=pltpu.SMEM)

    sent = pl.pallas_call(
        analyse_kernel,
        out_shape=jax.ShapeDtypeStruct((owners, lanes), F32),
        in_specs=[vmem, pl.BlockSpec(memory_space=pl.ANY)],
        out_specs=vmem,
        scratch_shapes=[
            pltpu.VMEM((2, hours_dev * SUB, lon_size // 2), F32),
            pltpu.VMEM((lanes, owners), F32),
            pltpu.VMEM(lon_into.shape, BF16),
            pltpu.SemaphoreType.DMA((2, half_slots)),
        ],
        compiler_params=params(16),
        name="analyse",
    )(observed, lon_into)
    got = lax.all_to_all(sent, ("tm", "space"), split_axis=0, concat_axis=0, tiled=True)

    where = jnp.stack([lax.axis_index("tm"), lax.axis_index("space") * spectral_var.shape[0] % 2]).astype(jnp.int32)
    transition, gains = pl.pallas_call(
        functools.partial(gains_kernel, half_slots),
        out_shape=(
            jax.ShapeDtypeStruct((9, SUB, lat_size), F32),
            jax.ShapeDtypeStruct((hours, 4, SUB, lat_size), F32),
        ),
        in_specs=[smem, smem, vmem, vmem],
        out_specs=(vmem, vmem),
        scratch_shapes=[pltpu.VMEM((SUB, lat_size), F32)] * 2,
        cost_estimate=pl.CostEstimate(flops=200 * hours * SUB * 256, bytes_accessed=2 * MIB, transcendentals=0),
        name="gains",
    )(where, noise_var, spectral_var, time_scale)

    smooth = pl.pallas_call(
        functools.partial(smooth_kernel, lat_dev),
        out_shape=jax.ShapeDtypeStruct((owners, lanes), F32),
        in_specs=[smem] + [vmem] * 5,
        out_specs=vmem,
        scratch_shapes=[
            pltpu.VMEM((owners // LANES, lanes, LANES), F32),
            pltpu.VMEM((hours * SUB, lat_size), F32),
            pltpu.VMEM((hours * SUB, lat_size), F32),
        ],
        compiler_params=params(16),
        name="smooth",
    )(noise_var, got, transition, gains, lat_into, lat_back)
    back = lax.all_to_all(smooth, ("tm", "space"), split_axis=0, concat_axis=0, tiled=True)

    return pl.pallas_call(
        synthesise_kernel,
        out_shape=jax.ShapeDtypeStruct(observed.shape, F32),
        in_specs=[vmem, vmem],
        out_specs=vmem,
        scratch_shapes=[pltpu.VMEM((lanes, owners), F32)],
        compiler_params=params(16),
        name="synthesise",
    )(back, lon_back)


def solution(mesh):
    placed = (P("tm", "space", None), P(), P("space", None), P("space", None))
    blocks, bands = mesh.shape["tm"], mesh.shape["space"]

    def whole(observed, noise_var, spectral_var, time_scale):
        lon_size = observed.shape[2]
        lat_size = spectral_var.shape[1]
        rows = lon_tables(lon_size, blocks, bands)
        by_lat = lat_basis(lat_size).reshape(lat_size, bands, lat_size // bands)
        by_lat = by_lat.transpose(0, 2, 1).reshape(lat_size, lat_size)
        tables = (
            two_halves(rows.transpose(0, 1, 3, 2)),
            two_halves(rows),
            two_halves(by_lat.T),
            two_halves(by_lat),
        )
        tables = tuple(jnp.asarray(table) for table in tables)
        return jax.shard_map(
            functools.partial(per_device, tables),
            mesh=mesh,
            in_specs=placed,
            out_specs=P("tm", "space", None),
            check_vma=False,
        )(observed, noise_var, spectral_var, time_scale)

    return whole
```

```python
import functools
import math

import jax
import jax.numpy as jnp
import ml_dtypes
import numpy as np
from jax import lax
from jax.experimental import pallas as pl
from jax.experimental.pallas import tpu as pltpu
from jax.sharding import PartitionSpec as P

ROOT_FIVE = 2.23606797749979
NILPOTENT = ((1.0, 1.0, 0.0), (0.0, 1.0, 1.0), (-1.0, -3.0, -2.0))
NILPOTENT_SQUARED = ((1.0, 2.0, 1.0), (-1.0, -2.0, -1.0), (1.0, 2.0, 1.0))
STATIONARY = ((1.0, 0.0, -1.0 / 3.0), (0.0, 1.0 / 3.0, 0.0), (-1.0 / 3.0, 0.0, 1.0))
F32 = jnp.float32
BF16 = jnp.bfloat16
SUB = 8
LANES = 128
STEP = 120
MIB = 2**20


def two_halves(table):
    high = table.astype(ml_dtypes.bfloat16)
    low = (table - high.astype(np.float64)).astype(ml_dtypes.bfloat16)
    return np.stack([high, low], axis=-3)


def lon_basis(size):
    mode = np.arange(size)[:, None]
    longitude = np.arange(size)[None, :]
    half = size // 2
    sine = mode > half
    frequency = np.where(sine, mode - half, mode)
    radians = (frequency * longitude % size) * (2.0 * math.pi / size)
    weight = np.where((mode == 0) | (mode == half), math.sqrt(1.0 / size), math.sqrt(2.0 / size))
    return np.where(sine, np.sin(radians), np.cos(radians)) * weight


def lat_basis(size):
    wavenumber = np.arange(size)[:, None]
    latitude = np.arange(size)[None, :]
    radians = (wavenumber * (2 * latitude + 1) % (4 * size)) * (math.pi / (2.0 * size))
    weight = np.where(wavenumber == 0, math.sqrt(1.0 / size), math.sqrt(2.0 / size))
    return np.cos(radians) * weight


def lon_tables(size, hour_blocks, bands):
    per_band = size // bands
    slots = -(-per_band // hour_blocks)
    half = size // 2
    slot = np.arange(slots)[:, None, None]
    block = np.arange(hour_blocks)[None, :, None]
    band = np.arange(bands)[None, None, :]
    within = slots * block + slot + 0 * band
    used = within < per_band
    mode = np.where(used, per_band * band + within, 0)
    rows = (lon_basis(size)[mode] * used[..., None]).reshape(slots, hour_blocks * bands, size)
    sine = mode > half
    frequency = np.where(sine, mode - half, mode)
    ahead = np.arange(size // STEP)[:, None, None, None] * STEP
    radians = (frequency * ahead % size) * (2.0 * math.pi / size)
    straight = np.where(used, np.cos(radians), 0.0)
    crossed = np.where(used & (mode % half != 0), np.sin(radians), 0.0) * np.where(sine, 1.0, -1.0)
    crossed = np.roll(crossed, bands // 2, axis=-1)
    turns = np.stack([straight, crossed]).reshape(2, size // STEP, slots, hour_blocks * bands)
    head = np.zeros((slots, hour_blocks * bands, LANES))
    head[..., :STEP] = rows[..., :STEP]
    return head, turns.transpose(2, 0, 1, 3).astype(np.float32)


def split(value):
    high = value.astype(BF16)
    return high, (value - high.astype(F32)).astype(BF16)


def product(value, table_high, table_low):
    rows = value.shape[0]
    high, low = split(value)
    both = jnp.dot(jnp.concatenate([high, low], axis=0), table_high, preferred_element_type=F32)
    return both[:rows] + both[rows:] + jnp.dot(high, table_low, preferred_element_type=F32)


def partners(value, bands):
    half = bands // 2
    width = value.shape[1]
    upper = lax.broadcasted_iota(jnp.int32, value.shape, 1) % bands >= half
    return jnp.where(upper, pltpu.roll(value, half, 1), pltpu.roll(value, width - half, 1))


def analyse_kernel(bands, x_hbm, table_hbm, turns_hbm, out_ref, x, table, turns, flat, blocks, slots_of, sems):
    lats, hours, lon = x.shape
    slots = table.shape[0]
    steps = lon // STEP
    rows = 2 * SUB
    fetch = [pltpu.make_async_copy(x_hbm, x, sems.at[0]), pltpu.make_async_copy(turns_hbm, turns, sems.at[1])]
    fetch += [pltpu.make_async_copy(table_hbm.at[m], table.at[m], sems.at[2 + m]) for m in range(slots)]
    fetch[0].start()
    fetch[2].start()
    fetch[1].start()
    for m in range(1, slots):
        fetch[2 + m].start()
    flat[...] = jnp.zeros_like(flat)
    blocks[...] = jnp.zeros_like(blocks)
    slots_of[...] = jnp.zeros_like(slots_of)
    fetch[0].wait()
    for lat in range(lats):
        flat[lat * hours : (lat + 1) * hours, :] = x[lat]
    for b in range(steps):
        blocks[b * rows : (b + 1) * rows, :STEP] = flat[:, b * STEP : (b + 1) * STEP]
    value = blocks[...]
    for m in range(slots):
        fetch[2 + m].wait()
        part = product(value, table[m, 0], table[m, 1])
        if m == 0:
            fetch[1].wait()
        straight = crossed = None
        for b in range(steps):
            here = part[b * rows : (b + 1) * rows]
            plain = here * turns[m, 0, b : b + 1, :]
            cross = here * turns[m, 1, b : b + 1, :]
            straight = plain if straight is None else straight + plain
            crossed = cross if crossed is None else crossed + cross
        slots_of[m * rows : (m + 1) * rows, :] = straight + partners(crossed, bands)
    out_ref[...] = slots_of[...].T


def gains_kernel(slots, where_ref, noise_ref, var_ref, scale_ref, out_ref, var, scale):
    last = var_ref.shape[0] - 1
    var[...] = jnp.ones_like(var)
    scale[...] = jnp.ones_like(scale)
    for m in range(slots):
        row = jnp.minimum(slots * where_ref[0] + m, last)
        var[m : m + 1, :] = var_ref[pl.ds(row, 1), :]
        scale[m : m + 1, :] = scale_ref[pl.ds(row, 1), :]
    variance = var[...]
    rate = ROOT_FIVE / scale[...]
    damping = jnp.exp(-rate)
    a = [
        [
            damping
            * (
                (1.0 if i == j else 0.0)
                + rate * NILPOTENT[i][j]
                + 0.5 * rate * rate * NILPOTENT_SQUARED[i][j]
            )
            for j in range(3)
        ]
        for i in range(3)
    ]
    for i in range(3):
        for j in range(3):
            out_ref[3 * i + j] = a[i][j]

    def carried(cov):
        ap = [[a[i][0] * cov[0][j] + a[i][1] * cov[1][j] + a[i][2] * cov[2][j] for j in range(3)] for i in range(3)]
        upper = {
            (i, j): ap[i][0] * a[j][0] + ap[i][1] * a[j][1] + ap[i][2] * a[j][2]
            for i in range(3)
            for j in range(i, 3)
        }
        return [[upper[min(i, j), max(i, j)] for j in range(3)] for i in range(3)]

    cov = [[variance * STATIONARY[i][j] for j in range(3)] for i in range(3)]
    start = carried(cov)
    noise_cov = [[cov[i][j] - start[i][j] for j in range(3)] for i in range(3)]
    for h in range((out_ref.shape[0] - 9) // 4):
        noise = noise_ref[h]
        moved = carried(cov)
        pm = {(i, j): moved[i][j] + noise_cov[i][j] for i in range(3) for j in range(i, 3)}
        inverse = 1.0 / (pm[0, 0] + noise)
        k = [pm[0, j] * inverse for j in range(3)]
        for j in range(3):
            out_ref[9 + 4 * h + j] = k[j]
        out_ref[9 + 4 * h + 3] = inverse
        first = [noise * k[j] for j in range(3)]
        c11 = pm[1, 1] - k[1] * pm[0, 1]
        c12 = pm[1, 2] - k[1] * pm[0, 2]
        c22 = pm[2, 2] - k[2] * pm[0, 2]
        cov = [[first[0], first[1], first[2]], [first[1], c11, c12], [first[2], c12, c22]]


def smooth_kernel(lats, noise_ref, x_ref, gain_ref, into_ref, back_ref, out_ref, turned, grid, series):
    owners, lanes = x_ref.shape
    hours = (gain_ref.shape[0] - 9) // 4
    bands = grid.shape[1] // lats
    blocks = owners // bands
    per_block = hours // blocks
    stride = per_block * SUB
    parts, _, width = turned.shape
    for part in range(parts):
        turned[part] = x_ref[part * width : (part + 1) * width, :].T
    per_part = width // bands
    for h in range(per_block):
        for lat in range(lats):
            for part in range(parts):
                rows = turned[part, pl.ds(lat * per_block + h, SUB, stride=stride), :]
                for t in range(per_part):
                    at = ((part * per_part + t) * per_block + h) * SUB
                    grid[at : at + SUB, lat * bands : (lat + 1) * bands] = rows[:, t * bands : (t + 1) * bands]
    series[...] = product(grid[...], into_ref[0], into_ref[1])

    a = [[gain_ref[3 * i + j] for j in range(3)] for i in range(3)]
    scaled = []
    mean = None
    for h in range(hours):
        seen = series[h * SUB : (h + 1) * SUB, :]
        if mean is None:
            error = seen
            mean = [gain_ref[9 + 4 * h + j] * error for j in range(3)]
        else:
            ahead = [a[i][0] * mean[0] + a[i][1] * mean[1] + a[i][2] * mean[2] for i in range(3)]
            error = seen - ahead[0]
            mean = [ahead[j] + gain_ref[9 + 4 * h + j] * error for j in range(3)]
        scaled.append(error * gain_ref[9 + 4 * h + 3])
    adjoint = None
    for h in reversed(range(hours)):
        drop = scaled[h]
        if adjoint is not None:
            drop = drop + (gain_ref[9 + 4 * h + 0] * adjoint[0] + gain_ref[9 + 4 * h + 1] * adjoint[1] + gain_ref[9 + 4 * h + 2] * adjoint[2])
        here = slice(h * SUB, (h + 1) * SUB)
        series[here, :] = series[here, :] - noise_ref[h] * drop
        if adjoint is None:
            adjoint = [-(a[0][j] * drop) for j in range(3)]
        else:
            less = adjoint[0] - drop
            adjoint = [a[0][j] * less + a[1][j] * adjoint[1] + a[2][j] * adjoint[2] for j in range(3)]

    grid[...] = product(series[...], back_ref[0], back_ref[1])
    turned[...] = jnp.zeros_like(turned)
    for h in range(per_block):
        for lat in range(lats):
            for part in range(parts):
                rows = jnp.concatenate(
                    [
                        grid[(t * per_block + h) * SUB : (t * per_block + h + 1) * SUB, lat * bands : (lat + 1) * bands]
                        for t in range(part * per_part, (part + 1) * per_part)
                    ],
                    axis=1,
                )
                turned[part, pl.ds(lat * per_block + h, SUB, stride=stride), :] = rows
    for part in range(parts):
        out_ref[part * width : (part + 1) * width, :] = turned[part].T


def synthesise_kernel(bands, x_ref, table_ref, turns_ref, out_ref, turned, flat):
    lats, hours, lon = out_ref.shape
    slots = table_ref.shape[0]
    steps = lon // STEP
    rows = 2 * SUB
    turned[...] = x_ref[...].T
    total = None
    for m in range(slots):
        plain = turned[m * rows : (m + 1) * rows, :]
        cross = partners(plain, bands)
        value = jnp.concatenate(
            [plain * turns_ref[m, 0, b : b + 1, :] + cross * turns_ref[m, 1, b : b + 1, :] for b in range(steps)], axis=0
        )
        part = product(value, table_ref[m, 0], table_ref[m, 1])
        total = part if total is None else total + part
    for b in range(steps):
        flat[:, b * STEP : (b + 1) * STEP] = total[b * rows : (b + 1) * rows, :STEP]
    for lat in range(lats):
        out_ref[lat] = flat[lat * hours : (lat + 1) * hours, :]


def params(mib):
    return pltpu.CompilerParams(vmem_limit_bytes=mib * MIB)


def per_device(tables, observed, noise_var, spectral_var, time_scale):
    lon_into, lon_back, turns, lat_into, lat_back = tables
    hours_dev, lat_dev, lon_size = observed.shape
    hours = noise_var.shape[0]
    bands = lax.axis_size("space")
    slots, _, _, owners = lon_into.shape
    lat_size = lat_into.shape[-1]
    rows = 2 * SUB
    lanes = SUB * rows
    vmem = pl.BlockSpec(memory_space=pltpu.VMEM)
    smem = pl.BlockSpec(memory_space=pltpu.SMEM)
    hbm = pl.BlockSpec(memory_space=pltpu.HBM)

    by_lat = observed.transpose(1, 0, 2)
    sent = pl.pallas_call(
        functools.partial(analyse_kernel, bands),
        out_shape=jax.ShapeDtypeStruct((owners, lanes), F32),
        in_specs=[hbm] * 3,
        out_specs=vmem,
        scratch_shapes=[
            pltpu.VMEM(by_lat.shape, F32),
            pltpu.VMEM(lon_into.shape, BF16),
            pltpu.VMEM(turns.shape, F32),
            pltpu.VMEM((rows, lon_size), F32),
            pltpu.VMEM((lon_size // STEP * rows, LANES), F32),
            pltpu.VMEM((lanes, owners), F32),
            pltpu.SemaphoreType.DMA((2 + slots,)),
        ],
        compiler_params=params(16),
        name="analyse",
    )(*(pltpu.with_memory_space_constraint(each, pltpu.HBM) for each in (by_lat, lon_into, turns)))
    got = lax.all_to_all(sent, ("tm", "space"), split_axis=0, concat_axis=0, tiled=True)

    where = lax.axis_index("tm").astype(jnp.int32).reshape(1)
    gains = pl.pallas_call(
        functools.partial(gains_kernel, slots),
        out_shape=jax.ShapeDtypeStruct((9 + 4 * hours, SUB, lat_size), F32),
        in_specs=[smem, smem, vmem, vmem],
        out_specs=vmem,
        scratch_shapes=[pltpu.VMEM((SUB, lat_size), F32)] * 2,
        cost_estimate=pl.CostEstimate(flops=200 * hours * SUB * 256, bytes_accessed=2 * MIB, transcendentals=0),
        compiler_params=params(8),
        name="gains",
    )(where, noise_var, spectral_var, time_scale)

    smooth = pl.pallas_call(
        functools.partial(smooth_kernel, lat_dev),
        out_shape=jax.ShapeDtypeStruct((owners, lanes), F32),
        in_specs=[smem] + [vmem] * 4,
        out_specs=vmem,
        scratch_shapes=[
            pltpu.VMEM((owners // LANES, lanes, LANES), F32),
            pltpu.VMEM((hours * SUB, lat_size), F32),
            pltpu.VMEM((hours * SUB, lat_size), F32),
        ],
        compiler_params=params(16),
        name="smooth",
    )(noise_var, got, gains, lat_into, lat_back)
    back = lax.all_to_all(smooth, ("tm", "space"), split_axis=0, concat_axis=0, tiled=True)

    field = pl.pallas_call(
        functools.partial(synthesise_kernel, bands),
        out_shape=jax.ShapeDtypeStruct(by_lat.shape, F32),
        in_specs=[vmem] * 3,
        out_specs=vmem,
        scratch_shapes=[pltpu.VMEM((lanes, owners), F32), pltpu.VMEM((rows, lon_size), F32)],
        compiler_params=params(16),
        name="synthesise",
    )(back, lon_back, turns)
    return field.transpose(1, 0, 2)


def solution(mesh):
    placed = (P("tm", "space", None), P(), P("space", None), P("space", None))
    blocks, bands = mesh.shape["tm"], mesh.shape["space"]

    def whole(observed, noise_var, spectral_var, time_scale):
        lon_size = observed.shape[2]
        lat_size = spectral_var.shape[1]
        head, turns = lon_tables(lon_size, blocks, bands)
        by_lat = lat_basis(lat_size).reshape(lat_size, bands, lat_size // bands)
        by_lat = by_lat.transpose(0, 2, 1).reshape(lat_size, lat_size)
        tables = (
            two_halves(head.transpose(0, 2, 1)),
            two_halves(head),
            turns,
            two_halves(by_lat.T),
            two_halves(by_lat),
        )
        tables = tuple(jnp.asarray(table) for table in tables)
        return jax.shard_map(
            functools.partial(per_device, tables),
            mesh=mesh,
            in_specs=placed,
            out_specs=P("tm", "space", None),
            check_vma=False,
        )(observed, noise_var, spectral_var, time_scale)

    return whole
```

```python
import functools
import math

import jax
import jax.numpy as jnp
import ml_dtypes
import numpy as np
from jax import lax
from jax.experimental import pallas as pl
from jax.experimental.pallas import tpu as pltpu
from jax.sharding import PartitionSpec as P

ROOT_FIVE = 2.23606797749979
NILPOTENT = ((1.0, 1.0, 0.0), (0.0, 1.0, 1.0), (-1.0, -3.0, -2.0))
NILPOTENT_SQUARED = ((1.0, 2.0, 1.0), (-1.0, -2.0, -1.0), (1.0, 2.0, 1.0))
STATIONARY = ((1.0, 0.0, -1.0 / 3.0), (0.0, 1.0 / 3.0, 0.0), (-1.0 / 3.0, 0.0, 1.0))
F32 = jnp.float32
BF16 = jnp.bfloat16
SUB = 8
LANES = 128
STEP = 120
MIB = 2**20


def two_halves(table):
    high = table.astype(ml_dtypes.bfloat16)
    low = (table - high.astype(np.float64)).astype(ml_dtypes.bfloat16)
    return np.stack([high, low], axis=-3)


def lon_basis(size):
    mode = np.arange(size)[:, None]
    longitude = np.arange(size)[None, :]
    half = size // 2
    sine = mode > half
    frequency = np.where(sine, mode - half, mode)
    radians = (frequency * longitude % size) * (2.0 * math.pi / size)
    weight = np.where((mode == 0) | (mode == half), math.sqrt(1.0 / size), math.sqrt(2.0 / size))
    return np.where(sine, np.sin(radians), np.cos(radians)) * weight


def lat_basis(size):
    wavenumber = np.arange(size)[:, None]
    latitude = np.arange(size)[None, :]
    radians = (wavenumber * (2 * latitude + 1) % (4 * size)) * (math.pi / (2.0 * size))
    weight = np.where(wavenumber == 0, math.sqrt(1.0 / size), math.sqrt(2.0 / size))
    return np.cos(radians) * weight


def lon_tables(size, hour_blocks, bands):
    per_band = size // bands
    slots = -(-per_band // hour_blocks)
    half = size // 2
    slot = np.arange(slots)[:, None, None]
    block = np.arange(hour_blocks)[None, :, None]
    band = np.arange(bands)[None, None, :]
    within = slots * block + slot + 0 * band
    used = within < per_band
    mode = np.where(used, per_band * band + within, 0)
    rows = (lon_basis(size)[mode] * used[..., None]).reshape(slots, hour_blocks * bands, size)
    sine = mode > half
    frequency = np.where(sine, mode - half, mode)
    ahead = np.arange(size // STEP)[:, None, None, None] * STEP
    radians = (frequency * ahead % size) * (2.0 * math.pi / size)
    straight = np.where(used, np.cos(radians), 0.0)
    crossed = np.where(used & (mode % half != 0), np.sin(radians), 0.0) * np.where(sine, 1.0, -1.0)
    crossed = np.roll(crossed, bands // 2, axis=-1)
    turns = np.stack([straight, crossed]).reshape(2, size // STEP, slots, hour_blocks * bands)
    head = np.zeros((slots, hour_blocks * bands, LANES))
    head[..., :STEP] = rows[..., :STEP]
    return head, turns.transpose(2, 0, 1, 3).astype(np.float32)


def split(value):
    high = value.astype(BF16)
    return high, (value - high.astype(F32)).astype(BF16)


def product(value, table_high, table_low):
    rows = value.shape[0]
    high, low = split(value)
    both = jnp.dot(jnp.concatenate([high, low], axis=0), table_high, preferred_element_type=F32)
    return both[:rows] + both[rows:] + jnp.dot(high, table_low, preferred_element_type=F32)


def partners(value, bands):
    half = bands // 2
    width = value.shape[1]
    upper = lax.broadcasted_iota(jnp.int32, value.shape, 1) % bands >= half
    return jnp.where(upper, pltpu.roll(value, half, 1), pltpu.roll(value, width - half, 1))


def analyse_kernel(bands, x_hbm, table_hbm, turns_hbm, out_ref, x, table, turns, flat, blocks, slots_of, sems):
    lats, hours, lon = x.shape
    slots = table.shape[0]
    steps = lon // STEP
    rows = 2 * SUB
    fetch = [
        pltpu.make_async_copy(here, there, sems.at[i])
        for i, (here, there) in enumerate(((x_hbm, x), (table_hbm, table), (turns_hbm, turns)))
    ]
    for copy in fetch:
        copy.start()
    flat[...] = jnp.zeros_like(flat)
    blocks[...] = jnp.zeros_like(blocks)
    slots_of[...] = jnp.zeros_like(slots_of)
    fetch[0].wait()
    for lat in range(lats):
        flat[lat * hours : (lat + 1) * hours, :] = x[lat]
    for b in range(steps):
        blocks[b * rows : (b + 1) * rows, :STEP] = flat[:, b * STEP : (b + 1) * STEP]
    value = blocks[...]
    for m in range(slots):
        if m == 0:
            fetch[1].wait()
        part = product(value, table[m, 0], table[m, 1])
        if m == 0:
            fetch[2].wait()
        straight = crossed = None
        for b in range(steps):
            here = part[b * rows : (b + 1) * rows]
            plain = here * turns[m, 0, b : b + 1, :]
            cross = here * turns[m, 1, b : b + 1, :]
            straight = plain if straight is None else straight + plain
            crossed = cross if crossed is None else crossed + cross
        slots_of[m * rows : (m + 1) * rows, :] = straight + partners(crossed, bands)
    out_ref[...] = slots_of[...].T


def gains_kernel(slots, where_ref, noise_ref, var_ref, scale_ref, out_ref, var, scale):
    last = var_ref.shape[0] - 1
    var[...] = jnp.ones_like(var)
    scale[...] = jnp.ones_like(scale)
    for m in range(slots):
        row = jnp.minimum(slots * where_ref[0] + m, last)
        var[m : m + 1, :] = var_ref[pl.ds(row, 1), :]
        scale[m : m + 1, :] = scale_ref[pl.ds(row, 1), :]
    variance = var[...]
    rate = ROOT_FIVE / scale[...]
    damping = jnp.exp(-rate)
    a = [
        [
            damping
            * (
                (1.0 if i == j else 0.0)
                + rate * NILPOTENT[i][j]
                + 0.5 * rate * rate * NILPOTENT_SQUARED[i][j]
            )
            for j in range(3)
        ]
        for i in range(3)
    ]
    for i in range(3):
        for j in range(3):
            out_ref[3 * i + j] = a[i][j]

    def carried(cov):
        ap = [[a[i][0] * cov[0][j] + a[i][1] * cov[1][j] + a[i][2] * cov[2][j] for j in range(3)] for i in range(3)]
        upper = {
            (i, j): ap[i][0] * a[j][0] + ap[i][1] * a[j][1] + ap[i][2] * a[j][2]
            for i in range(3)
            for j in range(i, 3)
        }
        return [[upper[min(i, j), max(i, j)] for j in range(3)] for i in range(3)]

    cov = [[variance * STATIONARY[i][j] for j in range(3)] for i in range(3)]
    start = carried(cov)
    noise_cov = [[cov[i][j] - start[i][j] for j in range(3)] for i in range(3)]
    for h in range((out_ref.shape[0] - 9) // 4):
        noise = noise_ref[h]
        moved = carried(cov)
        pm = {(i, j): moved[i][j] + noise_cov[i][j] for i in range(3) for j in range(i, 3)}
        inverse = 1.0 / (pm[0, 0] + noise)
        k = [pm[0, j] * inverse for j in range(3)]
        for j in range(3):
            out_ref[9 + 4 * h + j] = k[j]
        out_ref[9 + 4 * h + 3] = inverse
        first = [noise * k[j] for j in range(3)]
        c11 = pm[1, 1] - k[1] * pm[0, 1]
        c12 = pm[1, 2] - k[1] * pm[0, 2]
        c22 = pm[2, 2] - k[2] * pm[0, 2]
        cov = [[first[0], first[1], first[2]], [first[1], c11, c12], [first[2], c12, c22]]


def smooth_kernel(lats, noise_ref, x_ref, gain_ref, into_ref, back_ref, out_ref, turned, grid, series):
    owners, lanes = x_ref.shape
    hours = (gain_ref.shape[0] - 9) // 4
    bands = grid.shape[1] // lats
    blocks = owners // bands
    per_block = hours // blocks
    stride = per_block * SUB
    parts, _, width = turned.shape
    for part in range(parts):
        turned[part] = x_ref[part * width : (part + 1) * width, :].T
    per_part = width // bands
    for h in range(per_block):
        for lat in range(lats):
            for part in range(parts):
                rows = turned[part, pl.ds(lat * per_block + h, SUB, stride=stride), :]
                for t in range(per_part):
                    at = ((part * per_part + t) * per_block + h) * SUB
                    grid[at : at + SUB, lat * bands : (lat + 1) * bands] = rows[:, t * bands : (t + 1) * bands]
    series[...] = product(grid[...], into_ref[0], into_ref[1])

    a = [[gain_ref[3 * i + j] for j in range(3)] for i in range(3)]
    scaled = []
    mean = None
    for h in range(hours):
        seen = series[h * SUB : (h + 1) * SUB, :]
        if mean is None:
            error = seen
            mean = [gain_ref[9 + 4 * h + j] * error for j in range(3)]
        else:
            ahead = [a[i][0] * mean[0] + a[i][1] * mean[1] + a[i][2] * mean[2] for i in range(3)]
            error = seen - ahead[0]
            mean = [ahead[j] + gain_ref[9 + 4 * h + j] * error for j in range(3)]
        scaled.append(error * gain_ref[9 + 4 * h + 3])
    adjoint = None
    for h in reversed(range(hours)):
        drop = scaled[h]
        if adjoint is not None:
            drop = drop + (gain_ref[9 + 4 * h + 0] * adjoint[0] + gain_ref[9 + 4 * h + 1] * adjoint[1] + gain_ref[9 + 4 * h + 2] * adjoint[2])
        here = slice(h * SUB, (h + 1) * SUB)
        series[here, :] = series[here, :] - noise_ref[h] * drop
        if adjoint is None:
            adjoint = [-(a[0][j] * drop) for j in range(3)]
        else:
            less = adjoint[0] - drop
            adjoint = [a[0][j] * less + a[1][j] * adjoint[1] + a[2][j] * adjoint[2] for j in range(3)]

    grid[...] = product(series[...], back_ref[0], back_ref[1])
    turned[...] = jnp.zeros_like(turned)
    for h in range(per_block):
        for lat in range(lats):
            for part in range(parts):
                rows = jnp.concatenate(
                    [
                        grid[(t * per_block + h) * SUB : (t * per_block + h + 1) * SUB, lat * bands : (lat + 1) * bands]
                        for t in range(part * per_part, (part + 1) * per_part)
                    ],
                    axis=1,
                )
                turned[part, pl.ds(lat * per_block + h, SUB, stride=stride), :] = rows
    for part in range(parts):
        out_ref[part * width : (part + 1) * width, :] = turned[part].T


def synthesise_kernel(bands, x_ref, table_ref, turns_ref, out_ref, turned, flat):
    lats, hours, lon = out_ref.shape
    slots = table_ref.shape[0]
    steps = lon // STEP
    rows = 2 * SUB
    turned[...] = x_ref[...].T
    total = None
    for m in range(slots):
        plain = turned[m * rows : (m + 1) * rows, :]
        cross = partners(plain, bands)
        value = jnp.concatenate(
            [plain * turns_ref[m, 0, b : b + 1, :] + cross * turns_ref[m, 1, b : b + 1, :] for b in range(steps)], axis=0
        )
        part = product(value, table_ref[m, 0], table_ref[m, 1])
        total = part if total is None else total + part
    for b in range(steps):
        flat[:, b * STEP : (b + 1) * STEP] = total[b * rows : (b + 1) * rows, :STEP]
    for lat in range(lats):
        out_ref[lat] = flat[lat * hours : (lat + 1) * hours, :]


def params(mib):
    return pltpu.CompilerParams(vmem_limit_bytes=mib * MIB)


def per_device(tables, observed, noise_var, spectral_var, time_scale):
    lon_into, lon_back, turns, lat_into, lat_back = tables
    hours_dev, lat_dev, lon_size = observed.shape
    hours = noise_var.shape[0]
    bands = lax.axis_size("space")
    slots, _, _, owners = lon_into.shape
    lat_size = lat_into.shape[-1]
    rows = 2 * SUB
    lanes = SUB * rows
    vmem = pl.BlockSpec(memory_space=pltpu.VMEM)
    smem = pl.BlockSpec(memory_space=pltpu.SMEM)
    hbm = pl.BlockSpec(memory_space=pltpu.HBM)

    by_lat = observed.transpose(1, 0, 2)
    sent = pl.pallas_call(
        functools.partial(analyse_kernel, bands),
        out_shape=jax.ShapeDtypeStruct((owners, lanes), F32),
        in_specs=[hbm] * 3,
        out_specs=vmem,
        scratch_shapes=[
            pltpu.VMEM(by_lat.shape, F32),
            pltpu.VMEM(lon_into.shape, BF16),
            pltpu.VMEM(turns.shape, F32),
            pltpu.VMEM((rows, lon_size), F32),
            pltpu.VMEM((lon_size // STEP * rows, LANES), F32),
            pltpu.VMEM((lanes, owners), F32),
            pltpu.SemaphoreType.DMA((3,)),
        ],
        compiler_params=params(16),
        name="analyse",
    )(*(pltpu.with_memory_space_constraint(each, pltpu.HBM) for each in (by_lat, lon_into, turns)))
    got = lax.all_to_all(sent, ("tm", "space"), split_axis=0, concat_axis=0, tiled=True)

    where = lax.axis_index("tm").astype(jnp.int32).reshape(1)
    gains = pl.pallas_call(
        functools.partial(gains_kernel, slots),
        out_shape=jax.ShapeDtypeStruct((9 + 4 * hours, SUB, lat_size), F32),
        in_specs=[smem, smem, vmem, vmem],
        out_specs=vmem,
        scratch_shapes=[pltpu.VMEM((SUB, lat_size), F32)] * 2,
        cost_estimate=pl.CostEstimate(flops=200 * hours * SUB * 256, bytes_accessed=2 * MIB, transcendentals=0),
        compiler_params=params(8),
        name="gains",
    )(where, noise_var, spectral_var, time_scale)

    smooth = pl.pallas_call(
        functools.partial(smooth_kernel, lat_dev),
        out_shape=jax.ShapeDtypeStruct((owners, lanes), F32),
        in_specs=[smem] + [vmem] * 4,
        out_specs=vmem,
        scratch_shapes=[
            pltpu.VMEM((owners // LANES, lanes, LANES), F32),
            pltpu.VMEM((hours * SUB, lat_size), F32),
            pltpu.VMEM((hours * SUB, lat_size), F32),
        ],
        compiler_params=params(16),
        name="smooth",
    )(noise_var, got, gains, lat_into, lat_back)
    back = lax.all_to_all(smooth, ("tm", "space"), split_axis=0, concat_axis=0, tiled=True)

    field = pl.pallas_call(
        functools.partial(synthesise_kernel, bands),
        out_shape=jax.ShapeDtypeStruct(by_lat.shape, F32),
        in_specs=[vmem] * 3,
        out_specs=vmem,
        scratch_shapes=[pltpu.VMEM((lanes, owners), F32), pltpu.VMEM((rows, lon_size), F32)],
        compiler_params=params(16),
        name="synthesise",
    )(back, lon_back, turns)
    return field.transpose(1, 0, 2)


def solution(mesh):
    placed = (P("tm", "space", None), P(), P("space", None), P("space", None))
    blocks, bands = mesh.shape["tm"], mesh.shape["space"]

    def whole(observed, noise_var, spectral_var, time_scale):
        lon_size = observed.shape[2]
        lat_size = spectral_var.shape[1]
        head, turns = lon_tables(lon_size, blocks, bands)
        by_lat = lat_basis(lat_size).reshape(lat_size, bands, lat_size // bands)
        by_lat = by_lat.transpose(0, 2, 1).reshape(lat_size, lat_size)
        tables = (
            two_halves(head.transpose(0, 2, 1)),
            two_halves(head),
            turns,
            two_halves(by_lat.T),
            two_halves(by_lat),
        )
        tables = tuple(jnp.asarray(table) for table in tables)
        return jax.shard_map(
            functools.partial(per_device, tables),
            mesh=mesh,
            in_specs=placed,
            out_specs=P("tm", "space", None),
            check_vma=False,
        )(observed, noise_var, spectral_var, time_scale)

    return whole
```

```python
import functools
import math

import jax
import jax.numpy as jnp
import ml_dtypes
import numpy as np
from jax import lax
from jax.experimental import pallas as pl
from jax.experimental.pallas import tpu as pltpu
from jax.sharding import PartitionSpec as P

ROOT_FIVE = 2.23606797749979
NILPOTENT = ((1.0, 1.0, 0.0), (0.0, 1.0, 1.0), (-1.0, -3.0, -2.0))
NILPOTENT_SQUARED = ((1.0, 2.0, 1.0), (-1.0, -2.0, -1.0), (1.0, 2.0, 1.0))
STATIONARY = ((1.0, 0.0, -1.0 / 3.0), (0.0, 1.0 / 3.0, 0.0), (-1.0 / 3.0, 0.0, 1.0))
F32 = jnp.float32
BF16 = jnp.bfloat16
SUB = 8
LANES = 128
STEP = 120
STEP_BACK = 240
MIB = 2**20


def stacked(table):
    high = table.astype(ml_dtypes.bfloat16)
    low = (table - high.astype(np.float64)).astype(ml_dtypes.bfloat16)
    return np.concatenate([high, high, low], axis=-2)


def lon_basis(size):
    mode = np.arange(size)[:, None]
    longitude = np.arange(size)[None, :]
    half = size // 2
    sine = mode > half
    frequency = np.where(sine, mode - half, mode)
    radians = (frequency * longitude % size) * (2.0 * math.pi / size)
    weight = np.where((mode == 0) | (mode == half), math.sqrt(1.0 / size), math.sqrt(2.0 / size))
    return np.where(sine, np.sin(radians), np.cos(radians)) * weight


def lat_basis(size):
    wavenumber = np.arange(size)[:, None]
    latitude = np.arange(size)[None, :]
    radians = (wavenumber * (2 * latitude + 1) % (4 * size)) * (math.pi / (2.0 * size))
    weight = np.where(wavenumber == 0, math.sqrt(1.0 / size), math.sqrt(2.0 / size))
    return np.cos(radians) * weight


def lon_tables(size, step, hour_blocks, bands):
    per_band = size // bands
    slots = -(-per_band // hour_blocks)
    half = size // 2
    slot = np.arange(slots)[:, None, None]
    block = np.arange(hour_blocks)[None, :, None]
    band = np.arange(bands)[None, None, :]
    within = slots * block + slot + 0 * band
    used = within < per_band
    mode = np.where(used, per_band * band + within, 0)
    rows = (lon_basis(size)[mode] * used[..., None]).reshape(slots, hour_blocks * bands, size)
    sine = mode > half
    frequency = np.where(sine, mode - half, mode)
    ahead = np.arange(size // step)[:, None, None, None] * step
    radians = (frequency * ahead % size) * (2.0 * math.pi / size)
    straight = np.where(used, np.cos(radians), 0.0)
    crossed = np.where(used & (mode % half != 0), np.sin(radians), 0.0) * np.where(sine, 1.0, -1.0)
    crossed = np.roll(crossed, bands // 2, axis=-1)
    turns = np.stack([straight, crossed]).reshape(2, size // step, slots, hour_blocks * bands)
    head = np.zeros((slots, hour_blocks * bands, -(-step // LANES) * LANES))
    head[..., :step] = rows[..., :step]
    return head, turns.transpose(2, 0, 1, 3).astype(np.float32)


def all_tables(lon_size, lat_size, blocks, bands):
    head, turns = lon_tables(lon_size, STEP, blocks, bands)
    slots, owners, _ = head.shape
    into = np.concatenate([head[..., :STEP].transpose(0, 2, 1), turns.reshape(slots, -1, owners)], axis=1)
    head, turns = lon_tables(lon_size, STEP_BACK, blocks, bands)
    back = stacked(head).reshape(-1, head.shape[-1])
    by_lat = lat_basis(lat_size).reshape(lat_size, bands, lat_size // bands)
    by_lat = by_lat.transpose(0, 2, 1).reshape(lat_size, lat_size)
    pad = -lat_size % (2 * LANES)
    by_lat = np.pad(by_lat, ((0, pad), (0, pad)))
    return into.astype(np.float32), back, turns, stacked(by_lat.T), stacked(by_lat)


def split(value):
    high = value.astype(BF16)
    return high, (value - high.astype(F32)).astype(BF16)


def spread(value):
    high, low = split(value)
    return jnp.concatenate([high, low, high], axis=1)


def product(value, table):
    return jnp.dot(spread(value), table, preferred_element_type=F32)


def partners(value, bands):
    half = bands // 2
    width = value.shape[1]
    upper = lax.broadcasted_iota(jnp.int32, value.shape, 1) % bands >= half
    return jnp.where(upper, pltpu.roll(value, half, 1), pltpu.roll(value, width - half, 1))


def analyse_kernel(bands, x_hbm, table_hbm, out_ref, x, table, flat, blocks, slots_of, sems):
    lats, hours, lon = x.shape
    slots = table.shape[0]
    steps = lon // STEP
    rows = 2 * SUB
    fetch = [pltpu.make_async_copy(x_hbm, x, sems.at[0]), pltpu.make_async_copy(table_hbm, table, sems.at[1])]
    for copy in fetch:
        copy.start()
    flat[...] = jnp.zeros_like(flat)
    blocks[...] = jnp.zeros_like(blocks)
    slots_of[...] = jnp.zeros_like(slots_of)
    fetch[0].wait()
    for lat in range(lats):
        flat[lat * hours : (lat + 1) * hours, :] = x[lat]
    for b in range(steps):
        blocks[b * rows : (b + 1) * rows, :STEP] = flat[:, b * STEP : (b + 1) * STEP]
    value = spread(blocks[...])
    fetch[1].wait()
    for m in range(slots):
        high, low = split(table[m, :LANES, :])
        part = jnp.dot(value, jnp.concatenate([high, high, low], axis=0), preferred_element_type=F32)
        straight = crossed = None
        for b in range(steps):
            here = part[b * rows : (b + 1) * rows]
            plain = here * table[m, STEP + b : STEP + b + 1, :]
            cross = here * table[m, STEP + steps + b : STEP + steps + b + 1, :]
            straight = plain if straight is None else straight + plain
            crossed = cross if crossed is None else crossed + cross
        slots_of[m * rows : (m + 1) * rows, :] = straight + partners(crossed, bands)
    out_ref[...] = slots_of[...].T


def gains_kernel(slots, where_ref, noise_ref, var_ref, scale_ref, out_ref, var, scale):
    last = var_ref.shape[0] - 1
    var[...] = jnp.ones_like(var)
    scale[...] = jnp.ones_like(scale)
    for m in range(slots):
        row = jnp.minimum(slots * where_ref[0] + m, last)
        var[m : m + 1, : var_ref.shape[1]] = var_ref[pl.ds(row, 1), :]
        scale[m : m + 1, : var_ref.shape[1]] = scale_ref[pl.ds(row, 1), :]
    variance = var[...]
    rate = ROOT_FIVE / scale[...]
    damping = jnp.exp(-rate)
    a = [
        [
            damping
            * (
                (1.0 if i == j else 0.0)
                + rate * NILPOTENT[i][j]
                + 0.5 * rate * rate * NILPOTENT_SQUARED[i][j]
            )
            for j in range(3)
        ]
        for i in range(3)
    ]
    for i in range(3):
        for j in range(3):
            out_ref[3 * i + j] = a[i][j]

    def carried(cov):
        ap = [[a[i][0] * cov[0][j] + a[i][1] * cov[1][j] + a[i][2] * cov[2][j] for j in range(3)] for i in range(3)]
        upper = {
            (i, j): ap[i][0] * a[j][0] + ap[i][1] * a[j][1] + ap[i][2] * a[j][2]
            for i in range(3)
            for j in range(i, 3)
        }
        return [[upper[min(i, j), max(i, j)] for j in range(3)] for i in range(3)]

    cov = [[variance * STATIONARY[i][j] for j in range(3)] for i in range(3)]
    start = carried(cov)
    noise_cov = [[cov[i][j] - start[i][j] for j in range(3)] for i in range(3)]
    for h in range((out_ref.shape[0] - 9) // 4):
        noise = noise_ref[h]
        moved = carried(cov)
        pm = {(i, j): moved[i][j] + noise_cov[i][j] for i in range(3) for j in range(i, 3)}
        inverse = 1.0 / (pm[0, 0] + noise)
        k = [pm[0, j] * inverse for j in range(3)]
        for j in range(3):
            out_ref[9 + 4 * h + j] = k[j]
        out_ref[9 + 4 * h + 3] = inverse
        first = [noise * k[j] for j in range(3)]
        c11 = pm[1, 1] - k[1] * pm[0, 1]
        c12 = pm[1, 2] - k[1] * pm[0, 2]
        c22 = pm[2, 2] - k[2] * pm[0, 2]
        cov = [[first[0], first[1], first[2]], [first[1], c11, c12], [first[2], c12, c22]]


def smooth_kernel(lats, bands, noise_ref, x_ref, gain_ref, into_ref, back_ref, out_ref, turned, grid, series):
    owners, lanes = x_ref.shape
    hours = (gain_ref.shape[0] - 9) // 4
    blocks = owners // bands
    per_block = hours // blocks
    stride = per_block * SUB
    parts, _, width = turned.shape
    for part in range(parts):
        turned[part] = x_ref[part * width : (part + 1) * width, :].T
    per_part = width // bands
    grid[:, lats * bands :] = jnp.zeros((grid.shape[0], grid.shape[1] - lats * bands), F32)
    for h in range(per_block):
        for lat in range(lats):
            for part in range(parts):
                rows = turned[part, pl.ds(lat * per_block + h, SUB, stride=stride), :]
                for t in range(per_part):
                    at = ((part * per_part + t) * per_block + h) * SUB
                    grid[at : at + SUB, lat * bands : (lat + 1) * bands] = rows[:, t * bands : (t + 1) * bands]
    series[...] = product(grid[...], into_ref[...])

    a = [[gain_ref[3 * i + j] for j in range(3)] for i in range(3)]
    scaled = []
    mean = None
    for h in range(hours):
        seen = series[h * SUB : (h + 1) * SUB, :]
        if mean is None:
            error = seen
            mean = [gain_ref[9 + 4 * h + j] * error for j in range(3)]
        else:
            ahead = [a[i][0] * mean[0] + a[i][1] * mean[1] + a[i][2] * mean[2] for i in range(3)]
            error = seen - ahead[0]
            mean = [ahead[j] + gain_ref[9 + 4 * h + j] * error for j in range(3)]
        scaled.append(error * gain_ref[9 + 4 * h + 3])
    adjoint = None
    for h in reversed(range(hours)):
        drop = scaled[h]
        if adjoint is not None:
            drop = drop + (gain_ref[9 + 4 * h + 0] * adjoint[0] + gain_ref[9 + 4 * h + 1] * adjoint[1] + gain_ref[9 + 4 * h + 2] * adjoint[2])
        here = slice(h * SUB, (h + 1) * SUB)
        series[here, :] = series[here, :] - noise_ref[h] * drop
        if adjoint is None:
            adjoint = [-(a[0][j] * drop) for j in range(3)]
        else:
            less = adjoint[0] - drop
            adjoint = [a[0][j] * less + a[1][j] * adjoint[1] + a[2][j] * adjoint[2] for j in range(3)]

    grid[...] = product(series[...], back_ref[...])
    turned[...] = jnp.zeros_like(turned)
    for h in range(per_block):
        for lat in range(lats):
            for part in range(parts):
                rows = jnp.concatenate(
                    [
                        grid[(t * per_block + h) * SUB : (t * per_block + h + 1) * SUB, lat * bands : (lat + 1) * bands]
                        for t in range(part * per_part, (part + 1) * per_part)
                    ],
                    axis=1,
                )
                turned[part, pl.ds(lat * per_block + h, SUB, stride=stride), :] = rows
    for part in range(parts):
        out_ref[part * width : (part + 1) * width, :] = turned[part].T


def synthesise_kernel(bands, x_ref, table_ref, turns_ref, out_ref, turned, flat):
    lats, hours, lon = out_ref.shape
    slots = turns_ref.shape[0]
    steps = lon // STEP_BACK
    rows = 2 * SUB
    turned[...] = x_ref[...].T
    values = []
    for m in range(slots):
        plain = turned[m * rows : (m + 1) * rows, :]
        cross = partners(plain, bands)
        turned_on = [
            plain * turns_ref[m, 0, b : b + 1, :] + cross * turns_ref[m, 1, b : b + 1, :] for b in range(steps)
        ]
        values.append(spread(jnp.concatenate(turned_on, axis=0)))
    total = jnp.dot(jnp.concatenate(values, axis=1), table_ref[...], preferred_element_type=F32)
    for b in range(steps):
        flat[:, b * STEP_BACK : (b + 1) * STEP_BACK] = total[b * rows : (b + 1) * rows, :STEP_BACK]
    for lat in range(lats):
        out_ref[lat] = flat[lat * hours : (lat + 1) * hours, :]


def params(mib):
    return pltpu.CompilerParams(vmem_limit_bytes=mib * MIB)


def per_device(tables, observed, noise_var, spectral_var, time_scale):
    lon_into, lon_back, turns, lat_into, lat_back = tables
    hours_dev, lat_dev, lon_size = observed.shape
    hours = noise_var.shape[0]
    bands = lax.axis_size("space")
    slots, _, owners = lon_into.shape
    lat_pad = lat_into.shape[-1]
    rows = 2 * SUB
    lanes = SUB * rows
    vmem = pl.BlockSpec(memory_space=pltpu.VMEM)
    smem = pl.BlockSpec(memory_space=pltpu.SMEM)
    hbm = pl.BlockSpec(memory_space=pltpu.HBM)

    by_lat = observed.transpose(1, 0, 2)
    sent = pl.pallas_call(
        functools.partial(analyse_kernel, bands),
        out_shape=jax.ShapeDtypeStruct((owners, lanes), F32),
        in_specs=[hbm] * 2,
        out_specs=vmem,
        scratch_shapes=[
            pltpu.VMEM(by_lat.shape, F32),
            pltpu.VMEM(lon_into.shape, F32),
            pltpu.VMEM((rows, lon_size), F32),
            pltpu.VMEM((lon_size // STEP * rows, LANES), F32),
            pltpu.VMEM((lanes, owners), F32),
            pltpu.SemaphoreType.DMA((2,)),
        ],
        compiler_params=params(16),
        name="analyse",
    )(*(pltpu.with_memory_space_constraint(each, pltpu.HBM) for each in (by_lat, lon_into)))
    got = lax.all_to_all(sent, ("tm", "space"), split_axis=0, concat_axis=0, tiled=True)

    where = lax.axis_index("tm").astype(jnp.int32).reshape(1)
    gains = pl.pallas_call(
        functools.partial(gains_kernel, slots),
        out_shape=jax.ShapeDtypeStruct((9 + 4 * hours, SUB, lat_pad), F32),
        in_specs=[smem, smem, vmem, vmem],
        out_specs=vmem,
        scratch_shapes=[pltpu.VMEM((SUB, lat_pad), F32)] * 2,
        cost_estimate=pl.CostEstimate(flops=200 * hours * SUB * 256, bytes_accessed=2 * MIB, transcendentals=0),
        compiler_params=params(8),
        name="gains",
    )(where, noise_var, spectral_var, time_scale)

    smooth = pl.pallas_call(
        functools.partial(smooth_kernel, lat_dev, bands),
        out_shape=jax.ShapeDtypeStruct((owners, lanes), F32),
        in_specs=[smem] + [vmem] * 4,
        out_specs=vmem,
        scratch_shapes=[
            pltpu.VMEM((owners // LANES, lanes, LANES), F32),
            pltpu.VMEM((hours * SUB, lat_pad), F32),
            pltpu.VMEM((hours * SUB, lat_pad), F32),
        ],
        compiler_params=params(16),
        name="smooth",
    )(noise_var, got, gains, lat_into, lat_back)
    back = lax.all_to_all(smooth, ("tm", "space"), split_axis=0, concat_axis=0, tiled=True)

    field = pl.pallas_call(
        functools.partial(synthesise_kernel, bands),
        out_shape=jax.ShapeDtypeStruct(by_lat.shape, F32),
        in_specs=[vmem] * 3,
        out_specs=vmem,
        scratch_shapes=[pltpu.VMEM((lanes, owners), F32), pltpu.VMEM((rows, lon_size), F32)],
        compiler_params=params(16),
        name="synthesise",
    )(back, lon_back, turns)
    return field.transpose(1, 0, 2)


def solution(mesh):
    placed = (P("tm", "space", None), P(), P("space", None), P("space", None))
    blocks, bands = mesh.shape["tm"], mesh.shape["space"]

    def whole(observed, noise_var, spectral_var, time_scale):
        lon_size = observed.shape[2]
        lat_size = spectral_var.shape[1]
        tables = all_tables(observed.shape[2], spectral_var.shape[1], blocks, bands)
        tables = tuple(jnp.asarray(table) for table in tables)
        return jax.shard_map(
            functools.partial(per_device, tables),
            mesh=mesh,
            in_specs=placed,
            out_specs=P("tm", "space", None),
            check_vma=False,
        )(observed, noise_var, spectral_var, time_scale)

    return whole
```

```python
import functools
import math

import jax
import jax.numpy as jnp
import ml_dtypes
import numpy as np
from jax import lax
from jax.experimental import pallas as pl
from jax.experimental.pallas import tpu as pltpu
from jax.sharding import PartitionSpec as P

ROOT_FIVE = 2.23606797749979
NILPOTENT = ((1.0, 1.0, 0.0), (0.0, 1.0, 1.0), (-1.0, -3.0, -2.0))
NILPOTENT_SQUARED = ((1.0, 2.0, 1.0), (-1.0, -2.0, -1.0), (1.0, 2.0, 1.0))
STATIONARY = ((1.0, 0.0, -1.0 / 3.0), (0.0, 1.0 / 3.0, 0.0), (-1.0 / 3.0, 0.0, 1.0))
F32 = jnp.float32
BF16 = jnp.bfloat16
SUB = 8
LANES = 128
PER_HOUR = 5
STEP = 120
STEP_BACK = 240
MIB = 2**20


def halves(table):
    high = table.astype(ml_dtypes.bfloat16)
    low = (table - high.astype(np.float64)).astype(ml_dtypes.bfloat16)
    return np.concatenate([high, low], axis=-2)


def lon_basis(size):
    mode = np.arange(size)[:, None]
    longitude = np.arange(size)[None, :]
    half = size // 2
    sine = mode > half
    frequency = np.where(sine, mode - half, mode)
    radians = (frequency * longitude % size) * (2.0 * math.pi / size)
    weight = np.where((mode == 0) | (mode == half), math.sqrt(1.0 / size), math.sqrt(2.0 / size))
    return np.where(sine, np.sin(radians), np.cos(radians)) * weight


def lat_basis(size):
    wavenumber = np.arange(size)[:, None]
    latitude = np.arange(size)[None, :]
    radians = (wavenumber * (2 * latitude + 1) % (4 * size)) * (math.pi / (2.0 * size))
    weight = np.where(wavenumber == 0, math.sqrt(1.0 / size), math.sqrt(2.0 / size))
    return np.cos(radians) * weight


def lon_tables(size, step, hour_blocks, bands):
    per_band = size // bands
    slots = -(-per_band // hour_blocks)
    half = size // 2
    slot = np.arange(slots)[:, None, None]
    block = np.arange(hour_blocks)[None, :, None]
    band = np.arange(bands)[None, None, :]
    within = slots * block + slot + 0 * band
    used = within < per_band
    mode = np.where(used, per_band * band + within, 0)
    rows = (lon_basis(size)[mode] * used[..., None]).reshape(slots, hour_blocks * bands, size)
    sine = mode > half
    frequency = np.where(sine, mode - half, mode)
    ahead = np.arange(size // step)[:, None, None, None] * step
    radians = (frequency * ahead % size) * (2.0 * math.pi / size)
    straight = np.where(used, np.cos(radians), 0.0)
    crossed = np.where(used & (mode % half != 0), np.sin(radians), 0.0) * np.where(sine, 1.0, -1.0)
    crossed = np.roll(crossed, bands // 2, axis=-1)
    turns = np.stack([straight, crossed]).reshape(2, size // step, slots, hour_blocks * bands)
    head = np.zeros((slots, hour_blocks * bands, -(-step // LANES) * LANES))
    head[..., :step] = rows[..., :step]
    return head, turns.transpose(2, 0, 1, 3).astype(np.float32)


def all_tables(lon_size, lat_size, blocks, bands):
    head, turns = lon_tables(lon_size, STEP, blocks, bands)
    slots, owners, _ = head.shape
    into = np.concatenate([head[..., :STEP].transpose(0, 2, 1), turns.reshape(slots, -1, owners)], axis=1)
    head, turns = lon_tables(lon_size, STEP_BACK, blocks, bands)
    back = halves(head).reshape(-1, head.shape[-1])
    by_lat = lat_basis(lat_size).reshape(lat_size, bands, lat_size // bands)
    by_lat = by_lat.transpose(0, 2, 1).reshape(lat_size, lat_size)
    pad = -lat_size % (2 * LANES)
    by_lat = np.pad(by_lat, ((0, pad), (0, pad)))
    later = np.concatenate([halves(by_lat.T), halves(by_lat), back], axis=0)
    return into.astype(np.float32), later, turns.reshape(-1, SUB, owners)


def split(value):
    high = value.astype(BF16)
    return high, (value - high.astype(F32)).astype(BF16)


def spread(value):
    high, low = split(value)
    return jnp.concatenate([high, low, high], axis=1)


def facing(table):
    depth = table.shape[0] // 2
    return [table[:depth], table[:depth], table[depth:]]


def product(value, table):
    return jnp.dot(spread(value), jnp.concatenate(facing(table), axis=0), preferred_element_type=F32)


def partners(value, bands):
    half = bands // 2
    width = value.shape[1]
    upper = lax.broadcasted_iota(jnp.int32, value.shape, 1) % bands >= half
    return jnp.where(upper, pltpu.roll(value, half, 1), pltpu.roll(value, width - half, 1))


def analyse_kernel(bands, x_hbm, table_hbm, out_ref, x, table, flat, blocks, slots_of, sems):
    lats, hours, lon = x.shape
    slots = table.shape[0]
    steps = lon // STEP
    rows = 2 * SUB
    fetch = [pltpu.make_async_copy(x_hbm, x, sems.at[0]), pltpu.make_async_copy(table_hbm, table, sems.at[1])]
    for copy in fetch:
        copy.start()
    flat[...] = jnp.zeros_like(flat)
    blocks[...] = jnp.zeros_like(blocks)
    slots_of[...] = jnp.zeros_like(slots_of)
    fetch[0].wait()
    for lat in range(lats):
        flat[lat * hours : (lat + 1) * hours, :] = x[lat]
    for b in range(steps):
        blocks[b * rows : (b + 1) * rows, :STEP] = flat[:, b * STEP : (b + 1) * STEP]
    value = spread(blocks[...])
    fetch[1].wait()
    for m in range(slots):
        high, low = split(table[m, :LANES, :])
        part = jnp.dot(value, jnp.concatenate([high, high, low], axis=0), preferred_element_type=F32)
        straight = crossed = None
        for b in range(steps):
            here = part[b * rows : (b + 1) * rows]
            plain = here * table[m, STEP + b : STEP + b + 1, :]
            cross = here * table[m, STEP + steps + b : STEP + steps + b + 1, :]
            straight = plain if straight is None else straight + plain
            crossed = cross if crossed is None else crossed + cross
        slots_of[m * rows : (m + 1) * rows, :] = straight + partners(crossed, bands)
    out_ref[...] = slots_of[...].T


def gains_kernel(
    slots, where_ref, noise_hbm, var_hbm, scale_hbm, later_hbm, turns_hbm,
    out_ref, later_ref, noise_ref, var_ref, scale_ref, var, scale, sems,
):
    pairs = (
        (noise_hbm, noise_ref),
        (var_hbm, var_ref),
        (scale_hbm, scale_ref),
        (later_hbm, later_ref),
        (turns_hbm, out_ref.at[: turns_hbm.shape[0]]),
    )
    fetch = [pltpu.make_async_copy(here, there, sems.at[i]) for i, (here, there) in enumerate(pairs)]
    for copy in fetch:
        copy.start()
    first_gain = turns_hbm.shape[0]
    last = var_ref.shape[0] - 1
    var[...] = jnp.ones_like(var)
    scale[...] = jnp.ones_like(scale)
    for copy in fetch[:3]:
        copy.wait()
    for m in range(slots):
        row = jnp.minimum(slots * where_ref[0] + m, last)
        var[m : m + 1, : var_ref.shape[1]] = var_ref[pl.ds(row, 1), :]
        scale[m : m + 1, : var_ref.shape[1]] = scale_ref[pl.ds(row, 1), :]
    variance = var[...]
    rate = ROOT_FIVE / scale[...]
    damping = jnp.exp(-rate)
    a = [
        [
            damping
            * (
                (1.0 if i == j else 0.0)
                + rate * NILPOTENT[i][j]
                + 0.5 * rate * rate * NILPOTENT_SQUARED[i][j]
            )
            for j in range(3)
        ]
        for i in range(3)
    ]
    for i in range(3):
        for j in range(3):
            out_ref[first_gain + 3 * i + j] = a[i][j]

    def carried(cov):
        ap = [[a[i][0] * cov[0][j] + a[i][1] * cov[1][j] + a[i][2] * cov[2][j] for j in range(3)] for i in range(3)]
        upper = {
            (i, j): ap[i][0] * a[j][0] + ap[i][1] * a[j][1] + ap[i][2] * a[j][2]
            for i in range(3)
            for j in range(i, 3)
        }
        return [[upper[min(i, j), max(i, j)] for j in range(3)] for i in range(3)]

    cov = [[variance * STATIONARY[i][j] for j in range(3)] for i in range(3)]
    start = carried(cov)
    noise_cov = [[cov[i][j] - start[i][j] for j in range(3)] for i in range(3)]
    for h in range((out_ref.shape[0] - first_gain - 9) // PER_HOUR):
        at = first_gain + 9 + PER_HOUR * h
        noise = noise_ref[h]
        moved = carried(cov)
        pm = {(i, j): moved[i][j] + noise_cov[i][j] for i in range(3) for j in range(i, 3)}
        inverse = 1.0 / (pm[0, 0] + noise)
        k = [pm[0, j] * inverse for j in range(3)]
        for j in range(3):
            out_ref[at + j] = k[j]
        out_ref[at + 3] = inverse
        out_ref[at + 4] = jnp.full(inverse.shape, noise, F32)
        first = [noise * k[j] for j in range(3)]
        c11 = pm[1, 1] - k[1] * pm[0, 1]
        c12 = pm[1, 2] - k[1] * pm[0, 2]
        c22 = pm[2, 2] - k[2] * pm[0, 2]
        cov = [[first[0], first[1], first[2]], [first[1], c11, c12], [first[2], c12, c22]]
    for copy in fetch[3:]:
        copy.wait()


def smooth_kernel(lats, bands, first_gain, x_ref, gain_ref, later_ref, out_ref, turned, grid, series):
    owners, lanes = x_ref.shape
    hours = (gain_ref.shape[0] - first_gain - 9) // PER_HOUR
    blocks = owners // bands
    per_block = hours // blocks
    stride = per_block * SUB
    parts, _, width = turned.shape
    for part in range(parts):
        turned[part] = x_ref[part * width : (part + 1) * width, :].T
    per_part = width // bands
    depth = 2 * grid.shape[1]
    grid[:, lats * bands :] = jnp.zeros((grid.shape[0], grid.shape[1] - lats * bands), F32)
    for h in range(per_block):
        for lat in range(lats):
            for part in range(parts):
                rows = turned[part, pl.ds(lat * per_block + h, SUB, stride=stride), :]
                for t in range(per_part):
                    at = ((part * per_part + t) * per_block + h) * SUB
                    grid[at : at + SUB, lat * bands : (lat + 1) * bands] = rows[:, t * bands : (t + 1) * bands]
    series[...] = product(grid[...], later_ref[:depth, :])

    a = [[gain_ref[first_gain + 3 * i + j] for j in range(3)] for i in range(3)]
    gain = lambda h, which: gain_ref[first_gain + 9 + PER_HOUR * h + which]
    scaled = []
    mean = None
    for h in range(hours):
        seen = series[h * SUB : (h + 1) * SUB, :]
        if mean is None:
            error = seen
            mean = [gain(h, j) * error for j in range(3)]
        else:
            ahead = [a[i][0] * mean[0] + a[i][1] * mean[1] + a[i][2] * mean[2] for i in range(3)]
            error = seen - ahead[0]
            mean = [ahead[j] + gain(h, j) * error for j in range(3)]
        scaled.append(error * gain(h, 3))
    adjoint = None
    for h in reversed(range(hours)):
        drop = scaled[h]
        if adjoint is not None:
            drop = drop + (gain(h, 0) * adjoint[0] + gain(h, 1) * adjoint[1] + gain(h, 2) * adjoint[2])
        here = slice(h * SUB, (h + 1) * SUB)
        series[here, :] = series[here, :] - gain(h, 4) * drop
        if adjoint is None:
            adjoint = [-(a[0][j] * drop) for j in range(3)]
        else:
            less = adjoint[0] - drop
            adjoint = [a[0][j] * less + a[1][j] * adjoint[1] + a[2][j] * adjoint[2] for j in range(3)]

    grid[...] = product(series[...], later_ref[depth : 2 * depth, :])
    turned[...] = jnp.zeros_like(turned)
    for h in range(per_block):
        for lat in range(lats):
            for part in range(parts):
                rows = jnp.concatenate(
                    [
                        grid[(t * per_block + h) * SUB : (t * per_block + h + 1) * SUB, lat * bands : (lat + 1) * bands]
                        for t in range(part * per_part, (part + 1) * per_part)
                    ],
                    axis=1,
                )
                turned[part, pl.ds(lat * per_block + h, SUB, stride=stride), :] = rows
    for part in range(parts):
        out_ref[part * width : (part + 1) * width, :] = turned[part].T


def synthesise_kernel(bands, slots, x_ref, later_ref, turns_ref, out_ref, turned, flat):
    lats, hours, lon = out_ref.shape
    steps = lon // STEP_BACK
    rows = 2 * SUB
    turned[...] = x_ref[...].T

    def turn(m, which, b):
        at = (2 * m + which) * steps + b
        return turns_ref[at // SUB, at % SUB : at % SUB + 1, :]

    values = []
    tables = []
    depth = 2 * x_ref.shape[0]
    first = later_ref.shape[0] - slots * depth
    for m in range(slots):
        tables += facing(later_ref[first + m * depth : first + (m + 1) * depth, :])
        plain = turned[m * rows : (m + 1) * rows, :]
        cross = partners(plain, bands)
        turned_on = [
            plain * turn(m, 0, b) + cross * turn(m, 1, b) for b in range(steps)
        ]
        values.append(spread(jnp.concatenate(turned_on, axis=0)))
    total = jnp.dot(
        jnp.concatenate(values, axis=1), jnp.concatenate(tables, axis=0), preferred_element_type=F32
    )
    for b in range(steps):
        flat[:, b * STEP_BACK : (b + 1) * STEP_BACK] = total[b * rows : (b + 1) * rows, :STEP_BACK]
    for lat in range(lats):
        out_ref[lat] = flat[lat * hours : (lat + 1) * hours, :]


def params(mib):
    return pltpu.CompilerParams(vmem_limit_bytes=mib * MIB)


def in_hbm(value):
    return pltpu.with_memory_space_constraint(value, pltpu.HBM)


def per_device(tables, observed, noise_var, spectral_var, time_scale):
    lon_into, later, turns = tables
    hours_dev, lat_dev, lon_size = observed.shape
    hours = noise_var.shape[0]
    bands = lax.axis_size("space")
    slots, _, owners = lon_into.shape
    lat_pad = later.shape[-1]
    rows = 2 * SUB
    lanes = SUB * rows
    vmem = pl.BlockSpec(memory_space=pltpu.VMEM)
    smem = pl.BlockSpec(memory_space=pltpu.SMEM)
    hbm = pl.BlockSpec(memory_space=pltpu.HBM)

    by_lat = observed.transpose(1, 0, 2)
    sent = pl.pallas_call(
        functools.partial(analyse_kernel, bands),
        out_shape=jax.ShapeDtypeStruct((owners, lanes), F32),
        in_specs=[hbm] * 2,
        out_specs=vmem,
        scratch_shapes=[
            pltpu.VMEM(by_lat.shape, F32),
            pltpu.VMEM(lon_into.shape, F32),
            pltpu.VMEM((rows, lon_size), F32),
            pltpu.VMEM((lon_size // STEP * rows, LANES), F32),
            pltpu.VMEM((lanes, owners), F32),
            pltpu.SemaphoreType.DMA((2,)),
        ],
        compiler_params=params(16),
        name="analyse",
    )(in_hbm(by_lat), in_hbm(lon_into))
    got = lax.all_to_all(sent, ("tm", "space"), split_axis=0, concat_axis=0, tiled=True)

    where = lax.axis_index("tm").astype(jnp.int32).reshape(1)
    gains, later = pl.pallas_call(
        functools.partial(gains_kernel, slots),
        out_shape=(
            jax.ShapeDtypeStruct((turns.shape[0] + 9 + PER_HOUR * hours, SUB, lat_pad), F32),
            jax.ShapeDtypeStruct(later.shape, BF16),
        ),
        in_specs=[smem] + [hbm] * 5,
        out_specs=(vmem,) * 2,
        scratch_shapes=[
            pltpu.SMEM(noise_var.shape, F32),
            pltpu.VMEM(spectral_var.shape, F32),
            pltpu.VMEM(spectral_var.shape, F32),
            pltpu.VMEM((SUB, lat_pad), F32),
            pltpu.VMEM((SUB, lat_pad), F32),
            pltpu.SemaphoreType.DMA((5,)),
        ],
        cost_estimate=pl.CostEstimate(flops=200 * hours * SUB * 256, bytes_accessed=8 * MIB, transcendentals=0),
        compiler_params=params(16),
        name="gains",
    )(where, *(in_hbm(each) for each in (noise_var, spectral_var, time_scale, later, turns)))

    smooth = pl.pallas_call(
        functools.partial(smooth_kernel, lat_dev, bands, turns.shape[0]),
        out_shape=jax.ShapeDtypeStruct((owners, lanes), F32),
        in_specs=[vmem] * 3,
        out_specs=vmem,
        scratch_shapes=[
            pltpu.VMEM((owners // LANES, lanes, LANES), F32),
            pltpu.VMEM((hours * SUB, lat_pad), F32),
            pltpu.VMEM((hours * SUB, lat_pad), F32),
        ],
        compiler_params=params(16),
        name="smooth",
    )(got, gains, later)
    back = lax.all_to_all(smooth, ("tm", "space"), split_axis=0, concat_axis=0, tiled=True)

    field = pl.pallas_call(
        functools.partial(synthesise_kernel, bands, slots),
        out_shape=jax.ShapeDtypeStruct(by_lat.shape, F32),
        in_specs=[vmem] * 3,
        out_specs=vmem,
        scratch_shapes=[pltpu.VMEM((lanes, owners), F32), pltpu.VMEM((rows, lon_size), F32)],
        compiler_params=params(16),
        name="synthesise",
    )(back, later, gains)
    return field.transpose(1, 0, 2)


def solution(mesh):
    placed = (P("tm", "space", None), P(), P("space", None), P("space", None))
    blocks, bands = mesh.shape["tm"], mesh.shape["space"]

    def whole(observed, noise_var, spectral_var, time_scale):
        lon_size = observed.shape[2]
        lat_size = spectral_var.shape[1]
        tables = all_tables(observed.shape[2], spectral_var.shape[1], blocks, bands)
        tables = tuple(jnp.asarray(table) for table in tables)
        return jax.shard_map(
            functools.partial(per_device, tables),
            mesh=mesh,
            in_specs=placed,
            out_specs=P("tm", "space", None),
            check_vma=False,
        )(observed, noise_var, spectral_var, time_scale)

    return whole
```

```python
import functools
import math

import jax
import jax.numpy as jnp
import ml_dtypes
import numpy as np
from jax import lax
from jax.experimental import pallas as pl
from jax.experimental.pallas import tpu as pltpu
from jax.sharding import PartitionSpec as P

ROOT_FIVE = 2.23606797749979
NILPOTENT = ((1.0, 1.0, 0.0), (0.0, 1.0, 1.0), (-1.0, -3.0, -2.0))
NILPOTENT_SQUARED = ((1.0, 2.0, 1.0), (-1.0, -2.0, -1.0), (1.0, 2.0, 1.0))
STATIONARY = ((1.0, 0.0, -1.0 / 3.0), (0.0, 1.0 / 3.0, 0.0), (-1.0 / 3.0, 0.0, 1.0))
F32 = jnp.float32
BF16 = jnp.bfloat16
SUB = 8
LANES = 128
PER_HOUR = 5
STEP = 120
STEP_BACK = 240
MIB = 2**20


def halves(table):
    high = table.astype(ml_dtypes.bfloat16)
    low = (table - high.astype(np.float64)).astype(ml_dtypes.bfloat16)
    return np.concatenate([high, low], axis=-2)


def lon_basis(size):
    mode = np.arange(size)[:, None]
    longitude = np.arange(size)[None, :]
    half = size // 2
    sine = mode > half
    frequency = np.where(sine, mode - half, mode)
    radians = (frequency * longitude % size) * (2.0 * math.pi / size)
    weight = np.where((mode == 0) | (mode == half), math.sqrt(1.0 / size), math.sqrt(2.0 / size))
    return np.where(sine, np.sin(radians), np.cos(radians)) * weight


def lat_basis(size):
    wavenumber = np.arange(size)[:, None]
    latitude = np.arange(size)[None, :]
    radians = (wavenumber * (2 * latitude + 1) % (4 * size)) * (math.pi / (2.0 * size))
    weight = np.where(wavenumber == 0, math.sqrt(1.0 / size), math.sqrt(2.0 / size))
    return np.cos(radians) * weight


def lon_tables(size, step, hour_blocks, bands):
    per_band = size // bands
    slots = -(-per_band // hour_blocks)
    half = size // 2
    slot = np.arange(slots)[:, None, None]
    block = np.arange(hour_blocks)[None, :, None]
    band = np.arange(bands)[None, None, :]
    within = slots * block + slot + 0 * band
    used = within < per_band
    mode = np.where(used, per_band * band + within, 0)
    rows = (lon_basis(size)[mode] * used[..., None]).reshape(slots, hour_blocks * bands, size)
    sine = mode > half
    frequency = np.where(sine, mode - half, mode)
    ahead = np.arange(size // step)[:, None, None, None] * step
    radians = (frequency * ahead % size) * (2.0 * math.pi / size)
    straight = np.where(used, np.cos(radians), 0.0)
    crossed = np.where(used & (mode % half != 0), np.sin(radians), 0.0) * np.where(sine, 1.0, -1.0)
    crossed = np.roll(crossed, bands // 2, axis=-1)
    turns = np.stack([straight, crossed]).reshape(2, size // step, slots, hour_blocks * bands)
    head = np.zeros((slots, hour_blocks * bands, -(-step // LANES) * LANES))
    head[..., :step] = rows[..., :step]
    return head, turns.transpose(2, 0, 1, 3).astype(np.float32)


def all_tables(lon_size, lat_size, blocks, bands):
    head, turns = lon_tables(lon_size, STEP, blocks, bands)
    slots, owners, _ = head.shape
    into = np.concatenate([head[..., :STEP].transpose(0, 2, 1), turns.reshape(slots, -1, owners)], axis=1)
    head, turns = lon_tables(lon_size, STEP_BACK, blocks, bands)
    back = halves(head).reshape(-1, head.shape[-1])
    by_lat = lat_basis(lat_size).reshape(lat_size, bands, lat_size // bands)
    by_lat = by_lat.transpose(0, 2, 1).reshape(lat_size, lat_size)
    pad = -lat_size % (2 * LANES)
    by_lat = np.pad(by_lat, ((0, pad), (0, pad)))
    later = np.concatenate([halves(by_lat.T), halves(by_lat), back], axis=0)
    return into.astype(np.float32), later, turns.reshape(-1, SUB, owners)


def split(value):
    high = value.astype(BF16)
    return high, (value - high.astype(F32)).astype(BF16)


def spread(value):
    high, low = split(value)
    return jnp.concatenate([high, low, high], axis=1)


def facing(table):
    depth = table.shape[0] // 2
    return [table[:depth], table[:depth], table[depth:]]


def product(value, table):
    return jnp.dot(spread(value), jnp.concatenate(facing(table), axis=0), preferred_element_type=F32)


def partners(value, bands):
    half = bands // 2
    width = value.shape[1]
    upper = lax.broadcasted_iota(jnp.int32, value.shape, 1) % bands >= half
    return jnp.where(upper, pltpu.roll(value, half, 1), pltpu.roll(value, width - half, 1))


def fill_gains(slots, first_gain, out_ref, noise_ref, var_ref, scale_ref, var, scale):
    last = var_ref.shape[0] - 1
    var[...] = jnp.ones_like(var)
    scale[...] = jnp.ones_like(scale)
    for m in range(slots):
        row = jnp.minimum(slots * lax.axis_index("tm") + m, last)
        var[m : m + 1, : var_ref.shape[1]] = var_ref[pl.ds(row, 1), :]
        scale[m : m + 1, : var_ref.shape[1]] = scale_ref[pl.ds(row, 1), :]
    variance = var[...]
    rate = ROOT_FIVE / scale[...]
    damping = jnp.exp(-rate)
    a = [
        [
            damping
            * (
                (1.0 if i == j else 0.0)
                + rate * NILPOTENT[i][j]
                + 0.5 * rate * rate * NILPOTENT_SQUARED[i][j]
            )
            for j in range(3)
        ]
        for i in range(3)
    ]
    for i in range(3):
        for j in range(3):
            out_ref[first_gain + 3 * i + j] = a[i][j]

    def carried(cov):
        ap = [[a[i][0] * cov[0][j] + a[i][1] * cov[1][j] + a[i][2] * cov[2][j] for j in range(3)] for i in range(3)]
        upper = {
            (i, j): ap[i][0] * a[j][0] + ap[i][1] * a[j][1] + ap[i][2] * a[j][2]
            for i in range(3)
            for j in range(i, 3)
        }
        return [[upper[min(i, j), max(i, j)] for j in range(3)] for i in range(3)]

    cov = [[variance * STATIONARY[i][j] for j in range(3)] for i in range(3)]
    start = carried(cov)
    noise_cov = [[cov[i][j] - start[i][j] for j in range(3)] for i in range(3)]
    for h in range((out_ref.shape[0] - first_gain - 9) // PER_HOUR):
        at = first_gain + 9 + PER_HOUR * h
        noise = noise_ref[h]
        moved = carried(cov)
        pm = {(i, j): moved[i][j] + noise_cov[i][j] for i in range(3) for j in range(i, 3)}
        inverse = 1.0 / (pm[0, 0] + noise)
        k = [pm[0, j] * inverse for j in range(3)]
        for j in range(3):
            out_ref[at + j] = k[j]
        out_ref[at + 3] = inverse
        out_ref[at + 4] = jnp.full(inverse.shape, noise, F32)
        first = [noise * k[j] for j in range(3)]
        c11 = pm[1, 1] - k[1] * pm[0, 1]
        c12 = pm[1, 2] - k[1] * pm[0, 2]
        c22 = pm[2, 2] - k[2] * pm[0, 2]
        cov = [[first[0], first[1], first[2]], [first[1], c11, c12], [first[2], c12, c22]]


def analyse_kernel(
    bands, x_hbm, table_hbm, noise_hbm, var_hbm, scale_hbm, turns_hbm, later_hbm, out_ref, gain_ref,
    later_ref, x, table, flat, blocks, slots_of, noise_ref, var_ref, scale_ref, var, scale, sems,
):
    lats, hours, lon = x.shape
    slots = table.shape[0]
    steps = lon // STEP
    rows = 2 * SUB
    pairs = (
        (x_hbm, x),
        (table_hbm, table),
        (noise_hbm, noise_ref),
        (var_hbm, var_ref),
        (scale_hbm, scale_ref),
        (turns_hbm, gain_ref.at[: turns_hbm.shape[0]]),
        (later_hbm, later_ref),
    )
    fetch = [pltpu.make_async_copy(here, there, sems.at[i]) for i, (here, there) in enumerate(pairs)]
    for copy in fetch:
        copy.start()
    flat[...] = jnp.zeros_like(flat)
    blocks[...] = jnp.zeros_like(blocks)
    slots_of[...] = jnp.zeros_like(slots_of)
    fetch[0].wait()
    for lat in range(lats):
        flat[lat * hours : (lat + 1) * hours, :] = x[lat]
    for b in range(steps):
        blocks[b * rows : (b + 1) * rows, :STEP] = flat[:, b * STEP : (b + 1) * STEP]
    value = spread(blocks[...])
    for copy in fetch[1:5]:
        copy.wait()
    fill_gains(slots, turns_hbm.shape[0], gain_ref, noise_ref, var_ref, scale_ref, var, scale)
    for m in range(slots):
        high, low = split(table[m, :LANES, :])
        part = jnp.dot(value, jnp.concatenate([high, high, low], axis=0), preferred_element_type=F32)
        straight = crossed = None
        for b in range(steps):
            here = part[b * rows : (b + 1) * rows]
            plain = here * table[m, STEP + b : STEP + b + 1, :]
            cross = here * table[m, STEP + steps + b : STEP + steps + b + 1, :]
            straight = plain if straight is None else straight + plain
            crossed = cross if crossed is None else crossed + cross
        slots_of[m * rows : (m + 1) * rows, :] = straight + partners(crossed, bands)
    out_ref[...] = slots_of[...].T
    for copy in fetch[5:]:
        copy.wait()


def smooth_kernel(lats, bands, first_gain, x_ref, gain_ref, later_ref, out_ref, turned, grid, series):
    owners, lanes = x_ref.shape
    hours = (gain_ref.shape[0] - first_gain - 9) // PER_HOUR
    blocks = owners // bands
    per_block = hours // blocks
    stride = per_block * SUB
    parts, _, width = turned.shape
    for part in range(parts):
        turned[part] = x_ref[part * width : (part + 1) * width, :].T
    per_part = width // bands
    depth = 2 * grid.shape[1]
    grid[:, lats * bands :] = jnp.zeros((grid.shape[0], grid.shape[1] - lats * bands), F32)
    for h in range(per_block):
        for lat in range(lats):
            for part in range(parts):
                rows = turned[part, pl.ds(lat * per_block + h, SUB, stride=stride), :]
                for t in range(per_part):
                    at = ((part * per_part + t) * per_block + h) * SUB
                    grid[at : at + SUB, lat * bands : (lat + 1) * bands] = rows[:, t * bands : (t + 1) * bands]
    series[...] = product(grid[...], later_ref[:depth, :])

    a = [[gain_ref[first_gain + 3 * i + j] for j in range(3)] for i in range(3)]
    gain = lambda h, which: gain_ref[first_gain + 9 + PER_HOUR * h + which]
    scaled = []
    mean = None
    for h in range(hours):
        seen = series[h * SUB : (h + 1) * SUB, :]
        if mean is None:
            error = seen
            mean = [gain(h, j) * error for j in range(3)]
        else:
            ahead = [a[i][0] * mean[0] + a[i][1] * mean[1] + a[i][2] * mean[2] for i in range(3)]
            error = seen - ahead[0]
            mean = [ahead[j] + gain(h, j) * error for j in range(3)]
        scaled.append(error * gain(h, 3))
    adjoint = None
    for h in reversed(range(hours)):
        drop = scaled[h]
        if adjoint is not None:
            drop = drop + (gain(h, 0) * adjoint[0] + gain(h, 1) * adjoint[1] + gain(h, 2) * adjoint[2])
        here = slice(h * SUB, (h + 1) * SUB)
        series[here, :] = series[here, :] - gain(h, 4) * drop
        if adjoint is None:
            adjoint = [-(a[0][j] * drop) for j in range(3)]
        else:
            less = adjoint[0] - drop
            adjoint = [a[0][j] * less + a[1][j] * adjoint[1] + a[2][j] * adjoint[2] for j in range(3)]

    grid[...] = product(series[...], later_ref[depth : 2 * depth, :])
    turned[...] = jnp.zeros_like(turned)
    for h in range(per_block):
        for lat in range(lats):
            for part in range(parts):
                rows = jnp.concatenate(
                    [
                        grid[(t * per_block + h) * SUB : (t * per_block + h + 1) * SUB, lat * bands : (lat + 1) * bands]
                        for t in range(part * per_part, (part + 1) * per_part)
                    ],
                    axis=1,
                )
                turned[part, pl.ds(lat * per_block + h, SUB, stride=stride), :] = rows
    for part in range(parts):
        out_ref[part * width : (part + 1) * width, :] = turned[part].T


def synthesise_kernel(bands, slots, x_ref, later_ref, turns_ref, out_ref, turned, flat):
    lats, hours, lon = out_ref.shape
    steps = lon // STEP_BACK
    rows = 2 * SUB
    turned[...] = x_ref[...].T

    def turn(m, which, b):
        at = (2 * m + which) * steps + b
        return turns_ref[at // SUB, at % SUB : at % SUB + 1, :]

    values = []
    tables = []
    depth = 2 * x_ref.shape[0]
    first = later_ref.shape[0] - slots * depth
    for m in range(slots):
        tables += facing(later_ref[first + m * depth : first + (m + 1) * depth, :])
        plain = turned[m * rows : (m + 1) * rows, :]
        cross = partners(plain, bands)
        turned_on = [
            plain * turn(m, 0, b) + cross * turn(m, 1, b) for b in range(steps)
        ]
        values.append(spread(jnp.concatenate(turned_on, axis=0)))
    total = jnp.dot(
        jnp.concatenate(values, axis=1), jnp.concatenate(tables, axis=0), preferred_element_type=F32
    )
    for b in range(steps):
        flat[:, b * STEP_BACK : (b + 1) * STEP_BACK] = total[b * rows : (b + 1) * rows, :STEP_BACK]
    for lat in range(lats):
        out_ref[lat] = flat[lat * hours : (lat + 1) * hours, :]


def params(mib):
    return pltpu.CompilerParams(vmem_limit_bytes=mib * MIB)


def in_hbm(value):
    return pltpu.with_memory_space_constraint(value, pltpu.HBM)


def per_device(tables, observed, noise_var, spectral_var, time_scale):
    lon_into, later, turns = tables
    hours_dev, lat_dev, lon_size = observed.shape
    hours = noise_var.shape[0]
    bands = lax.axis_size("space")
    slots, _, owners = lon_into.shape
    lat_pad = later.shape[-1]
    rows = 2 * SUB
    lanes = SUB * rows
    vmem = pl.BlockSpec(memory_space=pltpu.VMEM)
    smem = pl.BlockSpec(memory_space=pltpu.SMEM)
    hbm = pl.BlockSpec(memory_space=pltpu.HBM)

    by_lat = observed.transpose(1, 0, 2)
    sent, gains, later = pl.pallas_call(
        functools.partial(analyse_kernel, bands),
        out_shape=(
            jax.ShapeDtypeStruct((owners, lanes), F32),
            jax.ShapeDtypeStruct((turns.shape[0] + 9 + PER_HOUR * hours, SUB, lat_pad), F32),
            jax.ShapeDtypeStruct(later.shape, BF16),
        ),
        in_specs=[hbm] * 7,
        out_specs=(vmem,) * 3,
        scratch_shapes=[
            pltpu.VMEM(by_lat.shape, F32),
            pltpu.VMEM(lon_into.shape, F32),
            pltpu.VMEM((rows, lon_size), F32),
            pltpu.VMEM((lon_size // STEP * rows, LANES), F32),
            pltpu.VMEM((lanes, owners), F32),
            pltpu.SMEM(noise_var.shape, F32),
            pltpu.VMEM(spectral_var.shape, F32),
            pltpu.VMEM(spectral_var.shape, F32),
            pltpu.VMEM((SUB, lat_pad), F32),
            pltpu.VMEM((SUB, lat_pad), F32),
            pltpu.SemaphoreType.DMA((7,)),
        ],
        compiler_params=params(16),
        name="analyse",
    )(*(in_hbm(each) for each in (by_lat, lon_into, noise_var, spectral_var, time_scale, turns, later)))
    got = lax.all_to_all(sent, ("tm", "space"), split_axis=0, concat_axis=0, tiled=True)

    smooth = pl.pallas_call(
        functools.partial(smooth_kernel, lat_dev, bands, turns.shape[0]),
        out_shape=jax.ShapeDtypeStruct((owners, lanes), F32),
        in_specs=[vmem] * 3,
        out_specs=vmem,
        scratch_shapes=[
            pltpu.VMEM((owners // LANES, lanes, LANES), F32),
            pltpu.VMEM((hours * SUB, lat_pad), F32),
            pltpu.VMEM((hours * SUB, lat_pad), F32),
        ],
        compiler_params=params(16),
        name="smooth",
    )(got, gains, later)
    back = lax.all_to_all(smooth, ("tm", "space"), split_axis=0, concat_axis=0, tiled=True)

    field = pl.pallas_call(
        functools.partial(synthesise_kernel, bands, slots),
        out_shape=jax.ShapeDtypeStruct(by_lat.shape, F32),
        in_specs=[vmem] * 3,
        out_specs=vmem,
        scratch_shapes=[pltpu.VMEM((lanes, owners), F32), pltpu.VMEM((rows, lon_size), F32)],
        compiler_params=params(16),
        name="synthesise",
    )(back, later, gains)
    return field.transpose(1, 0, 2)


def solution(mesh):
    placed = (P("tm", "space", None), P(), P("space", None), P("space", None))
    blocks, bands = mesh.shape["tm"], mesh.shape["space"]

    def whole(observed, noise_var, spectral_var, time_scale):
        lon_size = observed.shape[2]
        lat_size = spectral_var.shape[1]
        tables = all_tables(observed.shape[2], spectral_var.shape[1], blocks, bands)
        tables = tuple(jnp.asarray(table) for table in tables)
        return jax.shard_map(
            functools.partial(per_device, tables),
            mesh=mesh,
            in_specs=placed,
            out_specs=P("tm", "space", None),
            check_vma=False,
        )(observed, noise_var, spectral_var, time_scale)

    return whole
```

```python
import functools
import math

import jax
import jax.numpy as jnp
import ml_dtypes
import numpy as np
from jax import lax
from jax.experimental import pallas as pl
from jax.experimental.pallas import tpu as pltpu
from jax.sharding import PartitionSpec as P

ROOT_FIVE = 2.23606797749979
NILPOTENT = ((1.0, 1.0, 0.0), (0.0, 1.0, 1.0), (-1.0, -3.0, -2.0))
NILPOTENT_SQUARED = ((1.0, 2.0, 1.0), (-1.0, -2.0, -1.0), (1.0, 2.0, 1.0))
STATIONARY = ((1.0, 0.0, -1.0 / 3.0), (0.0, 1.0 / 3.0, 0.0), (-1.0 / 3.0, 0.0, 1.0))
F32 = jnp.float32
BF16 = jnp.bfloat16
SUB = 8
LANES = 128
PER_HOUR = 5
STEP = 120
STEP_BACK = 240
MIB = 2**20


def halves(table):
    high = table.astype(ml_dtypes.bfloat16)
    low = (table - high.astype(np.float64)).astype(ml_dtypes.bfloat16)
    return np.concatenate([high, low], axis=-2)


def lon_basis(size):
    mode = np.arange(size)[:, None]
    longitude = np.arange(size)[None, :]
    half = size // 2
    sine = mode > half
    frequency = np.where(sine, mode - half, mode)
    radians = (frequency * longitude % size) * (2.0 * math.pi / size)
    weight = np.where((mode == 0) | (mode == half), math.sqrt(1.0 / size), math.sqrt(2.0 / size))
    return np.where(sine, np.sin(radians), np.cos(radians)) * weight


def lat_basis(size):
    wavenumber = np.arange(size)[:, None]
    latitude = np.arange(size)[None, :]
    radians = (wavenumber * (2 * latitude + 1) % (4 * size)) * (math.pi / (2.0 * size))
    weight = np.where(wavenumber == 0, math.sqrt(1.0 / size), math.sqrt(2.0 / size))
    return np.cos(radians) * weight


def lon_tables(size, step, hour_blocks, bands):
    per_band = size // bands
    slots = -(-per_band // hour_blocks)
    half = size // 2
    slot = np.arange(slots)[:, None, None]
    block = np.arange(hour_blocks)[None, :, None]
    band = np.arange(bands)[None, None, :]
    within = slots * block + slot + 0 * band
    used = within < per_band
    mode = np.where(used, per_band * band + within, 0)
    rows = (lon_basis(size)[mode] * used[..., None]).reshape(slots, hour_blocks * bands, size)
    sine = mode > half
    frequency = np.where(sine, mode - half, mode)
    ahead = np.arange(size // step)[:, None, None, None] * step
    radians = (frequency * ahead % size) * (2.0 * math.pi / size)
    straight = np.where(used, np.cos(radians), 0.0)
    crossed = np.where(used & (mode % half != 0), np.sin(radians), 0.0) * np.where(sine, 1.0, -1.0)
    crossed = np.roll(crossed, bands // 2, axis=-1)
    turns = np.stack([straight, crossed]).reshape(2, size // step, slots, hour_blocks * bands)
    head = np.zeros((slots, hour_blocks * bands, -(-step // LANES) * LANES))
    head[..., :step] = rows[..., :step]
    return head, turns.transpose(2, 0, 1, 3).astype(np.float32)


def all_tables(lon_size, lat_size, blocks, bands):
    head, turns = lon_tables(lon_size, STEP, blocks, bands)
    slots, owners, _ = head.shape
    into = np.concatenate([head[..., :STEP].transpose(0, 2, 1), turns.reshape(slots, -1, owners)], axis=1)
    head, turns = lon_tables(lon_size, STEP_BACK, blocks, bands)
    back = halves(head).reshape(-1, head.shape[-1])
    by_lat = lat_basis(lat_size).reshape(lat_size, bands, lat_size // bands)
    by_lat = by_lat.transpose(0, 2, 1).reshape(lat_size, lat_size)
    pad = -lat_size % (2 * LANES)
    by_lat = np.pad(by_lat, ((0, pad), (0, pad)))
    later = np.concatenate([halves(by_lat.T), halves(by_lat), back], axis=0)
    return into.astype(np.float32), later, turns.reshape(-1, SUB, owners)


def split(value):
    high = value.astype(BF16)
    return high, (value - high.astype(F32)).astype(BF16)


def spread(value):
    high, low = split(value)
    return jnp.concatenate([high, low, high], axis=1)


def folded_product(high, low, table_high, table_low):
    rows = high.shape[0]
    both = jnp.dot(jnp.concatenate([high, low], axis=0), table_high, preferred_element_type=F32)
    return both[:rows] + both[rows:] + jnp.dot(high, table_low, preferred_element_type=F32)


def facing(table):
    depth = table.shape[0] // 2
    return [table[:depth], table[:depth], table[depth:]]


def product(value, table):
    return jnp.dot(spread(value), jnp.concatenate(facing(table), axis=0), preferred_element_type=F32)


def partners(value, bands):
    half = bands // 2
    width = value.shape[1]
    upper = lax.broadcasted_iota(jnp.int32, value.shape, 1) % bands >= half
    return jnp.where(upper, pltpu.roll(value, half, 1), pltpu.roll(value, width - half, 1))


def fill_gains(slots, first_gain, out_ref, noise_ref, var_ref, scale_ref, var, scale):
    last = var_ref.shape[0] - 1
    var[...] = jnp.ones_like(var)
    scale[...] = jnp.ones_like(scale)
    for m in range(slots):
        row = jnp.minimum(slots * lax.axis_index("tm") + m, last)
        var[m : m + 1, : var_ref.shape[1]] = var_ref[pl.ds(row, 1), :]
        scale[m : m + 1, : var_ref.shape[1]] = scale_ref[pl.ds(row, 1), :]
    variance = var[...]
    rate = ROOT_FIVE / scale[...]
    damping = jnp.exp(-rate)
    a = [
        [
            damping
            * (
                (1.0 if i == j else 0.0)
                + rate * NILPOTENT[i][j]
                + 0.5 * rate * rate * NILPOTENT_SQUARED[i][j]
            )
            for j in range(3)
        ]
        for i in range(3)
    ]
    for i in range(3):
        for j in range(3):
            out_ref[first_gain + 3 * i + j] = a[i][j]

    def carried(cov):
        ap = [[a[i][0] * cov[0][j] + a[i][1] * cov[1][j] + a[i][2] * cov[2][j] for j in range(3)] for i in range(3)]
        upper = {
            (i, j): ap[i][0] * a[j][0] + ap[i][1] * a[j][1] + ap[i][2] * a[j][2]
            for i in range(3)
            for j in range(i, 3)
        }
        return [[upper[min(i, j), max(i, j)] for j in range(3)] for i in range(3)]

    cov = [[variance * STATIONARY[i][j] for j in range(3)] for i in range(3)]
    start = carried(cov)
    noise_cov = [[cov[i][j] - start[i][j] for j in range(3)] for i in range(3)]
    for h in range((out_ref.shape[0] - first_gain - 9) // PER_HOUR):
        at = first_gain + 9 + PER_HOUR * h
        noise = noise_ref[h]
        moved = carried(cov)
        pm = {(i, j): moved[i][j] + noise_cov[i][j] for i in range(3) for j in range(i, 3)}
        inverse = 1.0 / (pm[0, 0] + noise)
        k = [pm[0, j] * inverse for j in range(3)]
        for j in range(3):
            out_ref[at + j] = k[j]
        out_ref[at + 3] = inverse
        out_ref[at + 4] = jnp.full(inverse.shape, noise, F32)
        first = [noise * k[j] for j in range(3)]
        c11 = pm[1, 1] - k[1] * pm[0, 1]
        c12 = pm[1, 2] - k[1] * pm[0, 2]
        c22 = pm[2, 2] - k[2] * pm[0, 2]
        cov = [[first[0], first[1], first[2]], [first[1], c11, c12], [first[2], c12, c22]]


def analyse_kernel(
    bands, x_hbm, table_hbm, noise_hbm, var_hbm, scale_hbm, turns_hbm, later_hbm, out_ref, gain_ref,
    later_ref, x, table, flat, blocks, slots_of, noise_ref, var_ref, scale_ref, var, scale, sems,
):
    lats, hours, lon = x.shape
    slots = table.shape[0]
    steps = lon // STEP
    rows = 2 * SUB
    pairs = (
        (var_hbm, var_ref),
        (scale_hbm, scale_ref),
        (noise_hbm, noise_ref),
        (x_hbm, x),
        (table_hbm, table),
        (turns_hbm, gain_ref.at[: turns_hbm.shape[0]]),
        (later_hbm, later_ref),
    )
    fetch = [pltpu.make_async_copy(here, there, sems.at[i]) for i, (here, there) in enumerate(pairs)]
    for copy in fetch:
        copy.start()
    flat[...] = jnp.zeros_like(flat)
    blocks[...] = jnp.zeros_like(blocks)
    slots_of[...] = jnp.zeros_like(slots_of)
    for copy in fetch[:3]:
        copy.wait()
    fill_gains(slots, turns_hbm.shape[0], gain_ref, noise_ref, var_ref, scale_ref, var, scale)
    fetch[3].wait()
    for lat in range(lats):
        flat[lat * hours : (lat + 1) * hours, :] = x[lat]
    for b in range(steps):
        blocks[b * rows : (b + 1) * rows, :STEP] = flat[:, b * STEP : (b + 1) * STEP]
    value = spread(blocks[...])
    fetch[4].wait()
    for m in range(slots):
        high, low = split(table[m, :LANES, :])
        part = jnp.dot(value, jnp.concatenate([high, high, low], axis=0), preferred_element_type=F32)
        straight = crossed = None
        for b in range(steps):
            here = part[b * rows : (b + 1) * rows]
            plain = here * table[m, STEP + b : STEP + b + 1, :]
            cross = here * table[m, STEP + steps + b : STEP + steps + b + 1, :]
            straight = plain if straight is None else straight + plain
            crossed = cross if crossed is None else crossed + cross
        slots_of[m * rows : (m + 1) * rows, :] = straight + partners(crossed, bands)
    out_ref[...] = slots_of[...].T
    for copy in fetch[5:]:
        copy.wait()


def smooth_kernel(lats, bands, first_gain, x_ref, gain_ref, later_ref, out_ref, turned, grid, series):
    owners, lanes = x_ref.shape
    hours = (gain_ref.shape[0] - first_gain - 9) // PER_HOUR
    blocks = owners // bands
    per_block = hours // blocks
    stride = per_block * SUB
    parts, _, width = turned.shape
    for part in range(parts):
        turned[part] = x_ref[part * width : (part + 1) * width, :].T
    per_part = width // bands
    depth = 2 * grid.shape[1]
    grid[:, lats * bands :] = jnp.zeros((grid.shape[0], grid.shape[1] - lats * bands), F32)
    for h in range(per_block):
        for lat in range(lats):
            for part in range(parts):
                rows = turned[part, pl.ds(lat * per_block + h, SUB, stride=stride), :]
                for t in range(per_part):
                    at = ((part * per_part + t) * per_block + h) * SUB
                    grid[at : at + SUB, lat * bands : (lat + 1) * bands] = rows[:, t * bands : (t + 1) * bands]
    series[...] = product(grid[...], later_ref[:depth, :])

    a = [[gain_ref[first_gain + 3 * i + j] for j in range(3)] for i in range(3)]
    gain = lambda h, which: gain_ref[first_gain + 9 + PER_HOUR * h + which]
    scaled = []
    mean = None
    for h in range(hours):
        seen = series[h * SUB : (h + 1) * SUB, :]
        if mean is None:
            error = seen
            mean = [gain(h, j) * error for j in range(3)]
        else:
            ahead = [a[i][0] * mean[0] + a[i][1] * mean[1] + a[i][2] * mean[2] for i in range(3)]
            error = seen - ahead[0]
            mean = [ahead[j] + gain(h, j) * error for j in range(3)]
        scaled.append(error * gain(h, 3))
    adjoint = None
    for h in reversed(range(hours)):
        drop = scaled[h]
        if adjoint is not None:
            drop = drop + (gain(h, 0) * adjoint[0] + gain(h, 1) * adjoint[1] + gain(h, 2) * adjoint[2])
        here = slice(h * SUB, (h + 1) * SUB)
        series[here, :] = series[here, :] - gain(h, 4) * drop
        if adjoint is None:
            adjoint = [-(a[0][j] * drop) for j in range(3)]
        else:
            less = adjoint[0] - drop
            adjoint = [a[0][j] * less + a[1][j] * adjoint[1] + a[2][j] * adjoint[2] for j in range(3)]

    grid[...] = product(series[...], later_ref[depth : 2 * depth, :])
    turned[...] = jnp.zeros_like(turned)
    for h in range(per_block):
        for lat in range(lats):
            for part in range(parts):
                rows = jnp.concatenate(
                    [
                        grid[(t * per_block + h) * SUB : (t * per_block + h + 1) * SUB, lat * bands : (lat + 1) * bands]
                        for t in range(part * per_part, (part + 1) * per_part)
                    ],
                    axis=1,
                )
                turned[part, pl.ds(lat * per_block + h, SUB, stride=stride), :] = rows
    for part in range(parts):
        out_ref[part * width : (part + 1) * width, :] = turned[part].T


def synthesise_kernel(bands, slots, x_ref, later_ref, turns_ref, out_ref, turned, flat):
    lats, hours, lon = out_ref.shape
    steps = lon // STEP_BACK
    rows = 2 * SUB
    turned[...] = x_ref[...].T

    def turn(m, which, b):
        at = (2 * m + which) * steps + b
        return turns_ref[at // SUB, at % SUB : at % SUB + 1, :]

    values = []
    highs = []
    lows = []
    depth = 2 * x_ref.shape[0]
    first = later_ref.shape[0] - slots * depth
    for m in range(slots):
        at = first + m * depth
        highs.append(later_ref[at : at + depth // 2, :])
        lows.append(later_ref[at + depth // 2 : at + depth, :])
        plain = turned[m * rows : (m + 1) * rows, :]
        cross = partners(plain, bands)
        turned_on = [
            plain * turn(m, 0, b) + cross * turn(m, 1, b) for b in range(steps)
        ]
        values.append(split(jnp.concatenate(turned_on, axis=0)))
    high = jnp.concatenate([each[0] for each in values], axis=1)
    low = jnp.concatenate([each[1] for each in values], axis=1)
    total = folded_product(high, low, jnp.concatenate(highs, axis=0), jnp.concatenate(lows, axis=0))
    for b in range(steps):
        flat[:, b * STEP_BACK : (b + 1) * STEP_BACK] = total[b * rows : (b + 1) * rows, :STEP_BACK]
    for lat in range(lats):
        out_ref[lat] = flat[lat * hours : (lat + 1) * hours, :]


def params(mib):
    return pltpu.CompilerParams(vmem_limit_bytes=mib * MIB)


def in_hbm(value):
    return pltpu.with_memory_space_constraint(value, pltpu.HBM)


def per_device(tables, observed, noise_var, spectral_var, time_scale):
    lon_into, later, turns = tables
    hours_dev, lat_dev, lon_size = observed.shape
    hours = noise_var.shape[0]
    bands = lax.axis_size("space")
    slots, _, owners = lon_into.shape
    lat_pad = later.shape[-1]
    rows = 2 * SUB
    lanes = SUB * rows
    vmem = pl.BlockSpec(memory_space=pltpu.VMEM)
    smem = pl.BlockSpec(memory_space=pltpu.SMEM)
    hbm = pl.BlockSpec(memory_space=pltpu.HBM)

    by_lat = observed.transpose(1, 0, 2)
    sent, gains, later = pl.pallas_call(
        functools.partial(analyse_kernel, bands),
        out_shape=(
            jax.ShapeDtypeStruct((owners, lanes), F32),
            jax.ShapeDtypeStruct((turns.shape[0] + 9 + PER_HOUR * hours, SUB, lat_pad), F32),
            jax.ShapeDtypeStruct(later.shape, BF16),
        ),
        in_specs=[hbm] * 7,
        out_specs=(vmem,) * 3,
        scratch_shapes=[
            pltpu.VMEM(by_lat.shape, F32),
            pltpu.VMEM(lon_into.shape, F32),
            pltpu.VMEM((rows, lon_size), F32),
            pltpu.VMEM((lon_size // STEP * rows, LANES), F32),
            pltpu.VMEM((lanes, owners), F32),
            pltpu.SMEM(noise_var.shape, F32),
            pltpu.VMEM(spectral_var.shape, F32),
            pltpu.VMEM(spectral_var.shape, F32),
            pltpu.VMEM((SUB, lat_pad), F32),
            pltpu.VMEM((SUB, lat_pad), F32),
            pltpu.SemaphoreType.DMA((7,)),
        ],
        compiler_params=params(16),
        name="analyse",
    )(*(in_hbm(each) for each in (by_lat, lon_into, noise_var, spectral_var, time_scale, turns, later)))
    got = lax.all_to_all(sent, ("tm", "space"), split_axis=0, concat_axis=0, tiled=True)

    smooth = pl.pallas_call(
        functools.partial(smooth_kernel, lat_dev, bands, turns.shape[0]),
        out_shape=jax.ShapeDtypeStruct((owners, lanes), F32),
        in_specs=[vmem] * 3,
        out_specs=vmem,
        scratch_shapes=[
            pltpu.VMEM((owners // LANES, lanes, LANES), F32),
            pltpu.VMEM((hours * SUB, lat_pad), F32),
            pltpu.VMEM((hours * SUB, lat_pad), F32),
        ],
        compiler_params=params(16),
        name="smooth",
    )(got, gains, later)
    back = lax.all_to_all(smooth, ("tm", "space"), split_axis=0, concat_axis=0, tiled=True)

    field = pl.pallas_call(
        functools.partial(synthesise_kernel, bands, slots),
        out_shape=jax.ShapeDtypeStruct(by_lat.shape, F32),
        in_specs=[vmem] * 3,
        out_specs=vmem,
        scratch_shapes=[pltpu.VMEM((lanes, owners), F32), pltpu.VMEM((rows, lon_size), F32)],
        compiler_params=params(16),
        name="synthesise",
    )(back, later, gains)
    return field.transpose(1, 0, 2)


def solution(mesh):
    placed = (P("tm", "space", None), P(), P("space", None), P("space", None))
    blocks, bands = mesh.shape["tm"], mesh.shape["space"]

    def whole(observed, noise_var, spectral_var, time_scale):
        lon_size = observed.shape[2]
        lat_size = spectral_var.shape[1]
        tables = all_tables(observed.shape[2], spectral_var.shape[1], blocks, bands)
        tables = tuple(jnp.asarray(table) for table in tables)
        return jax.shard_map(
            functools.partial(per_device, tables),
            mesh=mesh,
            in_specs=placed,
            out_specs=P("tm", "space", None),
            check_vma=False,
        )(observed, noise_var, spectral_var, time_scale)

    return whole
```

```python
import functools
import math

import jax
import jax.numpy as jnp
import ml_dtypes
import numpy as np
from jax import lax
from jax.experimental import pallas as pl
from jax.experimental.pallas import tpu as pltpu
from jax.sharding import PartitionSpec as P

ROOT_FIVE = 2.23606797749979
STATIONARY = ((1.0, 1.0, 2.0 / 3.0), (1.0, 4.0 / 3.0, 4.0 / 3.0), (2.0 / 3.0, 4.0 / 3.0, 8.0 / 3.0))
MOVES = 3
F32 = jnp.float32
BF16 = jnp.bfloat16
SUB = 8
LANES = 128
PER_HOUR = 5
STEP = 120
STEP_BACK = 240
MIB = 2**20


def halves(table):
    high = table.astype(ml_dtypes.bfloat16)
    low = (table - high.astype(np.float64)).astype(ml_dtypes.bfloat16)
    return np.concatenate([high, low], axis=-2)


def lon_basis(size):
    mode = np.arange(size)[:, None]
    longitude = np.arange(size)[None, :]
    half = size // 2
    sine = mode > half
    frequency = np.where(sine, mode - half, mode)
    radians = (frequency * longitude % size) * (2.0 * math.pi / size)
    weight = np.where((mode == 0) | (mode == half), math.sqrt(1.0 / size), math.sqrt(2.0 / size))
    return np.where(sine, np.sin(radians), np.cos(radians)) * weight


def lat_basis(size):
    wavenumber = np.arange(size)[:, None]
    latitude = np.arange(size)[None, :]
    radians = (wavenumber * (2 * latitude + 1) % (4 * size)) * (math.pi / (2.0 * size))
    weight = np.where(wavenumber == 0, math.sqrt(1.0 / size), math.sqrt(2.0 / size))
    return np.cos(radians) * weight


def lon_tables(size, step, hour_blocks, bands):
    per_band = size // bands
    slots = -(-per_band // hour_blocks)
    half = size // 2
    slot = np.arange(slots)[:, None, None]
    block = np.arange(hour_blocks)[None, :, None]
    band = np.arange(bands)[None, None, :]
    within = slots * block + slot + 0 * band
    used = within < per_band
    mode = np.where(used, per_band * band + within, 0)
    rows = (lon_basis(size)[mode] * used[..., None]).reshape(slots, hour_blocks * bands, size)
    sine = mode > half
    frequency = np.where(sine, mode - half, mode)
    ahead = np.arange(size // step)[:, None, None, None] * step
    radians = (frequency * ahead % size) * (2.0 * math.pi / size)
    straight = np.where(used, np.cos(radians), 0.0)
    crossed = np.where(used & (mode % half != 0), np.sin(radians), 0.0) * np.where(sine, 1.0, -1.0)
    crossed = np.roll(crossed, bands // 2, axis=-1)
    turns = np.stack([straight, crossed]).reshape(2, size // step, slots, hour_blocks * bands)
    head = np.zeros((slots, hour_blocks * bands, -(-step // LANES) * LANES))
    head[..., :step] = rows[..., :step]
    return head, turns.transpose(2, 0, 1, 3).astype(np.float32)


def all_tables(lon_size, lat_size, blocks, bands):
    head, turns = lon_tables(lon_size, STEP, blocks, bands)
    slots, owners, _ = head.shape
    into = np.concatenate([head[..., :STEP].transpose(0, 2, 1), turns.reshape(slots, -1, owners)], axis=1)
    head, turns = lon_tables(lon_size, STEP_BACK, blocks, bands)
    back = halves(head).reshape(-1, head.shape[-1])
    by_lat = lat_basis(lat_size).reshape(lat_size, bands, lat_size // bands)
    by_lat = by_lat.transpose(0, 2, 1).reshape(lat_size, lat_size)
    pad = -lat_size % (2 * LANES)
    by_lat = np.pad(by_lat, ((0, pad), (0, pad)))
    later = np.concatenate([halves(by_lat.T), halves(by_lat), back], axis=0)
    return into.astype(np.float32), later, turns.reshape(-1, SUB, owners)


def split(value):
    high = value.astype(BF16)
    return high, (value - high.astype(F32)).astype(BF16)


def spread(value):
    high, low = split(value)
    return jnp.concatenate([high, low, high], axis=1)


def folded_product(high, low, table_high, table_low):
    rows = high.shape[0]
    both = jnp.dot(jnp.concatenate([high, low], axis=0), table_high, preferred_element_type=F32)
    return both[:rows] + both[rows:] + jnp.dot(high, table_low, preferred_element_type=F32)


def facing(table):
    depth = table.shape[0] // 2
    return [table[:depth], table[:depth], table[depth:]]


def product(value, table):
    return jnp.dot(spread(value), jnp.concatenate(facing(table), axis=0), preferred_element_type=F32)


def partners(value, bands):
    half = bands // 2
    width = value.shape[1]
    upper = lax.broadcasted_iota(jnp.int32, value.shape, 1) % bands >= half
    return jnp.where(upper, pltpu.roll(value, half, 1), pltpu.roll(value, width - half, 1))


def fill_gains(slots, first_gain, out_ref, noise_ref, var_ref, scale_ref, var, scale):
    last = var_ref.shape[0] - 1
    var[...] = jnp.ones_like(var)
    scale[...] = jnp.ones_like(scale)
    for m in range(slots):
        row = jnp.minimum(slots * lax.axis_index("tm") + m, last)
        var[m : m + 1, : var_ref.shape[1]] = var_ref[pl.ds(row, 1), :]
        scale[m : m + 1, : var_ref.shape[1]] = scale_ref[pl.ds(row, 1), :]
    variance = var[...]
    rate = ROOT_FIVE / scale[...]
    damping = jnp.exp(-rate)
    half_square = 0.5 * rate * rate
    for i, move in enumerate((damping, damping * rate, damping * half_square)):
        out_ref[first_gain + i] = move
    twice = damping * damping

    def carried(p):
        top = [p[0, j] + rate * p[1, j] + half_square * p[2, j] for j in range(3)]
        middle = [p[1, j] + rate * p[2, j] for j in range(3)]
        full = {
            (0, 0): top[0] + rate * top[1] + half_square * top[2],
            (0, 1): top[1] + rate * top[2],
            (0, 2): top[2],
            (1, 1): middle[1] + rate * middle[2],
            (1, 2): middle[2],
            (2, 2): p[2, 2],
        }
        return {at: twice * each for at, each in full.items()}

    def symmetric(upper):
        return {(i, j): upper[min(i, j), max(i, j)] for i in range(3) for j in range(3)}

    start = {(i, j): variance * STATIONARY[i][j] for i in range(3) for j in range(i, 3)}
    moved = carried(symmetric(start))
    noise_cov = {at: start[at] - moved[at] for at in start}
    pm = start
    for h in range((out_ref.shape[0] - first_gain - MOVES) // PER_HOUR):
        at = first_gain + MOVES + PER_HOUR * h
        noise = noise_ref[h]
        if h > 0:
            moved = carried(symmetric(cov))
            pm = {entry: moved[entry] + noise_cov[entry] for entry in moved}
        inverse = 1.0 / (pm[0, 0] + noise)
        k = [pm[0, j] * inverse for j in range(3)]
        for j in range(3):
            out_ref[at + j] = k[j]
        out_ref[at + 3] = inverse
        out_ref[at + 4] = jnp.full(inverse.shape, noise, F32)
        cov = {(0, j): noise * k[j] for j in range(3)}
        for i in (1, 2):
            for j in range(i, 3):
                cov[i, j] = pm[i, j] - k[i] * pm[0, j]


def analyse_kernel(
    bands, x_hbm, table_hbm, noise_hbm, var_hbm, scale_hbm, turns_hbm, later_hbm, out_ref, gain_ref,
    later_ref, x, table, flat, blocks, slots_of, noise_ref, var_ref, scale_ref, var, scale, sems,
):
    lats, hours, lon = x.shape
    slots = table.shape[0]
    steps = lon // STEP
    rows = 2 * SUB
    pairs = (
        (var_hbm, var_ref),
        (scale_hbm, scale_ref),
        (noise_hbm, noise_ref),
        (x_hbm, x),
        (table_hbm, table),
        (turns_hbm, gain_ref.at[: turns_hbm.shape[0]]),
        (later_hbm, later_ref),
    )
    fetch = [pltpu.make_async_copy(here, there, sems.at[i]) for i, (here, there) in enumerate(pairs)]
    for copy in fetch:
        copy.start()
    flat[...] = jnp.zeros_like(flat)
    blocks[...] = jnp.zeros_like(blocks)
    slots_of[...] = jnp.zeros_like(slots_of)
    for copy in fetch[:3]:
        copy.wait()
    fill_gains(slots, turns_hbm.shape[0], gain_ref, noise_ref, var_ref, scale_ref, var, scale)
    fetch[3].wait()
    for lat in range(lats):
        flat[lat * hours : (lat + 1) * hours, :] = x[lat]
    for b in range(steps):
        blocks[b * rows : (b + 1) * rows, :STEP] = flat[:, b * STEP : (b + 1) * STEP]
    value = spread(blocks[...])
    fetch[4].wait()
    for m in range(slots):
        high, low = split(table[m, :LANES, :])
        part = jnp.dot(value, jnp.concatenate([high, high, low], axis=0), preferred_element_type=F32)
        straight = crossed = None
        for b in range(steps):
            here = part[b * rows : (b + 1) * rows]
            plain = here * table[m, STEP + b : STEP + b + 1, :]
            cross = here * table[m, STEP + steps + b : STEP + steps + b + 1, :]
            straight = plain if straight is None else straight + plain
            crossed = cross if crossed is None else crossed + cross
        slots_of[m * rows : (m + 1) * rows, :] = straight + partners(crossed, bands)
    out_ref[...] = slots_of[...].T
    for copy in fetch[5:]:
        copy.wait()


def smooth_kernel(lats, bands, first_gain, x_ref, gain_ref, later_ref, out_ref, turned, grid, series):
    owners, lanes = x_ref.shape
    hours = (gain_ref.shape[0] - first_gain - MOVES) // PER_HOUR
    blocks = owners // bands
    per_block = hours // blocks
    stride = per_block * SUB
    parts, _, width = turned.shape
    for part in range(parts):
        turned[part] = x_ref[part * width : (part + 1) * width, :].T
    per_part = width // bands
    depth = 2 * grid.shape[1]
    grid[:, lats * bands :] = jnp.zeros((grid.shape[0], grid.shape[1] - lats * bands), F32)
    for h in range(per_block):
        for lat in range(lats):
            for part in range(parts):
                rows = turned[part, pl.ds(lat * per_block + h, SUB, stride=stride), :]
                for t in range(per_part):
                    at = ((part * per_part + t) * per_block + h) * SUB
                    grid[at : at + SUB, lat * bands : (lat + 1) * bands] = rows[:, t * bands : (t + 1) * bands]
    series[...] = product(grid[...], later_ref[:depth, :])

    stay, once, both = (gain_ref[first_gain + i] for i in range(MOVES))
    gain = lambda h, which: gain_ref[first_gain + MOVES + PER_HOUR * h + which]
    scaled = []
    mean = None
    for h in range(hours):
        seen = series[h * SUB : (h + 1) * SUB, :]
        if mean is None:
            error = seen
            mean = [gain(h, j) * error for j in range(3)]
        else:
            ahead = [
                stay * mean[0] + once * mean[1] + both * mean[2],
                stay * mean[1] + once * mean[2],
                stay * mean[2],
            ]
            error = seen - ahead[0]
            mean = [ahead[j] + gain(h, j) * error for j in range(3)]
        scaled.append(error * gain(h, 3))
    adjoint = None
    for h in reversed(range(hours)):
        drop = scaled[h]
        if adjoint is not None:
            drop = drop + (gain(h, 0) * adjoint[0] + gain(h, 1) * adjoint[1] + gain(h, 2) * adjoint[2])
        here = slice(h * SUB, (h + 1) * SUB)
        series[here, :] = series[here, :] - gain(h, 4) * drop
        if adjoint is None:
            adjoint = [-(move * drop) for move in (stay, once, both)]
        else:
            less = adjoint[0] - drop
            adjoint = [
                stay * less,
                once * less + stay * adjoint[1],
                both * less + once * adjoint[1] + stay * adjoint[2],
            ]

    grid[...] = product(series[...], later_ref[depth : 2 * depth, :])
    turned[...] = jnp.zeros_like(turned)
    for h in range(per_block):
        for lat in range(lats):
            for part in range(parts):
                rows = jnp.concatenate(
                    [
                        grid[(t * per_block + h) * SUB : (t * per_block + h + 1) * SUB, lat * bands : (lat + 1) * bands]
                        for t in range(part * per_part, (part + 1) * per_part)
                    ],
                    axis=1,
                )
                turned[part, pl.ds(lat * per_block + h, SUB, stride=stride), :] = rows
    for part in range(parts):
        out_ref[part * width : (part + 1) * width, :] = turned[part].T


def synthesise_kernel(bands, slots, x_ref, later_ref, turns_ref, out_ref, turned, flat):
    lats, hours, lon = out_ref.shape
    steps = lon // STEP_BACK
    rows = 2 * SUB
    turned[...] = x_ref[...].T

    def turn(m, which, b):
        at = (2 * m + which) * steps + b
        return turns_ref[at // SUB, at % SUB : at % SUB + 1, :]

    values = []
    highs = []
    lows = []
    depth = 2 * x_ref.shape[0]
    first = later_ref.shape[0] - slots * depth
    for m in range(slots):
        at = first + m * depth
        highs.append(later_ref[at : at + depth // 2, :])
        lows.append(later_ref[at + depth // 2 : at + depth, :])
        plain = turned[m * rows : (m + 1) * rows, :]
        cross = partners(plain, bands)
        turned_on = [
            plain * turn(m, 0, b) + cross * turn(m, 1, b) for b in range(steps)
        ]
        values.append(split(jnp.concatenate(turned_on, axis=0)))
    high = jnp.concatenate([each[0] for each in values], axis=1)
    low = jnp.concatenate([each[1] for each in values], axis=1)
    total = folded_product(high, low, jnp.concatenate(highs, axis=0), jnp.concatenate(lows, axis=0))
    for b in range(steps):
        flat[:, b * STEP_BACK : (b + 1) * STEP_BACK] = total[b * rows : (b + 1) * rows, :STEP_BACK]
    for lat in range(lats):
        out_ref[lat] = flat[lat * hours : (lat + 1) * hours, :]


def params(mib):
    return pltpu.CompilerParams(vmem_limit_bytes=mib * MIB)


def in_hbm(value):
    return pltpu.with_memory_space_constraint(value, pltpu.HBM)


def per_device(tables, observed, noise_var, spectral_var, time_scale):
    lon_into, later, turns = tables
    hours_dev, lat_dev, lon_size = observed.shape
    hours = noise_var.shape[0]
    bands = lax.axis_size("space")
    slots, _, owners = lon_into.shape
    lat_pad = later.shape[-1]
    rows = 2 * SUB
    lanes = SUB * rows
    vmem = pl.BlockSpec(memory_space=pltpu.VMEM)
    smem = pl.BlockSpec(memory_space=pltpu.SMEM)
    hbm = pl.BlockSpec(memory_space=pltpu.HBM)

    by_lat = observed.transpose(1, 0, 2)
    sent, gains, later = pl.pallas_call(
        functools.partial(analyse_kernel, bands),
        out_shape=(
            jax.ShapeDtypeStruct((owners, lanes), F32),
            jax.ShapeDtypeStruct((turns.shape[0] + MOVES + PER_HOUR * hours, SUB, lat_pad), F32),
            jax.ShapeDtypeStruct(later.shape, BF16),
        ),
        in_specs=[hbm] * 7,
        out_specs=(vmem,) * 3,
        scratch_shapes=[
            pltpu.VMEM(by_lat.shape, F32),
            pltpu.VMEM(lon_into.shape, F32),
            pltpu.VMEM((rows, lon_size), F32),
            pltpu.VMEM((lon_size // STEP * rows, LANES), F32),
            pltpu.VMEM((lanes, owners), F32),
            pltpu.SMEM(noise_var.shape, F32),
            pltpu.VMEM(spectral_var.shape, F32),
            pltpu.VMEM(spectral_var.shape, F32),
            pltpu.VMEM((SUB, lat_pad), F32),
            pltpu.VMEM((SUB, lat_pad), F32),
            pltpu.SemaphoreType.DMA((7,)),
        ],
        compiler_params=params(16),
        name="analyse",
    )(*(in_hbm(each) for each in (by_lat, lon_into, noise_var, spectral_var, time_scale, turns, later)))
    got = lax.all_to_all(sent, ("tm", "space"), split_axis=0, concat_axis=0, tiled=True)

    smooth = pl.pallas_call(
        functools.partial(smooth_kernel, lat_dev, bands, turns.shape[0]),
        out_shape=jax.ShapeDtypeStruct((owners, lanes), F32),
        in_specs=[vmem] * 3,
        out_specs=vmem,
        scratch_shapes=[
            pltpu.VMEM((owners // LANES, lanes, LANES), F32),
            pltpu.VMEM((hours * SUB, lat_pad), F32),
            pltpu.VMEM((hours * SUB, lat_pad), F32),
        ],
        compiler_params=params(16),
        name="smooth",
    )(got, gains, later)
    back = lax.all_to_all(smooth, ("tm", "space"), split_axis=0, concat_axis=0, tiled=True)

    field = pl.pallas_call(
        functools.partial(synthesise_kernel, bands, slots),
        out_shape=jax.ShapeDtypeStruct(by_lat.shape, F32),
        in_specs=[vmem] * 3,
        out_specs=vmem,
        scratch_shapes=[pltpu.VMEM((lanes, owners), F32), pltpu.VMEM((rows, lon_size), F32)],
        compiler_params=params(16),
        name="synthesise",
    )(back, later, gains)
    return field.transpose(1, 0, 2)


def solution(mesh):
    placed = (P("tm", "space", None), P(), P("space", None), P("space", None))
    blocks, bands = mesh.shape["tm"], mesh.shape["space"]

    def whole(observed, noise_var, spectral_var, time_scale):
        lon_size = observed.shape[2]
        lat_size = spectral_var.shape[1]
        tables = all_tables(observed.shape[2], spectral_var.shape[1], blocks, bands)
        tables = tuple(jnp.asarray(table) for table in tables)
        return jax.shard_map(
            functools.partial(per_device, tables),
            mesh=mesh,
            in_specs=placed,
            out_specs=P("tm", "space", None),
            check_vma=False,
        )(observed, noise_var, spectral_var, time_scale)

    return whole
```

```python
import functools
import math

import jax
import jax.numpy as jnp
import ml_dtypes
import numpy as np
from jax import lax
from jax.experimental import pallas as pl
from jax.experimental.pallas import tpu as pltpu
from jax.sharding import PartitionSpec as P

ROOT_FIVE = 2.23606797749979
STATIONARY = ((1.0, 1.0, 2.0 / 3.0), (1.0, 4.0 / 3.0, 4.0 / 3.0), (2.0 / 3.0, 4.0 / 3.0, 8.0 / 3.0))
MOVES = 3
F32 = jnp.float32
BF16 = jnp.bfloat16
SUB = 8
LANES = 128
PER_HOUR = 5
STEP = 120
STEP_BACK = 240
MIB = 2**20


def halves(table):
    high = table.astype(ml_dtypes.bfloat16)
    low = (table - high.astype(np.float64)).astype(ml_dtypes.bfloat16)
    return np.concatenate([high, low], axis=-2)


def lon_basis(size):
    mode = np.arange(size)[:, None]
    longitude = np.arange(size)[None, :]
    half = size // 2
    sine = mode > half
    frequency = np.where(sine, mode - half, mode)
    radians = (frequency * longitude % size) * (2.0 * math.pi / size)
    weight = np.where((mode == 0) | (mode == half), math.sqrt(1.0 / size), math.sqrt(2.0 / size))
    return np.where(sine, np.sin(radians), np.cos(radians)) * weight


def lat_basis(size):
    wavenumber = np.arange(size)[:, None]
    latitude = np.arange(size)[None, :]
    radians = (wavenumber * (2 * latitude + 1) % (4 * size)) * (math.pi / (2.0 * size))
    weight = np.where(wavenumber == 0, math.sqrt(1.0 / size), math.sqrt(2.0 / size))
    return np.cos(radians) * weight


def lon_tables(size, step, hour_blocks, bands):
    per_band = size // bands
    slots = -(-per_band // hour_blocks)
    half = size // 2
    slot = np.arange(slots)[:, None, None]
    block = np.arange(hour_blocks)[None, :, None]
    band = np.arange(bands)[None, None, :]
    within = slots * block + slot + 0 * band
    used = within < per_band
    mode = np.where(used, per_band * band + within, 0)
    rows = (lon_basis(size)[mode] * used[..., None]).reshape(slots, hour_blocks * bands, size)
    sine = mode > half
    frequency = np.where(sine, mode - half, mode)
    ahead = np.arange(size // step)[:, None, None, None] * step
    radians = (frequency * ahead % size) * (2.0 * math.pi / size)
    straight = np.where(used, np.cos(radians), 0.0)
    crossed = np.where(used & (mode % half != 0), np.sin(radians), 0.0) * np.where(sine, 1.0, -1.0)
    crossed = np.roll(crossed, bands // 2, axis=-1)
    turns = np.stack([straight, crossed]).reshape(2, size // step, slots, hour_blocks * bands)
    head = np.zeros((slots, hour_blocks * bands, -(-step // LANES) * LANES))
    head[..., :step] = rows[..., :step]
    return head, turns.transpose(2, 0, 1, 3).astype(np.float32)


def all_tables(lon_size, lat_size, blocks, bands):
    head, turns = lon_tables(lon_size, STEP, blocks, bands)
    slots, owners, _ = head.shape
    into = np.concatenate([head[..., :STEP].transpose(0, 2, 1), turns.reshape(slots, -1, owners)], axis=1)
    head, turns = lon_tables(lon_size, STEP_BACK, blocks, bands)
    back = halves(head).reshape(-1, head.shape[-1])
    by_lat = lat_basis(lat_size).reshape(lat_size, bands, lat_size // bands)
    by_lat = by_lat.transpose(0, 2, 1).reshape(lat_size, lat_size)
    pad = -lat_size % (2 * LANES)
    by_lat = np.pad(by_lat, ((0, pad), (0, pad)))
    later = np.concatenate([halves(by_lat.T), halves(by_lat), back], axis=0)
    return into.astype(np.float32), later, turns.reshape(-1, SUB, owners)


def split(value):
    high = value.astype(BF16)
    return high, (value - high.astype(F32)).astype(BF16)


def spread(value):
    high, low = split(value)
    return jnp.concatenate([high, low, high], axis=1)


def folded_product(high, low, table_high, table_low):
    rows = high.shape[0]
    both = jnp.dot(jnp.concatenate([high, low], axis=0), table_high, preferred_element_type=F32)
    return both[:rows] + both[rows:] + jnp.dot(high, table_low, preferred_element_type=F32)


def facing(table):
    depth = table.shape[0] // 2
    return [table[:depth], table[:depth], table[depth:]]


def product(value, table):
    return jnp.dot(spread(value), jnp.concatenate(facing(table), axis=0), preferred_element_type=F32)


def partners(value, bands):
    half = bands // 2
    width = value.shape[1]
    upper = lax.broadcasted_iota(jnp.int32, value.shape, 1) % bands >= half
    return jnp.where(upper, pltpu.roll(value, half, 1), pltpu.roll(value, width - half, 1))


def fill_gains(slots, first_gain, out_ref, noise_ref, var_ref, scale_ref, var, scale):
    last = var_ref.shape[0] - 1
    var[...] = jnp.ones_like(var)
    scale[...] = jnp.ones_like(scale)
    for m in range(slots):
        row = jnp.minimum(slots * lax.axis_index("tm") + m, last)
        var[m : m + 1, : var_ref.shape[1]] = var_ref[pl.ds(row, 1), :]
        scale[m : m + 1, : var_ref.shape[1]] = scale_ref[pl.ds(row, 1), :]
    variance = var[...]
    rate = ROOT_FIVE / scale[...]
    damping = jnp.exp(-rate)
    half_square = 0.5 * rate * rate
    for i, move in enumerate((damping, damping * rate, damping * half_square)):
        out_ref[first_gain + i] = move
    twice = damping * damping

    def carried(p):
        top = [p[0, j] + rate * p[1, j] + half_square * p[2, j] for j in range(3)]
        middle = [p[1, j] + rate * p[2, j] for j in range(3)]
        full = {
            (0, 0): top[0] + rate * top[1] + half_square * top[2],
            (0, 1): top[1] + rate * top[2],
            (0, 2): top[2],
            (1, 1): middle[1] + rate * middle[2],
            (1, 2): middle[2],
            (2, 2): p[2, 2],
        }
        return {at: twice * each for at, each in full.items()}

    def symmetric(upper):
        return {(i, j): upper[min(i, j), max(i, j)] for i in range(3) for j in range(3)}

    start = {(i, j): variance * STATIONARY[i][j] for i in range(3) for j in range(i, 3)}
    moved = carried(symmetric(start))
    noise_cov = {at: start[at] - moved[at] for at in start}
    pm = start
    for h in range((out_ref.shape[0] - first_gain - MOVES) // PER_HOUR):
        at = first_gain + MOVES + PER_HOUR * h
        noise = noise_ref[h]
        if h > 0:
            moved = carried(symmetric(cov))
            pm = {entry: moved[entry] + noise_cov[entry] for entry in moved}
        inverse = 1.0 / (pm[0, 0] + noise)
        k = [pm[0, j] * inverse for j in range(3)]
        for j in range(3):
            out_ref[at + j] = k[j]
        out_ref[at + 3] = inverse
        out_ref[at + 4] = jnp.full(inverse.shape, noise, F32)
        cov = {(0, j): noise * k[j] for j in range(3)}
        for i in (1, 2):
            for j in range(i, 3):
                cov[i, j] = pm[i, j] - k[i] * pm[0, j]


def analyse_kernel(
    bands, x_hbm, table_hbm, noise_hbm, var_hbm, scale_hbm, turns_hbm, later_hbm, out_ref, gain_ref,
    later_ref, x, table, flat, blocks, slots_of, noise_ref, var_ref, scale_ref, var, scale, sems,
):
    lats, hours, lon = x.shape
    slots = table.shape[0]
    steps = lon // STEP
    rows = 2 * SUB
    pairs = (
        (var_hbm, var_ref),
        (scale_hbm, scale_ref),
        (noise_hbm, noise_ref),
        (x_hbm, x),
        (table_hbm, table),
        (turns_hbm, gain_ref.at[: turns_hbm.shape[0]]),
        (later_hbm, later_ref),
    )
    fetch = [pltpu.make_async_copy(here, there, sems.at[i]) for i, (here, there) in enumerate(pairs)]
    for copy in fetch:
        copy.start()
    flat[...] = jnp.zeros_like(flat)
    blocks[...] = jnp.zeros_like(blocks)
    slots_of[...] = jnp.zeros_like(slots_of)
    for copy in fetch[:3]:
        copy.wait()
    fill_gains(slots, turns_hbm.shape[0], gain_ref, noise_ref, var_ref, scale_ref, var, scale)
    fetch[3].wait()
    for lat in range(lats):
        flat[lat * hours : (lat + 1) * hours, :lon] = x[lat]
    for b in range(steps):
        blocks[b * rows : (b + 1) * rows, :STEP] = flat[:, b * STEP : (b + 1) * STEP]
    value = spread(blocks[...])
    fetch[4].wait()
    for m in range(slots):
        high, low = split(table[m, :LANES, :])
        part = jnp.dot(value, jnp.concatenate([high, high, low], axis=0), preferred_element_type=F32)
        straight = crossed = None
        for b in range(steps):
            here = part[b * rows : (b + 1) * rows]
            plain = here * table[m, STEP + b : STEP + b + 1, :]
            cross = here * table[m, STEP + steps + b : STEP + steps + b + 1, :]
            straight = plain if straight is None else straight + plain
            crossed = cross if crossed is None else crossed + cross
        slots_of[m * rows : (m + 1) * rows, :] = straight + partners(crossed, bands)
    out_ref[...] = slots_of[...].T
    for copy in fetch[5:]:
        copy.wait()


def smooth_kernel(lats, bands, first_gain, x_ref, gain_ref, later_ref, out_ref, turned, grid, series):
    owners, lanes = x_ref.shape
    hours = (gain_ref.shape[0] - first_gain - MOVES) // PER_HOUR
    blocks = owners // bands
    per_block = hours // blocks
    stride = per_block * SUB
    parts, _, width = turned.shape
    for part in range(parts):
        turned[part] = x_ref[part * width : (part + 1) * width, :].T
    per_part = width // bands
    depth = 2 * grid.shape[1]
    grid[:, lats * bands :] = jnp.zeros((grid.shape[0], grid.shape[1] - lats * bands), F32)
    for h in range(per_block):
        for lat in range(lats):
            for part in range(parts):
                rows = turned[part, pl.ds(lat * per_block + h, SUB, stride=stride), :]
                for t in range(per_part):
                    at = ((part * per_part + t) * per_block + h) * SUB
                    grid[at : at + SUB, lat * bands : (lat + 1) * bands] = rows[:, t * bands : (t + 1) * bands]
    series[...] = product(grid[...], later_ref[:depth, :])

    stay, once, both = (gain_ref[first_gain + i] for i in range(MOVES))
    gain = lambda h, which: gain_ref[first_gain + MOVES + PER_HOUR * h + which]
    scaled = []
    mean = None
    for h in range(hours):
        seen = series[h * SUB : (h + 1) * SUB, :]
        if mean is None:
            error = seen
            mean = [gain(h, j) * error for j in range(3)]
        else:
            ahead = [
                stay * mean[0] + once * mean[1] + both * mean[2],
                stay * mean[1] + once * mean[2],
                stay * mean[2],
            ]
            error = seen - ahead[0]
            mean = [ahead[j] + gain(h, j) * error for j in range(3)]
        scaled.append(error * gain(h, 3))
    adjoint = None
    for h in reversed(range(hours)):
        drop = scaled[h]
        if adjoint is not None:
            drop = drop + (gain(h, 0) * adjoint[0] + gain(h, 1) * adjoint[1] + gain(h, 2) * adjoint[2])
        here = slice(h * SUB, (h + 1) * SUB)
        series[here, :] = series[here, :] - gain(h, 4) * drop
        if adjoint is None:
            adjoint = [-(move * drop) for move in (stay, once, both)]
        else:
            less = adjoint[0] - drop
            adjoint = [
                stay * less,
                once * less + stay * adjoint[1],
                both * less + once * adjoint[1] + stay * adjoint[2],
            ]

    grid[...] = product(series[...], later_ref[depth : 2 * depth, :])
    turned[...] = jnp.zeros_like(turned)
    for h in range(per_block):
        for lat in range(lats):
            for part in range(parts):
                rows = jnp.concatenate(
                    [
                        grid[(t * per_block + h) * SUB : (t * per_block + h + 1) * SUB, lat * bands : (lat + 1) * bands]
                        for t in range(part * per_part, (part + 1) * per_part)
                    ],
                    axis=1,
                )
                turned[part, pl.ds(lat * per_block + h, SUB, stride=stride), :] = rows
    for part in range(parts):
        out_ref[part * width : (part + 1) * width, :] = turned[part].T


def synthesise_kernel(bands, slots, x_ref, later_ref, turns_ref, out_ref, turned, flat):
    lats, hours, lon = out_ref.shape
    steps = lon // STEP_BACK
    rows = 2 * SUB
    turned[...] = x_ref[...].T

    def turn(m, which, b):
        at = (2 * m + which) * steps + b
        return turns_ref[at // SUB, at % SUB : at % SUB + 1, :]

    values = []
    highs = []
    lows = []
    depth = 2 * x_ref.shape[0]
    first = later_ref.shape[0] - slots * depth
    for m in range(slots):
        at = first + m * depth
        highs.append(later_ref[at : at + depth // 2, :])
        lows.append(later_ref[at + depth // 2 : at + depth, :])
        plain = turned[m * rows : (m + 1) * rows, :]
        cross = partners(plain, bands)
        turned_on = [
            plain * turn(m, 0, b) + cross * turn(m, 1, b) for b in range(steps)
        ]
        values.append(split(jnp.concatenate(turned_on, axis=0)))
    high = jnp.concatenate([each[0] for each in values], axis=1)
    low = jnp.concatenate([each[1] for each in values], axis=1)
    total = folded_product(high, low, jnp.concatenate(highs, axis=0), jnp.concatenate(lows, axis=0))
    for b in range(steps):
        flat[:, b * STEP_BACK : (b + 1) * STEP_BACK] = total[b * rows : (b + 1) * rows, :STEP_BACK]
    for lat in range(lats):
        out_ref[lat] = flat[lat * hours : (lat + 1) * hours, :lon]


def params(mib):
    return pltpu.CompilerParams(vmem_limit_bytes=mib * MIB)


def in_hbm(value):
    return pltpu.with_memory_space_constraint(value, pltpu.HBM)


def per_device(tables, observed, noise_var, spectral_var, time_scale):
    lon_into, later, turns = tables
    hours_dev, lat_dev, lon_size = observed.shape
    hours = noise_var.shape[0]
    bands = lax.axis_size("space")
    slots, _, owners = lon_into.shape
    lat_pad = later.shape[-1]
    rows = 2 * SUB
    lanes = SUB * rows
    lon_pad = -(-lon_size // LANES) * LANES
    vmem = pl.BlockSpec(memory_space=pltpu.VMEM)
    smem = pl.BlockSpec(memory_space=pltpu.SMEM)
    hbm = pl.BlockSpec(memory_space=pltpu.HBM)

    by_lat = observed.transpose(1, 0, 2)
    sent, gains, later = pl.pallas_call(
        functools.partial(analyse_kernel, bands),
        out_shape=(
            jax.ShapeDtypeStruct((owners, lanes), F32),
            jax.ShapeDtypeStruct((turns.shape[0] + MOVES + PER_HOUR * hours, SUB, lat_pad), F32),
            jax.ShapeDtypeStruct(later.shape, BF16),
        ),
        in_specs=[hbm] * 7,
        out_specs=(vmem,) * 3,
        scratch_shapes=[
            pltpu.VMEM(by_lat.shape, F32),
            pltpu.VMEM(lon_into.shape, F32),
            pltpu.VMEM((rows, lon_pad), F32),
            pltpu.VMEM((lon_size // STEP * rows, LANES), F32),
            pltpu.VMEM((lanes, owners), F32),
            pltpu.SMEM(noise_var.shape, F32),
            pltpu.VMEM(spectral_var.shape, F32),
            pltpu.VMEM(spectral_var.shape, F32),
            pltpu.VMEM((SUB, lat_pad), F32),
            pltpu.VMEM((SUB, lat_pad), F32),
            pltpu.SemaphoreType.DMA((7,)),
        ],
        compiler_params=params(16),
        name="analyse",
    )(*(in_hbm(each) for each in (by_lat, lon_into, noise_var, spectral_var, time_scale, turns, later)))
    got = lax.all_to_all(sent, ("tm", "space"), split_axis=0, concat_axis=0, tiled=True)

    smooth = pl.pallas_call(
        functools.partial(smooth_kernel, lat_dev, bands, turns.shape[0]),
        out_shape=jax.ShapeDtypeStruct((owners, lanes), F32),
        in_specs=[vmem] * 3,
        out_specs=vmem,
        scratch_shapes=[
            pltpu.VMEM((owners // LANES, lanes, LANES), F32),
            pltpu.VMEM((hours * SUB, lat_pad), F32),
            pltpu.VMEM((hours * SUB, lat_pad), F32),
        ],
        compiler_params=params(16),
        name="smooth",
    )(got, gains, later)
    back = lax.all_to_all(smooth, ("tm", "space"), split_axis=0, concat_axis=0, tiled=True)

    field = pl.pallas_call(
        functools.partial(synthesise_kernel, bands, slots),
        out_shape=jax.ShapeDtypeStruct(by_lat.shape, F32),
        in_specs=[vmem] * 3,
        out_specs=vmem,
        scratch_shapes=[pltpu.VMEM((lanes, owners), F32), pltpu.VMEM((rows, lon_pad), F32)],
        compiler_params=params(16),
        name="synthesise",
    )(back, later, gains)
    return field.transpose(1, 0, 2)


def solution(mesh):
    placed = (P("tm", "space", None), P(), P("space", None), P("space", None))
    blocks, bands = mesh.shape["tm"], mesh.shape["space"]

    def whole(observed, noise_var, spectral_var, time_scale):
        lon_size = observed.shape[2]
        lat_size = spectral_var.shape[1]
        tables = all_tables(observed.shape[2], spectral_var.shape[1], blocks, bands)
        tables = tuple(jnp.asarray(table) for table in tables)
        return jax.shard_map(
            functools.partial(per_device, tables),
            mesh=mesh,
            in_specs=placed,
            out_specs=P("tm", "space", None),
            check_vma=False,
        )(observed, noise_var, spectral_var, time_scale)

    return whole
```

```python
import functools
import math

import jax
import jax.numpy as jnp
import ml_dtypes
import numpy as np
from jax import lax
from jax.experimental import pallas as pl
from jax.experimental.pallas import tpu as pltpu
from jax.sharding import PartitionSpec as P

ROOT_FIVE = 2.23606797749979
STATIONARY = ((1.0, 1.0, 2.0 / 3.0), (1.0, 4.0 / 3.0, 4.0 / 3.0), (2.0 / 3.0, 4.0 / 3.0, 8.0 / 3.0))
MOVES = 3
F32 = jnp.float32
BF16 = jnp.bfloat16
SUB = 8
LANES = 128
PER_HOUR = 5
STEP = 120
STEP_BACK = 240
MIB = 2**20


def halves(table):
    high = table.astype(ml_dtypes.bfloat16)
    low = (table - high.astype(np.float64)).astype(ml_dtypes.bfloat16)
    return np.concatenate([high, low], axis=-2)


def lon_basis(size):
    mode = np.arange(size)[:, None]
    longitude = np.arange(size)[None, :]
    half = size // 2
    sine = mode > half
    frequency = np.where(sine, mode - half, mode)
    radians = (frequency * longitude % size) * (2.0 * math.pi / size)
    weight = np.where((mode == 0) | (mode == half), math.sqrt(1.0 / size), math.sqrt(2.0 / size))
    return np.where(sine, np.sin(radians), np.cos(radians)) * weight


def lat_basis(size):
    wavenumber = np.arange(size)[:, None]
    latitude = np.arange(size)[None, :]
    radians = (wavenumber * (2 * latitude + 1) % (4 * size)) * (math.pi / (2.0 * size))
    weight = np.where(wavenumber == 0, math.sqrt(1.0 / size), math.sqrt(2.0 / size))
    return np.cos(radians) * weight


def lon_tables(size, step, hour_blocks, bands):
    per_band = size // bands
    slots = -(-per_band // hour_blocks)
    half = size // 2
    slot = np.arange(slots)[:, None, None]
    block = np.arange(hour_blocks)[None, :, None]
    band = np.arange(bands)[None, None, :]
    within = slots * block + slot + 0 * band
    used = within < per_band
    mode = np.where(used, per_band * band + within, 0)
    rows = (lon_basis(size)[mode] * used[..., None]).reshape(slots, hour_blocks * bands, size)
    sine = mode > half
    frequency = np.where(sine, mode - half, mode)
    ahead = np.arange(size // step)[:, None, None, None] * step
    radians = (frequency * ahead % size) * (2.0 * math.pi / size)
    straight = np.where(used, np.cos(radians), 0.0)
    crossed = np.where(used & (mode % half != 0), np.sin(radians), 0.0) * np.where(sine, 1.0, -1.0)
    crossed = np.roll(crossed, bands // 2, axis=-1)
    turns = np.stack([straight, crossed]).reshape(2, size // step, slots, hour_blocks * bands)
    head = np.zeros((slots, hour_blocks * bands, -(-step // LANES) * LANES))
    head[..., :step] = rows[..., :step]
    return head, turns.transpose(2, 0, 1, 3).astype(np.float32)


def all_tables(lon_size, lat_size, blocks, bands):
    head, turns = lon_tables(lon_size, STEP, blocks, bands)
    slots, owners, _ = head.shape
    into = np.concatenate([head[..., :STEP].transpose(0, 2, 1), turns.reshape(slots, -1, owners)], axis=1)
    head, turns = lon_tables(lon_size, STEP_BACK, blocks, bands)
    back = halves(head).reshape(-1, head.shape[-1])
    by_lat = lat_basis(lat_size).reshape(lat_size, bands, lat_size // bands)
    by_lat = by_lat.transpose(0, 2, 1).reshape(lat_size, lat_size)
    pad = -lat_size % (2 * LANES)
    by_lat = [np.pad(each, ((0, 0), (0, pad))) for each in (by_lat.T, by_lat)]
    later = np.concatenate([*map(halves, by_lat), back], axis=0)
    into = np.concatenate([into.reshape(-1, owners), turns.reshape(-1, owners)], axis=0)
    return into.astype(np.float32), later


def split(value):
    high = value.astype(BF16)
    return high, (value - high.astype(F32)).astype(BF16)


def spread(value):
    high, low = split(value)
    return jnp.concatenate([high, low, high], axis=1)


def folded_product(high, low, table_high, table_low):
    rows = high.shape[0]
    both = jnp.dot(jnp.concatenate([high, low], axis=0), table_high, preferred_element_type=F32)
    return both[:rows] + both[rows:] + jnp.dot(high, table_low, preferred_element_type=F32)


def product(value, table):
    depth = table.shape[0] // 2
    high, low = split(value[:, :depth])
    return folded_product(high, low, table[:depth], table[depth:])


def partners(value, bands):
    half = bands // 2
    width = value.shape[1]
    upper = lax.broadcasted_iota(jnp.int32, value.shape, 1) % bands >= half
    return jnp.where(upper, pltpu.roll(value, half, 1), pltpu.roll(value, width - half, 1))


def fill_gains(slots, first_gain, out_ref, noise_ref, var_ref, scale_ref, var, scale):
    last = var_ref.shape[0] - 1
    var[...] = jnp.ones_like(var)
    scale[...] = jnp.ones_like(scale)
    for m in range(slots):
        row = jnp.minimum(slots * lax.axis_index("tm") + m, last)
        var[m : m + 1, : var_ref.shape[1]] = var_ref[pl.ds(row, 1), :]
        scale[m : m + 1, : var_ref.shape[1]] = scale_ref[pl.ds(row, 1), :]
    variance = var[...]
    rate = ROOT_FIVE / scale[...]
    damping = jnp.exp(-rate)
    half_square = 0.5 * rate * rate
    for i, move in enumerate((damping, damping * rate, damping * half_square)):
        out_ref[first_gain + i] = move
    twice = damping * damping

    def carried(p):
        top = [p[0, j] + rate * p[1, j] + half_square * p[2, j] for j in range(3)]
        middle = [p[1, j] + rate * p[2, j] for j in range(3)]
        full = {
            (0, 0): top[0] + rate * top[1] + half_square * top[2],
            (0, 1): top[1] + rate * top[2],
            (0, 2): top[2],
            (1, 1): middle[1] + rate * middle[2],
            (1, 2): middle[2],
            (2, 2): p[2, 2],
        }
        return {at: twice * each for at, each in full.items()}

    def symmetric(upper):
        return {(i, j): upper[min(i, j), max(i, j)] for i in range(3) for j in range(3)}

    start = {(i, j): variance * STATIONARY[i][j] for i in range(3) for j in range(i, 3)}
    moved = carried(symmetric(start))
    noise_cov = {at: start[at] - moved[at] for at in start}
    pm = start
    for h in range((out_ref.shape[0] - first_gain - MOVES) // PER_HOUR):
        at = first_gain + MOVES + PER_HOUR * h
        noise = noise_ref[h]
        if h > 0:
            moved = carried(symmetric(cov))
            pm = {entry: moved[entry] + noise_cov[entry] for entry in moved}
        inverse = 1.0 / (pm[0, 0] + noise)
        k = [pm[0, j] * inverse for j in range(3)]
        for j in range(3):
            out_ref[at + j] = k[j]
        out_ref[at + 3] = inverse
        out_ref[at + 4] = jnp.full(inverse.shape, noise, F32)
        cov = {(0, j): noise * k[j] for j in range(3)}
        for i in (1, 2):
            for j in range(i, 3):
                cov[i, j] = pm[i, j] - k[i] * pm[0, j]


def analyse_kernel(
    bands, slots, x_hbm, table_hbm, noise_hbm, var_hbm, scale_hbm, later_hbm, out_ref, gain_ref,
    later_ref, x, table, flat, blocks, slots_of, noise_ref, var_ref, scale_ref, var, scale, sems,
):
    lats, hours, lon = x.shape
    steps = lon // STEP
    depth = STEP + 2 * steps
    turns = (table.shape[0] - slots * depth) // SUB
    rows = 2 * SUB
    pairs = (
        (var_hbm, var_ref),
        (scale_hbm, scale_ref),
        (noise_hbm, noise_ref),
        (x_hbm, x),
        (table_hbm, table),
        (later_hbm, later_ref),
    )
    fetch = [pltpu.make_async_copy(here, there, sems.at[i]) for i, (here, there) in enumerate(pairs)]
    for copy in fetch:
        copy.start()
    flat[...] = jnp.zeros_like(flat)
    blocks[...] = jnp.zeros_like(blocks)
    slots_of[...] = jnp.zeros_like(slots_of)
    for copy in fetch[:3]:
        copy.wait()
    fill_gains(slots, turns, gain_ref, noise_ref, var_ref, scale_ref, var, scale)
    fetch[3].wait()
    for lat in range(lats):
        flat[lat * hours : (lat + 1) * hours, :lon] = x[lat]
    for b in range(steps):
        blocks[b * rows : (b + 1) * rows, :STEP] = flat[:, b * STEP : (b + 1) * STEP]
    value = spread(blocks[...])
    fetch[4].wait()
    for i in range(turns):
        gain_ref[i] = table[slots * depth + i * SUB : slots * depth + (i + 1) * SUB, :]
    for m in range(slots):
        high, low = split(table[m * depth : m * depth + LANES, :])
        part = jnp.dot(value, jnp.concatenate([high, high, low], axis=0), preferred_element_type=F32)
        straight = crossed = None
        for b in range(steps):
            here = part[b * rows : (b + 1) * rows]
            plain = here * table[m * depth + STEP + b : m * depth + STEP + b + 1, :]
            cross = here * table[m * depth + STEP + steps + b : m * depth + STEP + steps + b + 1, :]
            straight = plain if straight is None else straight + plain
            crossed = cross if crossed is None else crossed + cross
        slots_of[m * rows : (m + 1) * rows, :] = straight + partners(crossed, bands)
    out_ref[...] = slots_of[...].T
    for copy in fetch[5:]:
        copy.wait()


def smooth_kernel(lats, bands, first_gain, x_ref, gain_ref, later_ref, out_ref, turned, grid, series):
    owners, lanes = x_ref.shape
    hours = (gain_ref.shape[0] - first_gain - MOVES) // PER_HOUR
    blocks = owners // bands
    per_block = hours // blocks
    stride = per_block * SUB
    parts, _, width = turned.shape
    for part in range(parts):
        turned[part] = x_ref[part * width : (part + 1) * width, :].T
    per_part = width // bands
    depth = 2 * lats * bands
    for h in range(per_block):
        for lat in range(lats):
            for part in range(parts):
                rows = turned[part, pl.ds(lat * per_block + h, SUB, stride=stride), :]
                for t in range(per_part):
                    at = ((part * per_part + t) * per_block + h) * SUB
                    grid[at : at + SUB, lat * bands : (lat + 1) * bands] = rows[:, t * bands : (t + 1) * bands]
    series[...] = product(grid[...], later_ref[:depth, :])

    stay, once, both = (gain_ref[first_gain + i] for i in range(MOVES))
    gain = lambda h, which: gain_ref[first_gain + MOVES + PER_HOUR * h + which]
    scaled = []
    mean = None
    for h in range(hours):
        seen = series[h * SUB : (h + 1) * SUB, :]
        if mean is None:
            error = seen
            mean = [gain(h, j) * error for j in range(3)]
        else:
            ahead = [
                stay * mean[0] + once * mean[1] + both * mean[2],
                stay * mean[1] + once * mean[2],
                stay * mean[2],
            ]
            error = seen - ahead[0]
            mean = [ahead[j] + gain(h, j) * error for j in range(3)]
        scaled.append(error * gain(h, 3))
    adjoint = None
    for h in reversed(range(hours)):
        drop = scaled[h]
        if adjoint is not None:
            drop = drop + (gain(h, 0) * adjoint[0] + gain(h, 1) * adjoint[1] + gain(h, 2) * adjoint[2])
        here = slice(h * SUB, (h + 1) * SUB)
        series[here, :] = series[here, :] - gain(h, 4) * drop
        if adjoint is None:
            adjoint = [-(move * drop) for move in (stay, once, both)]
        else:
            less = adjoint[0] - drop
            adjoint = [
                stay * less,
                once * less + stay * adjoint[1],
                both * less + once * adjoint[1] + stay * adjoint[2],
            ]

    grid[...] = product(series[...], later_ref[depth : 2 * depth, :])
    for h in range(per_block):
        for lat in range(lats):
            for part in range(parts):
                rows = jnp.concatenate(
                    [
                        grid[(t * per_block + h) * SUB : (t * per_block + h + 1) * SUB, lat * bands : (lat + 1) * bands]
                        for t in range(part * per_part, (part + 1) * per_part)
                    ],
                    axis=1,
                )
                turned[part, pl.ds(lat * per_block + h, SUB, stride=stride), :] = rows
    for part in range(parts):
        out_ref[part * width : (part + 1) * width, :] = turned[part].T


def synthesise_kernel(bands, slots, x_ref, later_ref, turns_ref, out_ref, turned, flat):
    lats, hours, lon = out_ref.shape
    steps = lon // STEP_BACK
    rows = 2 * SUB
    turned[...] = x_ref[...].T

    def turn(m, which, b):
        at = (2 * m + which) * steps + b
        return turns_ref[at // SUB, at % SUB : at % SUB + 1, :]

    values = []
    highs = []
    lows = []
    depth = 2 * x_ref.shape[0]
    first = later_ref.shape[0] - slots * depth
    for m in range(slots):
        at = first + m * depth
        highs.append(later_ref[at : at + depth // 2, :])
        lows.append(later_ref[at + depth // 2 : at + depth, :])
        plain = turned[m * rows : (m + 1) * rows, :]
        cross = partners(plain, bands)
        turned_on = [
            plain * turn(m, 0, b) + cross * turn(m, 1, b) for b in range(steps)
        ]
        values.append(split(jnp.concatenate(turned_on, axis=0)))
    high = jnp.concatenate([each[0] for each in values], axis=1)
    low = jnp.concatenate([each[1] for each in values], axis=1)
    total = folded_product(high, low, jnp.concatenate(highs, axis=0), jnp.concatenate(lows, axis=0))
    for b in range(steps):
        flat[:, b * STEP_BACK : (b + 1) * STEP_BACK] = total[b * rows : (b + 1) * rows, :STEP_BACK]
    for lat in range(lats):
        out_ref[lat] = flat[lat * hours : (lat + 1) * hours, :lon]


def params(mib):
    return pltpu.CompilerParams(vmem_limit_bytes=mib * MIB)


def in_hbm(value):
    return pltpu.with_memory_space_constraint(value, pltpu.HBM)


def per_device(tables, observed, noise_var, spectral_var, time_scale):
    lon_into, later = tables
    hours_dev, lat_dev, lon_size = observed.shape
    hours = noise_var.shape[0]
    bands = lax.axis_size("space")
    owners = lon_into.shape[1]
    slots = -(-spectral_var.shape[0] // lax.axis_size("tm"))
    turns = 2 * slots * (lon_size // STEP_BACK) // SUB
    lat_pad = later.shape[-1]
    rows = 2 * SUB
    lanes = SUB * rows
    lon_pad = -(-lon_size // LANES) * LANES
    vmem = pl.BlockSpec(memory_space=pltpu.VMEM)
    smem = pl.BlockSpec(memory_space=pltpu.SMEM)
    hbm = pl.BlockSpec(memory_space=pltpu.HBM)

    by_lat = observed.transpose(1, 0, 2)
    sent, gains, later = pl.pallas_call(
        functools.partial(analyse_kernel, bands, slots),
        out_shape=(
            jax.ShapeDtypeStruct((owners, lanes), F32),
            jax.ShapeDtypeStruct((turns + MOVES + PER_HOUR * hours, SUB, lat_pad), F32),
            jax.ShapeDtypeStruct(later.shape, BF16),
        ),
        in_specs=[hbm] * 6,
        out_specs=(vmem,) * 3,
        scratch_shapes=[
            pltpu.VMEM(by_lat.shape, F32),
            pltpu.VMEM(lon_into.shape, F32),
            pltpu.VMEM((rows, lon_pad), F32),
            pltpu.VMEM((lon_size // STEP * rows, LANES), F32),
            pltpu.VMEM((lanes, owners), F32),
            pltpu.SMEM(noise_var.shape, F32),
            pltpu.VMEM(spectral_var.shape, F32),
            pltpu.VMEM(spectral_var.shape, F32),
            pltpu.VMEM((SUB, lat_pad), F32),
            pltpu.VMEM((SUB, lat_pad), F32),
            pltpu.SemaphoreType.DMA((6,)),
        ],
        compiler_params=params(16),
        name="analyse",
    )(*(in_hbm(each) for each in (by_lat, lon_into, noise_var, spectral_var, time_scale, later)))
    got = lax.all_to_all(sent, ("tm", "space"), split_axis=0, concat_axis=0, tiled=True)

    smooth = pl.pallas_call(
        functools.partial(smooth_kernel, lat_dev, bands, turns),
        out_shape=jax.ShapeDtypeStruct((owners, lanes), F32),
        in_specs=[vmem] * 3,
        out_specs=vmem,
        scratch_shapes=[
            pltpu.VMEM((owners // LANES, lanes, LANES), F32),
            pltpu.VMEM((hours * SUB, lat_pad), F32),
            pltpu.VMEM((hours * SUB, lat_pad), F32),
        ],
        compiler_params=params(16),
        name="smooth",
    )(got, gains, later)
    back = lax.all_to_all(smooth, ("tm", "space"), split_axis=0, concat_axis=0, tiled=True)

    field = pl.pallas_call(
        functools.partial(synthesise_kernel, bands, slots),
        out_shape=jax.ShapeDtypeStruct(by_lat.shape, F32),
        in_specs=[vmem] * 3,
        out_specs=vmem,
        scratch_shapes=[pltpu.VMEM((lanes, owners), F32), pltpu.VMEM((rows, lon_pad), F32)],
        compiler_params=params(16),
        name="synthesise",
    )(back, later, gains)
    return field.transpose(1, 0, 2)


def solution(mesh):
    placed = (P("tm", "space", None), P(), P("space", None), P("space", None))
    blocks, bands = mesh.shape["tm"], mesh.shape["space"]

    def whole(observed, noise_var, spectral_var, time_scale):
        lon_size = observed.shape[2]
        lat_size = spectral_var.shape[1]
        tables = all_tables(observed.shape[2], spectral_var.shape[1], blocks, bands)
        tables = tuple(jnp.asarray(table) for table in tables)
        return jax.shard_map(
            functools.partial(per_device, tables),
            mesh=mesh,
            in_specs=placed,
            out_specs=P("tm", "space", None),
            check_vma=False,
        )(observed, noise_var, spectral_var, time_scale)

    return whole
```

```python
import functools
import math

import jax
import jax.numpy as jnp
import ml_dtypes
import numpy as np
from jax import lax
from jax.experimental import pallas as pl
from jax.experimental.pallas import tpu as pltpu
from jax.sharding import PartitionSpec as P

ROOT_FIVE = 2.23606797749979
STATIONARY = ((1.0, 1.0, 2.0 / 3.0), (1.0, 4.0 / 3.0, 4.0 / 3.0), (2.0 / 3.0, 4.0 / 3.0, 8.0 / 3.0))
MOVES = 3
F32 = jnp.float32
BF16 = jnp.bfloat16
SUB = 8
LANES = 128
PER_HOUR = 5
STEP = 120
STEP_BACK = 240
MIB = 2**20


def halves(table):
    high = table.astype(ml_dtypes.bfloat16)
    low = (table - high.astype(np.float64)).astype(ml_dtypes.bfloat16)
    return np.concatenate([high, low], axis=-2)


def lon_basis(size):
    mode = np.arange(size)[:, None]
    longitude = np.arange(size)[None, :]
    half = size // 2
    sine = mode > half
    frequency = np.where(sine, mode - half, mode)
    radians = (frequency * longitude % size) * (2.0 * math.pi / size)
    weight = np.where((mode == 0) | (mode == half), math.sqrt(1.0 / size), math.sqrt(2.0 / size))
    return np.where(sine, np.sin(radians), np.cos(radians)) * weight


def lat_basis(size):
    wavenumber = np.arange(size)[:, None]
    latitude = np.arange(size)[None, :]
    radians = (wavenumber * (2 * latitude + 1) % (4 * size)) * (math.pi / (2.0 * size))
    weight = np.where(wavenumber == 0, math.sqrt(1.0 / size), math.sqrt(2.0 / size))
    return np.cos(radians) * weight


def lon_tables(size, step, hour_blocks, bands):
    per_band = size // bands
    slots = -(-per_band // hour_blocks)
    half = size // 2
    slot = np.arange(slots)[:, None, None]
    block = np.arange(hour_blocks)[None, :, None]
    band = np.arange(bands)[None, None, :]
    within = slots * block + slot + 0 * band
    used = within < per_band
    mode = np.where(used, per_band * band + within, 0)
    rows = (lon_basis(size)[mode] * used[..., None]).reshape(slots, hour_blocks * bands, size)
    sine = mode > half
    frequency = np.where(sine, mode - half, mode)
    ahead = np.arange(size // step)[:, None, None, None] * step
    radians = (frequency * ahead % size) * (2.0 * math.pi / size)
    straight = np.where(used, np.cos(radians), 0.0)
    crossed = np.where(used & (mode % half != 0), np.sin(radians), 0.0) * np.where(sine, 1.0, -1.0)
    crossed = np.roll(crossed, bands // 2, axis=-1)
    turns = np.stack([straight, crossed]).reshape(2, size // step, slots, hour_blocks * bands)
    head = np.zeros((slots, hour_blocks * bands, -(-step // LANES) * LANES))
    head[..., :step] = rows[..., :step]
    return head, turns.transpose(2, 0, 1, 3).astype(np.float32)


def all_tables(lon_size, lat_size, blocks, bands):
    head, turns = lon_tables(lon_size, STEP, blocks, bands)
    slots, owners, _ = head.shape
    into = np.concatenate([head[..., :STEP].transpose(0, 2, 1), turns.reshape(slots, -1, owners)], axis=1)
    head, turns = lon_tables(lon_size, STEP_BACK, blocks, bands)
    back = halves(head).reshape(-1, head.shape[-1])
    by_lat = lat_basis(lat_size).reshape(lat_size, bands, lat_size // bands)
    by_lat = by_lat.transpose(0, 2, 1).reshape(lat_size, lat_size)
    pad = -lat_size % (2 * LANES)
    by_lat = [np.pad(each, ((0, 0), (0, pad))) for each in (by_lat.T, by_lat)]
    later = np.concatenate([*map(halves, by_lat), back], axis=0)
    into = np.concatenate([into.reshape(-1, owners), turns.reshape(-1, owners)], axis=0)
    return into.astype(np.float32), later


def split(value):
    high = value.astype(BF16)
    return high, (value - high.astype(F32)).astype(BF16)


def spread(value):
    high, low = split(value)
    return jnp.concatenate([high, low, high], axis=1)


def folded_product(high, low, table_high, table_low):
    rows = high.shape[0]
    both = jnp.dot(jnp.concatenate([high, low], axis=0), table_high, preferred_element_type=F32)
    return both[:rows] + both[rows:] + jnp.dot(high, table_low, preferred_element_type=F32)


def product(value, table):
    depth = table.shape[0] // 2
    high, low = split(value[:, :depth])
    return folded_product(high, low, table[:depth], table[depth:])


def partners(value, bands):
    half = bands // 2
    width = value.shape[1]
    upper = lax.broadcasted_iota(jnp.int32, value.shape, 1) % bands >= half
    return jnp.where(upper, pltpu.roll(value, half, 1), pltpu.roll(value, width - half, 1))


def fill_gains(slots, first_gain, out_ref, noise_ref, var_ref, scale_ref, var, scale):
    last = var_ref.shape[0] - 1
    var[...] = jnp.ones_like(var)
    scale[...] = jnp.ones_like(scale)
    for m in range(slots):
        row = jnp.minimum(slots * lax.axis_index("tm") + m, last)
        var[m : m + 1, : var_ref.shape[1]] = var_ref[pl.ds(row, 1), :]
        scale[m : m + 1, : var_ref.shape[1]] = scale_ref[pl.ds(row, 1), :]
    variance = var[...]
    rate = ROOT_FIVE / scale[...]
    damping = jnp.exp(-rate)
    half_square = 0.5 * rate * rate
    for i, move in enumerate((damping, damping * rate, damping * half_square)):
        out_ref[first_gain + i] = move
    twice = damping * damping

    def carried(p):
        top = [p[0, j] + rate * p[1, j] + half_square * p[2, j] for j in range(3)]
        middle = [p[1, j] + rate * p[2, j] for j in range(3)]
        full = {
            (0, 0): top[0] + rate * top[1] + half_square * top[2],
            (0, 1): top[1] + rate * top[2],
            (0, 2): top[2],
            (1, 1): middle[1] + rate * middle[2],
            (1, 2): middle[2],
            (2, 2): p[2, 2],
        }
        return {at: twice * each for at, each in full.items()}

    def symmetric(upper):
        return {(i, j): upper[min(i, j), max(i, j)] for i in range(3) for j in range(3)}

    start = {(i, j): variance * STATIONARY[i][j] for i in range(3) for j in range(i, 3)}
    moved = carried(symmetric(start))
    noise_cov = {at: start[at] - moved[at] for at in start}
    pm = start
    for h in range((out_ref.shape[0] - first_gain - MOVES) // PER_HOUR):
        at = first_gain + MOVES + PER_HOUR * h
        noise = noise_ref[h]
        if h > 0:
            moved = carried(symmetric(cov))
            pm = {entry: moved[entry] + noise_cov[entry] for entry in moved}
        inverse = 1.0 / (pm[0, 0] + noise)
        k = [pm[0, j] * inverse for j in range(3)]
        for j in range(3):
            out_ref[at + j] = k[j]
        out_ref[at + 3] = inverse
        out_ref[at + 4] = jnp.full(inverse.shape, noise, F32)
        cov = {(0, j): noise * k[j] for j in range(3)}
        for i in (1, 2):
            for j in range(i, 3):
                cov[i, j] = pm[i, j] - k[i] * pm[0, j]


def analyse_kernel(
    bands, slots, x_hbm, table_hbm, noise_hbm, var_hbm, scale_hbm, later_hbm, out_ref, gain_ref,
    later_ref, x, table, flat, blocks, slots_of, noise_ref, var_ref, scale_ref, var, scale, sems,
):
    lats, hours, lon = x.shape
    steps = lon // STEP
    depth = STEP + 2 * steps
    turns = (table.shape[0] - slots * depth) // SUB
    rows = 2 * SUB
    pairs = (
        (var_hbm, var_ref),
        (scale_hbm, scale_ref),
        (noise_hbm, noise_ref),
        (x_hbm, x),
        (table_hbm, table),
        (later_hbm, later_ref),
    )
    fetch = [pltpu.make_async_copy(here, there, sems.at[i]) for i, (here, there) in enumerate(pairs)]
    for copy in fetch:
        copy.start()
    flat[...] = jnp.zeros_like(flat)
    blocks[...] = jnp.zeros_like(blocks)
    slots_of[...] = jnp.zeros_like(slots_of)
    for copy in fetch[:3]:
        copy.wait()
    fill_gains(slots, turns, gain_ref, noise_ref, var_ref, scale_ref, var, scale)
    fetch[3].wait()
    for lat in range(lats):
        flat[lat * hours : (lat + 1) * hours, :lon] = x[lat]
    for b in range(steps):
        blocks[b * rows : (b + 1) * rows, :STEP] = flat[:, b * STEP : (b + 1) * STEP]
    value = spread(blocks[...])
    fetch[4].wait()
    for i in range(turns):
        gain_ref[i] = table[slots * depth + i * SUB : slots * depth + (i + 1) * SUB, :]
    for m in range(slots):
        high, low = split(table[m * depth : m * depth + LANES, :])
        part = jnp.dot(value, jnp.concatenate([high, high, low], axis=0), preferred_element_type=F32)
        straight = crossed = None
        for b in range(steps):
            here = part[b * rows : (b + 1) * rows]
            plain = here * table[m * depth + STEP + b : m * depth + STEP + b + 1, :]
            cross = here * table[m * depth + STEP + steps + b : m * depth + STEP + steps + b + 1, :]
            straight = plain if straight is None else straight + plain
            crossed = cross if crossed is None else crossed + cross
        slots_of[m * rows : (m + 1) * rows, :] = straight + partners(crossed, bands)
    out_ref[...] = slots_of[...].T
    for copy in fetch[5:]:
        copy.wait()


def smooth_kernel(lats, bands, first_gain, x_ref, gain_ref, later_ref, out_ref, turned, grid, series):
    owners, lanes = x_ref.shape
    hours = (gain_ref.shape[0] - first_gain - MOVES) // PER_HOUR
    blocks = owners // bands
    per_block = hours // blocks
    stride = per_block * SUB
    parts, _, width = turned.shape
    for part in range(parts):
        turned[part] = x_ref[part * width : (part + 1) * width, :].T
    per_part = width // bands
    depth = 2 * lats * bands
    for h in range(per_block):
        for lat in range(lats):
            for part in range(parts):
                rows = turned[part, pl.ds(lat * per_block + h, SUB, stride=stride), :]
                for t in range(per_part):
                    at = ((part * per_part + t) * per_block + h) * SUB
                    grid[at : at + SUB, lat * bands : (lat + 1) * bands] = rows[:, t * bands : (t + 1) * bands]
    series[...] = product(grid[...], later_ref[:depth, :])

    stay, once, both = (gain_ref[first_gain + i] for i in range(MOVES))
    gain = lambda h, which: gain_ref[first_gain + MOVES + PER_HOUR * h + which]
    scaled = []
    mean = None
    for h in range(hours):
        seen = series[h * SUB : (h + 1) * SUB, :]
        if mean is None:
            error = seen
            mean = [gain(h, j) * error for j in range(3)]
        else:
            kept, shift = stay * mean[0], once * mean[1] + both * mean[2]
            ahead = [kept + shift, stay * mean[1] + once * mean[2], stay * mean[2]]
            error = (seen - kept) - shift
            mean = [ahead[j] + gain(h, j) * error for j in range(3)]
        scaled.append(error * gain(h, 3))
    adjoint = None
    for h in reversed(range(hours)):
        drop = scaled[h]
        if adjoint is not None:
            drop = (drop + gain(h, 0) * adjoint[0]) + (gain(h, 1) * adjoint[1] + gain(h, 2) * adjoint[2])
        here = slice(h * SUB, (h + 1) * SUB)
        series[here, :] = series[here, :] - gain(h, 4) * drop
        if adjoint is None:
            adjoint = [-(move * drop) for move in (stay, once, both)]
        else:
            moved = [
                stay * adjoint[0],
                once * adjoint[0] + stay * adjoint[1],
                both * adjoint[0] + (once * adjoint[1] + stay * adjoint[2]),
            ]
            adjoint = [value - move * drop for value, move in zip(moved, (stay, once, both))]

    grid[...] = product(series[...], later_ref[depth : 2 * depth, :])
    for h in range(per_block):
        for lat in range(lats):
            for part in range(parts):
                rows = jnp.concatenate(
                    [
                        grid[(t * per_block + h) * SUB : (t * per_block + h + 1) * SUB, lat * bands : (lat + 1) * bands]
                        for t in range(part * per_part, (part + 1) * per_part)
                    ],
                    axis=1,
                )
                turned[part, pl.ds(lat * per_block + h, SUB, stride=stride), :] = rows
    for part in range(parts):
        out_ref[part * width : (part + 1) * width, :] = turned[part].T


def synthesise_kernel(bands, slots, x_ref, later_ref, turns_ref, out_ref, turned, flat):
    lats, hours, lon = out_ref.shape
    steps = lon // STEP_BACK
    rows = 2 * SUB
    turned[...] = x_ref[...].T

    def turn(m, which, b):
        at = (2 * m + which) * steps + b
        return turns_ref[at // SUB, at % SUB : at % SUB + 1, :]

    values = []
    highs = []
    lows = []
    depth = 2 * x_ref.shape[0]
    first = later_ref.shape[0] - slots * depth
    for m in range(slots):
        at = first + m * depth
        highs.append(later_ref[at : at + depth // 2, :])
        lows.append(later_ref[at + depth // 2 : at + depth, :])
        plain = turned[m * rows : (m + 1) * rows, :]
        cross = partners(plain, bands)
        turned_on = [
            plain * turn(m, 0, b) + cross * turn(m, 1, b) for b in range(steps)
        ]
        values.append(split(jnp.concatenate(turned_on, axis=0)))
    high = jnp.concatenate([each[0] for each in values], axis=1)
    low = jnp.concatenate([each[1] for each in values], axis=1)
    total = folded_product(high, low, jnp.concatenate(highs, axis=0), jnp.concatenate(lows, axis=0))
    for b in range(steps):
        flat[:, b * STEP_BACK : (b + 1) * STEP_BACK] = total[b * rows : (b + 1) * rows, :STEP_BACK]
    for lat in range(lats):
        out_ref[lat] = flat[lat * hours : (lat + 1) * hours, :lon]


def params(mib):
    return pltpu.CompilerParams(vmem_limit_bytes=mib * MIB)


def in_hbm(value):
    return pltpu.with_memory_space_constraint(value, pltpu.HBM)


def per_device(tables, observed, noise_var, spectral_var, time_scale):
    lon_into, later = tables
    hours_dev, lat_dev, lon_size = observed.shape
    hours = noise_var.shape[0]
    bands = lax.axis_size("space")
    owners = lon_into.shape[1]
    slots = -(-spectral_var.shape[0] // lax.axis_size("tm"))
    turns = 2 * slots * (lon_size // STEP_BACK) // SUB
    lat_pad = later.shape[-1]
    rows = 2 * SUB
    lanes = SUB * rows
    lon_pad = -(-lon_size // LANES) * LANES
    vmem = pl.BlockSpec(memory_space=pltpu.VMEM)
    smem = pl.BlockSpec(memory_space=pltpu.SMEM)
    hbm = pl.BlockSpec(memory_space=pltpu.HBM)

    by_lat = observed.transpose(1, 0, 2)
    sent, gains, later = pl.pallas_call(
        functools.partial(analyse_kernel, bands, slots),
        out_shape=(
            jax.ShapeDtypeStruct((owners, lanes), F32),
            jax.ShapeDtypeStruct((turns + MOVES + PER_HOUR * hours, SUB, lat_pad), F32),
            jax.ShapeDtypeStruct(later.shape, BF16),
        ),
        in_specs=[hbm] * 6,
        out_specs=(vmem,) * 3,
        scratch_shapes=[
            pltpu.VMEM(by_lat.shape, F32),
            pltpu.VMEM(lon_into.shape, F32),
            pltpu.VMEM((rows, lon_pad), F32),
            pltpu.VMEM((lon_size // STEP * rows, LANES), F32),
            pltpu.VMEM((lanes, owners), F32),
            pltpu.SMEM(noise_var.shape, F32),
            pltpu.VMEM(spectral_var.shape, F32),
            pltpu.VMEM(spectral_var.shape, F32),
            pltpu.VMEM((SUB, lat_pad), F32),
            pltpu.VMEM((SUB, lat_pad), F32),
            pltpu.SemaphoreType.DMA((6,)),
        ],
        compiler_params=params(16),
        name="analyse",
    )(*(in_hbm(each) for each in (by_lat, lon_into, noise_var, spectral_var, time_scale, later)))
    got = lax.all_to_all(sent, ("tm", "space"), split_axis=0, concat_axis=0, tiled=True)

    smooth = pl.pallas_call(
        functools.partial(smooth_kernel, lat_dev, bands, turns),
        out_shape=jax.ShapeDtypeStruct((owners, lanes), F32),
        in_specs=[vmem] * 3,
        out_specs=vmem,
        scratch_shapes=[
            pltpu.VMEM((owners // LANES, lanes, LANES), F32),
            pltpu.VMEM((hours * SUB, lat_pad), F32),
            pltpu.VMEM((hours * SUB, lat_pad), F32),
        ],
        compiler_params=params(16),
        name="smooth",
    )(got, gains, later)
    back = lax.all_to_all(smooth, ("tm", "space"), split_axis=0, concat_axis=0, tiled=True)

    field = pl.pallas_call(
        functools.partial(synthesise_kernel, bands, slots),
        out_shape=jax.ShapeDtypeStruct(by_lat.shape, F32),
        in_specs=[vmem] * 3,
        out_specs=vmem,
        scratch_shapes=[pltpu.VMEM((lanes, owners), F32), pltpu.VMEM((rows, lon_pad), F32)],
        compiler_params=params(16),
        name="synthesise",
    )(back, later, gains)
    return field.transpose(1, 0, 2)


def solution(mesh):
    placed = (P("tm", "space", None), P(), P("space", None), P("space", None))
    blocks, bands = mesh.shape["tm"], mesh.shape["space"]

    def whole(observed, noise_var, spectral_var, time_scale):
        lon_size = observed.shape[2]
        lat_size = spectral_var.shape[1]
        tables = all_tables(observed.shape[2], spectral_var.shape[1], blocks, bands)
        tables = tuple(jnp.asarray(table) for table in tables)
        return jax.shard_map(
            functools.partial(per_device, tables),
            mesh=mesh,
            in_specs=placed,
            out_specs=P("tm", "space", None),
            check_vma=False,
        )(observed, noise_var, spectral_var, time_scale)

    return whole
```

```python
import functools
import math

import jax
import jax.numpy as jnp
import ml_dtypes
import numpy as np
from jax import lax
from jax.experimental import pallas as pl
from jax.experimental.pallas import tpu as pltpu
from jax.sharding import PartitionSpec as P

ROOT_FIVE = 2.23606797749979
STATIONARY = ((1.0, 1.0, 2.0 / 3.0), (1.0, 4.0 / 3.0, 4.0 / 3.0), (2.0 / 3.0, 4.0 / 3.0, 8.0 / 3.0))
MOVES = 3
F32 = jnp.float32
BF16 = jnp.bfloat16
SUB = 8
LANES = 128
PER_HOUR = 5
STEP = 120
STEP_BACK = 240
MIB = 2**20


def halves(table):
    high = table.astype(ml_dtypes.bfloat16)
    low = (table - high.astype(np.float64)).astype(ml_dtypes.bfloat16)
    return np.concatenate([high, low], axis=-2)


def lon_basis(size):
    mode = np.arange(size)[:, None]
    longitude = np.arange(size)[None, :]
    half = size // 2
    sine = mode > half
    frequency = np.where(sine, mode - half, mode)
    radians = (frequency * longitude % size) * (2.0 * math.pi / size)
    weight = np.where((mode == 0) | (mode == half), math.sqrt(1.0 / size), math.sqrt(2.0 / size))
    return np.where(sine, np.sin(radians), np.cos(radians)) * weight


def lat_basis(size):
    wavenumber = np.arange(size)[:, None]
    latitude = np.arange(size)[None, :]
    radians = (wavenumber * (2 * latitude + 1) % (4 * size)) * (math.pi / (2.0 * size))
    weight = np.where(wavenumber == 0, math.sqrt(1.0 / size), math.sqrt(2.0 / size))
    return np.cos(radians) * weight


def lon_tables(size, step, hour_blocks, bands):
    per_band = size // bands
    slots = -(-per_band // hour_blocks)
    half = size // 2
    slot = np.arange(slots)[:, None, None]
    block = np.arange(hour_blocks)[None, :, None]
    band = np.arange(bands)[None, None, :]
    within = slots * block + slot + 0 * band
    used = within < per_band
    mode = np.where(used, per_band * band + within, 0)
    rows = (lon_basis(size)[mode] * used[..., None]).reshape(slots, hour_blocks * bands, size)
    sine = mode > half
    frequency = np.where(sine, mode - half, mode)
    ahead = np.arange(size // step)[:, None, None, None] * step
    radians = (frequency * ahead % size) * (2.0 * math.pi / size)
    straight = np.where(used, np.cos(radians), 0.0)
    crossed = np.where(used & (mode % half != 0), np.sin(radians), 0.0) * np.where(sine, 1.0, -1.0)
    crossed = np.roll(crossed, bands // 2, axis=-1)
    turns = np.stack([straight, crossed]).reshape(2, size // step, slots, hour_blocks * bands)
    head = np.zeros((slots, hour_blocks * bands, -(-step // LANES) * LANES))
    head[..., :step] = rows[..., :step]
    return head, turns.transpose(2, 0, 1, 3).astype(np.float32)


def all_tables(lon_size, lat_size, blocks, bands):
    head, turns = lon_tables(lon_size, STEP, blocks, bands)
    slots, owners, _ = head.shape
    into = np.concatenate([head[..., :STEP].transpose(0, 2, 1), turns.reshape(slots, -1, owners)], axis=1)
    head, turns = lon_tables(lon_size, STEP_BACK, blocks, bands)
    back = halves(head).reshape(-1, head.shape[-1])
    by_lat = lat_basis(lat_size).reshape(lat_size, bands, lat_size // bands)
    by_lat = by_lat.transpose(0, 2, 1).reshape(lat_size, lat_size)
    pad = -lat_size % (2 * LANES)
    by_lat = [np.pad(each, ((0, 0), (0, pad))) for each in (by_lat.T, by_lat)]
    later = np.concatenate([*map(halves, by_lat), back], axis=0)
    into = np.concatenate([into.reshape(-1, owners), turns.reshape(-1, owners)], axis=0)
    return into.astype(np.float32), later


def split(value):
    high = value.astype(BF16)
    return high, (value - high.astype(F32)).astype(BF16)


def spread(value):
    high, low = split(value)
    return jnp.concatenate([high, low, high], axis=1)


def folded_product(high, low, table_high, table_low):
    rows = high.shape[0]
    both = jnp.dot(jnp.concatenate([high, low], axis=0), table_high, preferred_element_type=F32)
    return both[:rows] + both[rows:] + jnp.dot(high, table_low, preferred_element_type=F32)


def product(value, table):
    depth = table.shape[0] // 2
    high, low = split(value[:, :depth])
    return folded_product(high, low, table[:depth], table[depth:])


def partners(value, bands):
    half = bands // 2
    width = value.shape[1]
    upper = lax.broadcasted_iota(jnp.int32, value.shape, 1) % bands >= half
    return jnp.where(upper, pltpu.roll(value, half, 1), pltpu.roll(value, width - half, 1))


def fill_gains(slots, first_gain, out_ref, noise_ref, var_ref, scale_ref, var, scale):
    last = var_ref.shape[0] - 1
    var[...] = jnp.ones_like(var)
    scale[...] = jnp.ones_like(scale)
    for m in range(slots):
        row = jnp.minimum(slots * lax.axis_index("tm") + m, last)
        var[m : m + 1, : var_ref.shape[1]] = var_ref[pl.ds(row, 1), :]
        scale[m : m + 1, : var_ref.shape[1]] = scale_ref[pl.ds(row, 1), :]
    variance = var[...]
    rate = ROOT_FIVE / scale[...]
    damping = jnp.exp(-rate)
    half_square = 0.5 * rate * rate
    for i, move in enumerate((damping, damping * rate, damping * half_square)):
        out_ref[first_gain + i] = move
    twice = damping * damping

    def carried(p):
        top = [p[0, j] + rate * p[1, j] + half_square * p[2, j] for j in range(3)]
        middle = [p[1, j] + rate * p[2, j] for j in range(3)]
        full = {
            (0, 0): top[0] + rate * top[1] + half_square * top[2],
            (0, 1): top[1] + rate * top[2],
            (0, 2): top[2],
            (1, 1): middle[1] + rate * middle[2],
            (1, 2): middle[2],
            (2, 2): p[2, 2],
        }
        return {at: twice * each for at, each in full.items()}

    def symmetric(upper):
        return {(i, j): upper[min(i, j), max(i, j)] for i in range(3) for j in range(3)}

    start = {(i, j): variance * STATIONARY[i][j] for i in range(3) for j in range(i, 3)}
    moved = carried(symmetric(start))
    noise_cov = {at: start[at] - moved[at] for at in start}
    pm = start
    for h in range((out_ref.shape[0] - first_gain - MOVES) // PER_HOUR):
        at = first_gain + MOVES + PER_HOUR * h
        noise = noise_ref[h]
        if h > 0:
            moved = carried(symmetric(cov))
            pm = {entry: moved[entry] + noise_cov[entry] for entry in moved}
        inverse = 1.0 / (pm[0, 0] + noise)
        k = [pm[0, j] * inverse for j in range(3)]
        for j in range(3):
            out_ref[at + j] = k[j]
        out_ref[at + 3] = inverse
        out_ref[at + 4] = jnp.full(inverse.shape, noise, F32)
        cov = {(0, j): noise * k[j] for j in range(3)}
        for i in (1, 2):
            for j in range(i, 3):
                cov[i, j] = pm[i, j] - k[i] * pm[0, j]


def analyse_kernel(
    bands, slots, x_hbm, table_hbm, noise_hbm, var_hbm, scale_hbm, later_hbm, out_ref, gain_ref,
    later_ref, x, table, flat, blocks, slots_of, noise_ref, var_ref, scale_ref, var, scale, sems,
):
    lats, hours, lon = x.shape
    steps = lon // STEP
    depth = STEP + 2 * steps
    turns = (table.shape[0] - slots * depth) // SUB
    rows = 2 * SUB
    pairs = (
        (var_hbm, var_ref),
        (scale_hbm, scale_ref),
        (noise_hbm, noise_ref),
        (x_hbm, x),
        (table_hbm, table),
        (later_hbm, later_ref),
    )
    fetch = [pltpu.make_async_copy(here, there, sems.at[i]) for i, (here, there) in enumerate(pairs)]
    for copy in fetch:
        copy.start()
    flat[...] = jnp.zeros_like(flat)
    blocks[...] = jnp.zeros_like(blocks)
    slots_of[...] = jnp.zeros_like(slots_of)
    for copy in fetch[:3]:
        copy.wait()
    fill_gains(slots, turns, gain_ref, noise_ref, var_ref, scale_ref, var, scale)
    fetch[3].wait()
    for lat in range(lats):
        flat[lat * hours : (lat + 1) * hours, :lon] = x[lat]
    for b in range(steps):
        blocks[b * rows : (b + 1) * rows, :STEP] = flat[:, b * STEP : (b + 1) * STEP]
    value = spread(blocks[...])
    fetch[4].wait()
    for i in range(turns):
        gain_ref[i] = table[slots * depth + i * SUB : slots * depth + (i + 1) * SUB, :]
    for m in range(slots):
        high, low = split(table[m * depth : m * depth + LANES, :])
        part = jnp.dot(value, jnp.concatenate([high, high, low], axis=0), preferred_element_type=F32)
        straight = crossed = None
        for b in range(steps):
            here = part[b * rows : (b + 1) * rows]
            plain = here * table[m * depth + STEP + b : m * depth + STEP + b + 1, :]
            cross = here * table[m * depth + STEP + steps + b : m * depth + STEP + steps + b + 1, :]
            straight = plain if straight is None else straight + plain
            crossed = cross if crossed is None else crossed + cross
        slots_of[m * rows : (m + 1) * rows, :] = straight + partners(crossed, bands)
    out_ref[...] = slots_of[...].T
    for copy in fetch[5:]:
        copy.wait()


def smooth_kernel(lats, bands, first_gain, x_ref, gain_ref, later_ref, out_ref, turned, grid, series):
    owners, lanes = x_ref.shape
    hours = (gain_ref.shape[0] - first_gain - MOVES) // PER_HOUR
    blocks = owners // bands
    per_block = hours // blocks
    stride = per_block * SUB
    parts, _, width = turned.shape
    for part in range(parts):
        turned[part] = x_ref[part * width : (part + 1) * width, :].T
    per_part = width // bands
    depth = 2 * lats * bands
    for h in range(per_block):
        for lat in range(lats):
            for part in range(parts):
                rows = turned[part, pl.ds(lat * per_block + h, SUB, stride=stride), :]
                for t in range(per_part):
                    at = ((part * per_part + t) * per_block + h) * SUB
                    grid[at : at + SUB, lat * bands : (lat + 1) * bands] = rows[:, t * bands : (t + 1) * bands]
    series[...] = product(grid[...], later_ref[:depth, :])

    stay, once, both = (gain_ref[first_gain + i] for i in range(MOVES))
    gain = lambda h, which: gain_ref[first_gain + MOVES + PER_HOUR * h + which]
    scaled = []
    mean = None
    for h in range(hours):
        seen = series[h * SUB : (h + 1) * SUB, :]
        if mean is None:
            error = seen
            mean = [gain(h, j) * error for j in range(3)]
        else:
            kept, shift = stay * mean[0], once * mean[1] + both * mean[2]
            ahead = [kept + shift, stay * mean[1] + once * mean[2], stay * mean[2]]
            error = (seen - kept) - shift
            mean = [ahead[j] + gain(h, j) * error for j in range(3)]
        scaled.append(error * gain(h, 3))
    adjoint = None
    for h in reversed(range(hours)):
        drop = scaled[h]
        if adjoint is not None:
            drop = (drop + gain(h, 0) * adjoint[0]) + (gain(h, 1) * adjoint[1] + gain(h, 2) * adjoint[2])
        here = slice(h * SUB, (h + 1) * SUB)
        series[here, :] = series[here, :] - gain(h, 4) * drop
        if adjoint is None:
            adjoint = [-(move * drop) for move in (stay, once, both)]
        else:
            moved = [
                stay * adjoint[0],
                once * adjoint[0] + stay * adjoint[1],
                both * adjoint[0] + (once * adjoint[1] + stay * adjoint[2]),
            ]
            adjoint = [value - move * drop for value, move in zip(moved, (stay, once, both))]

    grid[...] = product(series[...], later_ref[depth : 2 * depth, :])
    for h in range(per_block):
        for lat in range(lats):
            for part in range(parts):
                rows = jnp.concatenate(
                    [
                        grid[(t * per_block + h) * SUB : (t * per_block + h + 1) * SUB, lat * bands : (lat + 1) * bands]
                        for t in range(part * per_part, (part + 1) * per_part)
                    ],
                    axis=1,
                )
                turned[part, pl.ds(lat * per_block + h, SUB, stride=stride), :] = rows
    for part in range(parts):
        out_ref[part * width : (part + 1) * width, :] = turned[part].T


def synthesise_kernel(bands, slots, x_ref, later_ref, turns_ref, out_ref, turned):
    lats, hours, lon = out_ref.shape
    steps = lon // STEP_BACK
    rows = 2 * SUB
    turned[...] = x_ref[...].T

    def turn(m, which, b):
        at = (2 * m + which) * steps + b
        return turns_ref[at // SUB, at % SUB : at % SUB + 1, :]

    values = []
    highs = []
    lows = []
    depth = 2 * x_ref.shape[0]
    first = later_ref.shape[0] - slots * depth
    for m in range(slots):
        at = first + m * depth
        highs.append(later_ref[at : at + depth // 2, :])
        lows.append(later_ref[at + depth // 2 : at + depth, :])
        plain = turned[m * rows : (m + 1) * rows, :]
        cross = partners(plain, bands)
        turned_on = [
            plain * turn(m, 0, b) + cross * turn(m, 1, b) for b in range(steps)
        ]
        values.append(split(jnp.concatenate(turned_on, axis=0)))
    high = jnp.concatenate([each[0] for each in values], axis=1)
    low = jnp.concatenate([each[1] for each in values], axis=1)
    total = folded_product(high, low, jnp.concatenate(highs, axis=0), jnp.concatenate(lows, axis=0))
    field = jnp.concatenate([total[b * rows : (b + 1) * rows, :STEP_BACK] for b in range(steps)], axis=1)
    for lat in range(lats):
        out_ref[lat] = field[lat * hours : (lat + 1) * hours, :]


def params(mib):
    return pltpu.CompilerParams(vmem_limit_bytes=mib * MIB)


def in_hbm(value):
    return pltpu.with_memory_space_constraint(value, pltpu.HBM)


def per_device(tables, observed, noise_var, spectral_var, time_scale):
    lon_into, later = tables
    hours_dev, lat_dev, lon_size = observed.shape
    hours = noise_var.shape[0]
    bands = lax.axis_size("space")
    owners = lon_into.shape[1]
    slots = -(-spectral_var.shape[0] // lax.axis_size("tm"))
    turns = 2 * slots * (lon_size // STEP_BACK) // SUB
    lat_pad = later.shape[-1]
    rows = 2 * SUB
    lanes = SUB * rows
    lon_pad = -(-lon_size // LANES) * LANES
    vmem = pl.BlockSpec(memory_space=pltpu.VMEM)
    smem = pl.BlockSpec(memory_space=pltpu.SMEM)
    hbm = pl.BlockSpec(memory_space=pltpu.HBM)

    by_lat = observed.transpose(1, 0, 2)
    sent, gains, later = pl.pallas_call(
        functools.partial(analyse_kernel, bands, slots),
        out_shape=(
            jax.ShapeDtypeStruct((owners, lanes), F32),
            jax.ShapeDtypeStruct((turns + MOVES + PER_HOUR * hours, SUB, lat_pad), F32),
            jax.ShapeDtypeStruct(later.shape, BF16),
        ),
        in_specs=[hbm] * 6,
        out_specs=(vmem,) * 3,
        scratch_shapes=[
            pltpu.VMEM(by_lat.shape, F32),
            pltpu.VMEM(lon_into.shape, F32),
            pltpu.VMEM((rows, lon_pad), F32),
            pltpu.VMEM((lon_size // STEP * rows, LANES), F32),
            pltpu.VMEM((lanes, owners), F32),
            pltpu.SMEM(noise_var.shape, F32),
            pltpu.VMEM(spectral_var.shape, F32),
            pltpu.VMEM(spectral_var.shape, F32),
            pltpu.VMEM((SUB, lat_pad), F32),
            pltpu.VMEM((SUB, lat_pad), F32),
            pltpu.SemaphoreType.DMA((6,)),
        ],
        compiler_params=params(16),
        name="analyse",
    )(*(in_hbm(each) for each in (by_lat, lon_into, noise_var, spectral_var, time_scale, later)))
    got = lax.all_to_all(sent, ("tm", "space"), split_axis=0, concat_axis=0, tiled=True)

    smooth = pl.pallas_call(
        functools.partial(smooth_kernel, lat_dev, bands, turns),
        out_shape=jax.ShapeDtypeStruct((owners, lanes), F32),
        in_specs=[vmem] * 3,
        out_specs=vmem,
        scratch_shapes=[
            pltpu.VMEM((owners // LANES, lanes, LANES), F32),
            pltpu.VMEM((hours * SUB, lat_pad), F32),
            pltpu.VMEM((hours * SUB, lat_pad), F32),
        ],
        compiler_params=params(16),
        name="smooth",
    )(got, gains, later)
    back = lax.all_to_all(smooth, ("tm", "space"), split_axis=0, concat_axis=0, tiled=True)

    field = pl.pallas_call(
        functools.partial(synthesise_kernel, bands, slots),
        out_shape=jax.ShapeDtypeStruct(by_lat.shape, F32),
        in_specs=[vmem] * 3,
        out_specs=vmem,
        scratch_shapes=[pltpu.VMEM((lanes, owners), F32)],
        compiler_params=params(16),
        name="synthesise",
    )(back, later, gains)
    return field.transpose(1, 0, 2)


def solution(mesh):
    placed = (P("tm", "space", None), P(), P("space", None), P("space", None))
    blocks, bands = mesh.shape["tm"], mesh.shape["space"]

    def whole(observed, noise_var, spectral_var, time_scale):
        lon_size = observed.shape[2]
        lat_size = spectral_var.shape[1]
        tables = all_tables(observed.shape[2], spectral_var.shape[1], blocks, bands)
        tables = tuple(jnp.asarray(table) for table in tables)
        return jax.shard_map(
            functools.partial(per_device, tables),
            mesh=mesh,
            in_specs=placed,
            out_specs=P("tm", "space", None),
            check_vma=False,
        )(observed, noise_var, spectral_var, time_scale)

    return whole
```

```python
import functools
import math

import jax
import jax.numpy as jnp
import ml_dtypes
import numpy as np
from jax import lax
from jax.experimental import pallas as pl
from jax.experimental.pallas import tpu as pltpu
from jax.sharding import PartitionSpec as P

ROOT_FIVE = 2.23606797749979
STATIONARY = ((1.0, 1.0, 2.0 / 3.0), (1.0, 4.0 / 3.0, 4.0 / 3.0), (2.0 / 3.0, 4.0 / 3.0, 8.0 / 3.0))
MOVES = 3
F32 = jnp.float32
BF16 = jnp.bfloat16
SUB = 8
LANES = 128
PER_HOUR = 5
STEP = 120
STEP_BACK = 240
MIB = 2**20


def halves(table):
    high = table.astype(ml_dtypes.bfloat16)
    low = (table - high.astype(np.float64)).astype(ml_dtypes.bfloat16)
    return np.concatenate([high, low], axis=-2)


def lon_basis(size):
    mode = np.arange(size)[:, None]
    longitude = np.arange(size)[None, :]
    half = size // 2
    sine = mode > half
    frequency = np.where(sine, mode - half, mode)
    radians = (frequency * longitude % size) * (2.0 * math.pi / size)
    weight = np.where((mode == 0) | (mode == half), math.sqrt(1.0 / size), math.sqrt(2.0 / size))
    return np.where(sine, np.sin(radians), np.cos(radians)) * weight


def lat_basis(size):
    wavenumber = np.arange(size)[:, None]
    latitude = np.arange(size)[None, :]
    radians = (wavenumber * (2 * latitude + 1) % (4 * size)) * (math.pi / (2.0 * size))
    weight = np.where(wavenumber == 0, math.sqrt(1.0 / size), math.sqrt(2.0 / size))
    return np.cos(radians) * weight


def lon_tables(size, step, hour_blocks, bands):
    per_band = size // bands
    slots = -(-per_band // hour_blocks)
    half = size // 2
    slot = np.arange(slots)[:, None, None]
    block = np.arange(hour_blocks)[None, :, None]
    band = np.arange(bands)[None, None, :]
    within = slots * block + slot + 0 * band
    used = within < per_band
    mode = np.where(used, per_band * band + within, 0)
    rows = (lon_basis(size)[mode] * used[..., None]).reshape(slots, hour_blocks * bands, size)
    sine = mode > half
    frequency = np.where(sine, mode - half, mode)
    ahead = np.arange(size // step)[:, None, None, None] * step
    radians = (frequency * ahead % size) * (2.0 * math.pi / size)
    straight = np.where(used, np.cos(radians), 0.0)
    crossed = np.where(used & (mode % half != 0), np.sin(radians), 0.0) * np.where(sine, 1.0, -1.0)
    crossed = np.roll(crossed, bands // 2, axis=-1)
    turns = np.stack([straight, crossed]).reshape(2, size // step, slots, hour_blocks * bands)
    head = np.zeros((slots, hour_blocks * bands, -(-step // LANES) * LANES))
    head[..., :step] = rows[..., :step]
    return head, turns.transpose(2, 0, 1, 3).astype(np.float32)


def all_tables(lon_size, lat_size, blocks, bands):
    head, turns = lon_tables(lon_size, STEP, blocks, bands)
    slots, owners, _ = head.shape
    into = np.concatenate([head[..., :STEP].transpose(0, 2, 1), turns.reshape(slots, -1, owners)], axis=1)
    head, turns = lon_tables(lon_size, STEP_BACK, blocks, bands)
    back = halves(head).reshape(-1, head.shape[-1])
    by_lat = lat_basis(lat_size).reshape(lat_size, bands, lat_size // bands)
    by_lat = by_lat.transpose(0, 2, 1).reshape(lat_size, lat_size)
    pad = -lat_size % (2 * LANES)
    by_lat = [np.pad(each, ((0, 0), (0, pad))) for each in (by_lat.T, by_lat)]
    later = np.concatenate([*map(halves, by_lat), back], axis=0)
    into = np.concatenate([into.reshape(-1, owners), turns.reshape(-1, owners)], axis=0)
    return into.astype(np.float32), later


def split(value):
    high = value.astype(BF16)
    return high, (value - high.astype(F32)).astype(BF16)


def spread(value):
    high, low = split(value)
    return jnp.concatenate([high, low, high], axis=1)


def folded_product(high, low, table_high, table_low):
    rows = high.shape[0]
    both = jnp.dot(jnp.concatenate([high, low], axis=0), table_high, preferred_element_type=F32)
    return both[:rows] + both[rows:] + jnp.dot(high, table_low, preferred_element_type=F32)


def product(value, table):
    depth = table.shape[0] // 2
    high, low = split(value[:, :depth])
    return folded_product(high, low, table[:depth], table[depth:])


def partners(value, bands):
    half = bands // 2
    width = value.shape[1]
    upper = lax.broadcasted_iota(jnp.int32, value.shape, 1) % bands >= half
    return jnp.where(upper, pltpu.roll(value, half, 1), pltpu.roll(value, width - half, 1))


def fill_gains(slots, first_gain, out_ref, noise_ref, var_ref, scale_ref, var, scale):
    last = var_ref.shape[0] - 1
    var[...] = jnp.ones_like(var)
    scale[...] = jnp.ones_like(scale)
    for m in range(slots):
        row = jnp.minimum(slots * lax.axis_index("tm") + m, last)
        var[m : m + 1, : var_ref.shape[1]] = var_ref[pl.ds(row, 1), :]
        scale[m : m + 1, : var_ref.shape[1]] = scale_ref[pl.ds(row, 1), :]
    variance = var[...]
    rate = ROOT_FIVE / scale[...]
    damping = jnp.exp(-rate)
    half_square = 0.5 * rate * rate
    stay, once, both = damping, damping * rate, damping * half_square
    for i, move in enumerate((stay, once, both)):
        out_ref[first_gain + i] = move

    def carried(p):
        top = [stay * p[0, j] + (once * p[1, j] + both * p[2, j]) for j in range(3)]
        middle = [stay * p[1, j] + once * p[2, j] for j in range(3)]
        last_one = stay * p[2, 2]
        return {
            (0, 0): stay * top[0] + (once * top[1] + both * top[2]),
            (0, 1): stay * top[1] + once * top[2],
            (0, 2): stay * top[2],
            (1, 1): stay * middle[1] + once * middle[2],
            (1, 2): stay * middle[2],
            (2, 2): stay * last_one,
        }

    def symmetric(upper):
        return {(i, j): upper[min(i, j), max(i, j)] for i in range(3) for j in range(3)}

    start = {(i, j): variance * STATIONARY[i][j] for i in range(3) for j in range(i, 3)}
    moved = carried(symmetric(start))
    noise_cov = {at: start[at] - moved[at] for at in start}
    pm = start
    for h in range((out_ref.shape[0] - first_gain - MOVES) // PER_HOUR):
        at = first_gain + MOVES + PER_HOUR * h
        noise = noise_ref[h]
        if h > 0:
            moved = carried(symmetric(cov))
            pm = {entry: moved[entry] + noise_cov[entry] for entry in moved}
            inverse = 1.0 / (moved[0, 0] + (noise_cov[0, 0] + noise))
        else:
            inverse = 1.0 / (pm[0, 0] + noise)
        k = [pm[0, j] * inverse for j in range(3)]
        for j in range(3):
            out_ref[at + j] = k[j]
        out_ref[at + 3] = inverse
        out_ref[at + 4] = jnp.full(inverse.shape, noise, F32)
        cov = {(0, j): (noise * pm[0, j]) * inverse for j in range(3)}
        for i in (1, 2):
            for j in range(i, 3):
                cov[i, j] = pm[i, j] - (pm[0, i] * pm[0, j]) * inverse


def analyse_kernel(
    bands, slots, x_hbm, table_hbm, noise_hbm, var_hbm, scale_hbm, later_hbm, out_ref, gain_ref,
    later_ref, x, table, flat, blocks, slots_of, noise_ref, var_ref, scale_ref, var, scale, sems,
):
    lats, hours, lon = x.shape
    steps = lon // STEP
    depth = STEP + 2 * steps
    turns = (table.shape[0] - slots * depth) // SUB
    rows = 2 * SUB
    pairs = (
        (var_hbm, var_ref),
        (scale_hbm, scale_ref),
        (noise_hbm, noise_ref),
        (x_hbm, x),
        (table_hbm, table),
        (later_hbm, later_ref),
    )
    fetch = [pltpu.make_async_copy(here, there, sems.at[i]) for i, (here, there) in enumerate(pairs)]
    for copy in fetch:
        copy.start()
    flat[...] = jnp.zeros_like(flat)
    blocks[...] = jnp.zeros_like(blocks)
    slots_of[...] = jnp.zeros_like(slots_of)
    for copy in fetch[:3]:
        copy.wait()
    fill_gains(slots, turns, gain_ref, noise_ref, var_ref, scale_ref, var, scale)
    fetch[3].wait()
    for lat in range(lats):
        flat[lat * hours : (lat + 1) * hours, :lon] = x[lat]
    for b in range(steps):
        blocks[b * rows : (b + 1) * rows, :STEP] = flat[:, b * STEP : (b + 1) * STEP]
    value = spread(blocks[...])
    fetch[4].wait()
    for i in range(turns):
        gain_ref[i] = table[slots * depth + i * SUB : slots * depth + (i + 1) * SUB, :]
    for m in range(slots):
        high, low = split(table[m * depth : m * depth + LANES, :])
        part = jnp.dot(value, jnp.concatenate([high, high, low], axis=0), preferred_element_type=F32)
        straight = crossed = None
        for b in range(steps):
            here = part[b * rows : (b + 1) * rows]
            plain = here * table[m * depth + STEP + b : m * depth + STEP + b + 1, :]
            cross = here * table[m * depth + STEP + steps + b : m * depth + STEP + steps + b + 1, :]
            straight = plain if straight is None else straight + plain
            crossed = cross if crossed is None else crossed + cross
        slots_of[m * rows : (m + 1) * rows, :] = straight + partners(crossed, bands)
    out_ref[...] = slots_of[...].T
    for copy in fetch[5:]:
        copy.wait()


def smooth_kernel(lats, bands, first_gain, x_ref, gain_ref, later_ref, out_ref, turned, grid, series):
    owners, lanes = x_ref.shape
    hours = (gain_ref.shape[0] - first_gain - MOVES) // PER_HOUR
    blocks = owners // bands
    per_block = hours // blocks
    stride = per_block * SUB
    parts, _, width = turned.shape
    for part in range(parts):
        turned[part] = x_ref[part * width : (part + 1) * width, :].T
    per_part = width // bands
    depth = 2 * lats * bands
    for h in range(per_block):
        for lat in range(lats):
            for part in range(parts):
                rows = turned[part, pl.ds(lat * per_block + h, SUB, stride=stride), :]
                for t in range(per_part):
                    at = ((part * per_part + t) * per_block + h) * SUB
                    grid[at : at + SUB, lat * bands : (lat + 1) * bands] = rows[:, t * bands : (t + 1) * bands]
    series[...] = product(grid[...], later_ref[:depth, :])

    stay, once, both = (gain_ref[first_gain + i] for i in range(MOVES))
    gain = lambda h, which: gain_ref[first_gain + MOVES + PER_HOUR * h + which]
    scaled = []
    mean = None
    for h in range(hours):
        seen = series[h * SUB : (h + 1) * SUB, :]
        if mean is None:
            error = seen
            mean = [gain(h, j) * error for j in range(3)]
        else:
            kept, shift = stay * mean[0], once * mean[1] + both * mean[2]
            ahead = [kept + shift, stay * mean[1] + once * mean[2], stay * mean[2]]
            error = (seen - kept) - shift
            mean = [ahead[j] + gain(h, j) * error for j in range(3)]
        scaled.append(error * gain(h, 3))
    adjoint = None
    for h in reversed(range(hours)):
        drop = scaled[h]
        if adjoint is not None:
            drop = (drop + gain(h, 0) * adjoint[0]) + (gain(h, 1) * adjoint[1] + gain(h, 2) * adjoint[2])
        here = slice(h * SUB, (h + 1) * SUB)
        series[here, :] = series[here, :] - gain(h, 4) * drop
        if adjoint is None:
            adjoint = [-(move * drop) for move in (stay, once, both)]
        else:
            moved = [
                stay * adjoint[0],
                once * adjoint[0] + stay * adjoint[1],
                both * adjoint[0] + (once * adjoint[1] + stay * adjoint[2]),
            ]
            adjoint = [value - move * drop for value, move in zip(moved, (stay, once, both))]

    grid[...] = product(series[...], later_ref[depth : 2 * depth, :])
    for h in range(per_block):
        for lat in range(lats):
            for part in range(parts):
                rows = jnp.concatenate(
                    [
                        grid[(t * per_block + h) * SUB : (t * per_block + h + 1) * SUB, lat * bands : (lat + 1) * bands]
                        for t in range(part * per_part, (part + 1) * per_part)
                    ],
                    axis=1,
                )
                turned[part, pl.ds(lat * per_block + h, SUB, stride=stride), :] = rows
    for part in range(parts):
        out_ref[part * width : (part + 1) * width, :] = turned[part].T


def synthesise_kernel(bands, slots, x_ref, later_ref, turns_ref, out_ref, turned):
    lats, hours, lon = out_ref.shape
    steps = lon // STEP_BACK
    rows = 2 * SUB
    turned[...] = x_ref[...].T

    def turn(m, which, b):
        at = (2 * m + which) * steps + b
        return turns_ref[at // SUB, at % SUB : at % SUB + 1, :]

    values = []
    highs = []
    lows = []
    depth = 2 * x_ref.shape[0]
    first = later_ref.shape[0] - slots * depth
    for m in range(slots):
        at = first + m * depth
        highs.append(later_ref[at : at + depth // 2, :])
        lows.append(later_ref[at + depth // 2 : at + depth, :])
        plain = turned[m * rows : (m + 1) * rows, :]
        cross = partners(plain, bands)
        turned_on = [
            plain * turn(m, 0, b) + cross * turn(m, 1, b) for b in range(steps)
        ]
        values.append(split(jnp.concatenate(turned_on, axis=0)))
    high = jnp.concatenate([each[0] for each in values], axis=1)
    low = jnp.concatenate([each[1] for each in values], axis=1)
    total = folded_product(high, low, jnp.concatenate(highs, axis=0), jnp.concatenate(lows, axis=0))
    field = jnp.concatenate([total[b * rows : (b + 1) * rows, :STEP_BACK] for b in range(steps)], axis=1)
    for lat in range(lats):
        out_ref[lat] = field[lat * hours : (lat + 1) * hours, :]


def params(mib):
    return pltpu.CompilerParams(vmem_limit_bytes=mib * MIB)


def in_hbm(value):
    return pltpu.with_memory_space_constraint(value, pltpu.HBM)


def per_device(tables, observed, noise_var, spectral_var, time_scale):
    lon_into, later = tables
    hours_dev, lat_dev, lon_size = observed.shape
    hours = noise_var.shape[0]
    bands = lax.axis_size("space")
    owners = lon_into.shape[1]
    slots = -(-spectral_var.shape[0] // lax.axis_size("tm"))
    turns = 2 * slots * (lon_size // STEP_BACK) // SUB
    lat_pad = later.shape[-1]
    rows = 2 * SUB
    lanes = SUB * rows
    lon_pad = -(-lon_size // LANES) * LANES
    vmem = pl.BlockSpec(memory_space=pltpu.VMEM)
    smem = pl.BlockSpec(memory_space=pltpu.SMEM)
    hbm = pl.BlockSpec(memory_space=pltpu.HBM)

    by_lat = observed.transpose(1, 0, 2)
    sent, gains, later = pl.pallas_call(
        functools.partial(analyse_kernel, bands, slots),
        out_shape=(
            jax.ShapeDtypeStruct((owners, lanes), F32),
            jax.ShapeDtypeStruct((turns + MOVES + PER_HOUR * hours, SUB, lat_pad), F32),
            jax.ShapeDtypeStruct(later.shape, BF16),
        ),
        in_specs=[hbm] * 6,
        out_specs=(vmem,) * 3,
        scratch_shapes=[
            pltpu.VMEM(by_lat.shape, F32),
            pltpu.VMEM(lon_into.shape, F32),
            pltpu.VMEM((rows, lon_pad), F32),
            pltpu.VMEM((lon_size // STEP * rows, LANES), F32),
            pltpu.VMEM((lanes, owners), F32),
            pltpu.SMEM(noise_var.shape, F32),
            pltpu.VMEM(spectral_var.shape, F32),
            pltpu.VMEM(spectral_var.shape, F32),
            pltpu.VMEM((SUB, lat_pad), F32),
            pltpu.VMEM((SUB, lat_pad), F32),
            pltpu.SemaphoreType.DMA((6,)),
        ],
        compiler_params=params(16),
        name="analyse",
    )(*(in_hbm(each) for each in (by_lat, lon_into, noise_var, spectral_var, time_scale, later)))
    got = lax.all_to_all(sent, ("tm", "space"), split_axis=0, concat_axis=0, tiled=True)

    smooth = pl.pallas_call(
        functools.partial(smooth_kernel, lat_dev, bands, turns),
        out_shape=jax.ShapeDtypeStruct((owners, lanes), F32),
        in_specs=[vmem] * 3,
        out_specs=vmem,
        scratch_shapes=[
            pltpu.VMEM((owners // LANES, lanes, LANES), F32),
            pltpu.VMEM((hours * SUB, lat_pad), F32),
            pltpu.VMEM((hours * SUB, lat_pad), F32),
        ],
        compiler_params=params(16),
        name="smooth",
    )(got, gains, later)
    back = lax.all_to_all(smooth, ("tm", "space"), split_axis=0, concat_axis=0, tiled=True)

    field = pl.pallas_call(
        functools.partial(synthesise_kernel, bands, slots),
        out_shape=jax.ShapeDtypeStruct(by_lat.shape, F32),
        in_specs=[vmem] * 3,
        out_specs=vmem,
        scratch_shapes=[pltpu.VMEM((lanes, owners), F32)],
        compiler_params=params(16),
        name="synthesise",
    )(back, later, gains)
    return field.transpose(1, 0, 2)


def solution(mesh):
    placed = (P("tm", "space", None), P(), P("space", None), P("space", None))
    blocks, bands = mesh.shape["tm"], mesh.shape["space"]

    def whole(observed, noise_var, spectral_var, time_scale):
        lon_size = observed.shape[2]
        lat_size = spectral_var.shape[1]
        tables = all_tables(observed.shape[2], spectral_var.shape[1], blocks, bands)
        tables = tuple(jnp.asarray(table) for table in tables)
        return jax.shard_map(
            functools.partial(per_device, tables),
            mesh=mesh,
            in_specs=placed,
            out_specs=P("tm", "space", None),
            check_vma=False,
        )(observed, noise_var, spectral_var, time_scale)

    return whole
```
